256 devices in a mesh: section: 4 (over z_hi), fsdp: 64 (over z_lo, y, x, core).
Axes of the slice: x: 4, y: 4, z: 8 (z_hi: 4, z_lo: 2; z = z_hi * 2 + z_lo), core: 2. Of those that a mesh axis runs over, the one named last changes fastest.
Arguments:
- inputs: bfloat16 [2, 8192, 2048], P(None, 'fsdp'), may hold values from -6 to 6
- weights: bfloat16 [4, 2048, 2048], P('section', 'fsdp'), may hold values from -0.125 to 0.125
- cotangents: bfloat16 [2, 8192, 2048], P(None, 'fsdp'), may hold values from -0.125 to 0.125
- lengths: int32 [2, 128], P(None, 'fsdp'), may hold values from 1 to 64
Outputs:
- weight_grads: float32 [4, 2048, 2048], P('section', 'fsdp')
The draws below stay inside these ranges and needn't reach their ends.
Inputs may be any that keep to these rules, and one draw needn't show every extreme that they name: `lengths`: each sequence's count of real tokens; its other positions up to 64 are padding.
All inputs are finite; a program needn't handle non-finite values.
Results may differ from the reference program's by a relative error of at most 0.009.
Values may be sent and summed in bfloat16 or wider, within the bound.
A program may use at most 128 MiB of HBM per device.

```python
import jax
import jax.numpy as jnp
from jax import lax

D = 2048
SEQ_LEN = 64
SEQS = 128
TOKENS = 8192
N_SECTION = 4


def with_ends(entries, key, low, high):
    longest = entries.shape.index(max(entries.shape))
    spots = []
    for shift in (0, 1):
        where = [jax.random.randint(jax.random.fold_in(key, axis), (), 0, length) for axis, length in enumerate(entries.shape)]
        where[longest] = (where[longest] + shift) % entries.shape[longest]
        spots.append(tuple(where))
    return entries.at[spots[0]].set(low).at[spots[1]].set(high)


def level_of(stream_key, shape, cuts, least, largest):
    loudness, own = 1.0, jax.random.fold_in(stream_key, 6)
    for dim, parts in cuts:
        steps = jnp.exp(jax.random.uniform(jax.random.fold_in(own, dim), (parts,), jnp.float32, least / len(cuts), largest / len(cuts)))
        loudness = loudness * jnp.repeat(steps, shape[dim] // parts).reshape([-1 if axis == dim else 1 for axis in range(len(shape))])
    return loudness


def bell_draw(key, dims, spread, reach, shards=(), held_as=jnp.bfloat16):
    result = spread * jax.random.normal(key, dims, jnp.float32)
    if shards:
        result = result * level_of(key, dims, shards, -0.22, 0.18)
    return jnp.clip(result, -reach, reach).astype(held_as)


def setup_inputs(seed: int = 0) -> dict:
    keys = jax.random.split(jax.random.key(seed), 5)
    inputs = bell_draw(keys[0], (2, TOKENS, D), 1.0, 6.0, ((1, 64),))
    weights = bell_draw(keys[1], (N_SECTION, D, D), D ** -0.5, 0.125, ((0, 4), (1, 64)))
    cotangents = bell_draw(keys[2], (2, TOKENS, D), ((2 * TOKENS) ** -0.5), 0.125, ((1, 64),))
    lengths = with_ends(jax.random.randint(keys[3], (2, SEQS), 1, SEQ_LEN + 1), jax.random.fold_in(keys[3], 1), 1, SEQ_LEN).astype(jnp.int32)
    return dict(inputs=inputs, weights=weights, cotangents=cotangents, lengths=lengths)


epsilon = 1e-06

def section_forward(section_input, section_weight):
    as_float = section_input.astype(jnp.float32)
    inverse = lax.rsqrt(lax.optimization_barrier(jnp.mean(as_float * as_float, axis=-1, keepdims=True)) + epsilon)
    normed = (as_float * inverse).astype(jnp.bfloat16)
    preact = jnp.dot(normed, section_weight, preferred_element_type=jnp.float32)
    return (as_float, inverse, normed, preact)

def section_output(section_input, section_weight):
    as_float, inverse, normed, preact = section_forward(section_input, section_weight)
    return (as_float + jax.nn.gelu(preact)).astype(jnp.bfloat16)

def section_backward(section_input, section_weight, grad_output):
    as_float, inverse, normed, preact = section_forward(section_input, section_weight)
    grad_float = grad_output.astype(jnp.float32)
    unused, pullback = jax.vjp(jax.nn.gelu, preact)
    grad_pre = pullback(grad_float)[0].astype(jnp.bfloat16)
    grad_normed = lax.dot_general(grad_pre, section_weight, (((1,), (1,)), ((), ())), preferred_element_type=jnp.float32)
    grad_input = grad_float + inverse * grad_normed - as_float * inverse ** 3 * lax.optimization_barrier(jnp.mean(grad_normed * as_float, axis=-1, keepdims=True))
    return (grad_input.astype(jnp.bfloat16), normed, grad_pre)

def weight_term(normed, grad_pre):
    return lax.dot_general(normed, grad_pre, (((0,), (0,)), ((), ())), preferred_element_type=jnp.float32)

def reference(inputs, weights, cotangents, lengths):
    current = inputs.reshape(2 * TOKENS, D)
    stored = []
    for section_number in range(N_SECTION):
        stored.append(current)
        if section_number + 1 < N_SECTION:
            current = section_output(current, weights[section_number])
    positions = jnp.arange(SEQ_LEN, dtype=jnp.int32)
    live_rows = (positions[None, None, :] < lengths[:, :, None]).reshape(2 * TOKENS, 1)
    flowing = jnp.where(live_rows, cotangents.reshape(2 * TOKENS, D), jnp.zeros((), cotangents.dtype))
    results = [None] * N_SECTION
    for section_number in reversed(range(N_SECTION)):
        flowing, normed, grad_pre = section_backward(stored[section_number], weights[section_number], flowing)
        results[section_number] = weight_term(normed, grad_pre)
    return jnp.stack(results)
```

```python
import functools

import jax
import jax.numpy as jnp
from jax import lax
from jax.experimental import pallas as pl
from jax.experimental.pallas import tpu as pltpu
from jax.sharding import PartitionSpec as P

MESH = pl.DeviceIdType.MESH
F32 = jnp.float32
BF16 = jnp.bfloat16
EPS = 1e-06
GELU_C = 0.7978845608028654
GELU_A = 0.044715

D = 2048
ROWS = 256
HALF = 1024
UNITS = 8
FIRST, SECOND = pl.ds(0, 2), pl.ds(2, 2)
TOP, BOTTOM = pl.ds(0, 32), pl.ds(32, 32)


def position():
    s, f = lax.axis_index("section"), lax.axis_index("fsdp")
    c = lax.rem(f, 2)
    x = lax.rem(f // 2, 4)
    y = lax.rem(f // 8, 4)
    zl = f // 32
    return s, zl, x, y, c


def device(x, y, z, c):
    return (z // 2, lax.rem(z, 2) * 32 + y * 8 + x * 2 + c)


def remote(src, dst, send, recv, dev):
    return pltpu.make_async_remote_copy(
        src_ref=src, dst_ref=dst, send_sem=send, recv_sem=recv, device_id=dev, device_id_type=MESH
    )


def kernel(
    x_ref, w_ref, cot_ref, len_ref, out_ref,
    wb, xs, gd, iv, gp, nw, gw, gr, gn, r1, r2, t1, t2, z1, sf, o1,
    loc, xsend, xrecv, rsend, rrecv, psend, precv, qsend, qrecv, dsend, drecv,
    nsend, nrecv, r1s, r1r, r2s, r2r, t1s, t1r, t2s, t2r, zsend, zrecv, osend, orecv,
):
    s, zl, x, y, c = position()
    z = 2 * s + zl
    sib = device(x, y, z, 1 - c)
    xp, xm = lax.rem(x + 1, 4), lax.rem(x + 3, 4)
    yp, ym = lax.rem(y + 1, 4), lax.rem(y + 3, 4)
    x2, y2 = lax.rem(x + 2, 4), lax.rem(y + 2, 4)
    dxp, dxm = device(xp, y, z, c), device(xm, y, z, c)
    dyp, dym = device(x, yp, z, c), device(x, ym, z, c)

    barrier = pltpu.get_barrier_semaphore()
    for partner in (dxp, dxm, dyp, dym, sib):
        pl.semaphore_signal(barrier, inc=1, device_id=partner, device_id_type=MESH)
    for d in range(1, 8):
        pl.semaphore_signal(
            barrier, inc=1, device_id=device(x, y, lax.rem(z + d, 8), c), device_id_type=MESH
        )

    in_x = pltpu.make_async_copy(x_ref, xs.at[0], loc.at[0])
    in_x.start()
    mine = pl.ds(pl.multiple_of(c * HALF, HALF), HALF)
    other = pl.ds(pl.multiple_of((1 - c) * HALF, HALF), HALF)
    my_rows = pl.ds(pl.multiple_of(c * 32, 32), 32)
    sib_rows = pl.ds(pl.multiple_of((1 - c) * 32, 32), 32)
    in_w = pltpu.make_async_copy(
        w_ref.at[:, mine], wb.at[2 * s + c, zl, y, x, my_rows], loc.at[1]
    )
    in_w.start()
    for m in range(2):
        for q in range(2):
            rows = pl.ds(128 * m + 64 * q, 64)
            live = lax.broadcasted_iota(jnp.int32, (64, D), 0) < len_ref[m, q]
            gr[rows, :] = jnp.where(live, cot_ref[rows, :].astype(F32), 0.0).astype(BF16)
    pl.semaphore_wait(barrier, 12)

    give = remote(
        w_ref.at[:, other], wb.at[2 * s + 1 - c, zl, y, x, my_rows], xsend, xrecv, sib
    )
    give.start()
    in_x.wait()
    in_w.wait()
    remote(
        w_ref.at[:, mine], wb.at[2 * s + c, zl, y, x, sib_rows], xsend, xrecv, sib
    ).wait_recv()

    def raw(d):
        block = wb.at[2 * s + c, zl, y, x]
        dest = device(x, y, lax.rem(z + d, 8), c)
        return remote(block, block, rsend.at[d - 1], rrecv.at[z], dest)

    def row(cc, kh, uz, i, part=None):
        if cc == 0:
            return wb.at[kh, uz, i] if part is None else wb.at[kh, uz, i, part]
        return wb.at[kh, uz, :, i] if part is None else wb.at[kh, uz, part, i]

    def chip(cc, kh, uz, i, part=None):
        at = (kh, uz, y, i) if cc == 0 else (kh, uz, i, x)
        return wb.at[at] if part is None else wb.at[at + (part,)]

    def p_copies(cc, u):
        kh, uz = 2 * (u // 2) + cc, lax.rem(u, 2)
        me, plus, minus = (x, xp, xm) if cc == 0 else (y, yp, ym)
        to_plus, to_minus = (dxp, dxm) if cc == 0 else (dyp, dym)
        own = chip(cc, kh, uz, me)
        from_minus, from_plus = chip(cc, kh, uz, minus, TOP), chip(cc, kh, uz, plus, BOTTOM)
        return (
            remote(own, own, psend.at[u, 0], precv.at[u, 0], to_plus),
            remote(own, own, psend.at[u, 1], precv.at[u, 1], to_minus),
            remote(from_minus, from_minus, psend.at[u, 2], precv.at[u, 2], to_plus),
            remote(from_plus, from_plus, psend.at[u, 3], precv.at[u, 3], to_minus),
        )

    def p_landed(cc, u, i):
        kh, uz = 2 * (u // 2) + cc, lax.rem(u, 2)
        plus, minus, far = (xp, xm, x2) if cc == 0 else (yp, ym, y2)
        land = (
            chip(cc, kh, uz, minus),
            chip(cc, kh, uz, plus),
            chip(cc, kh, uz, far, TOP),
            chip(cc, kh, uz, far, BOTTOM),
        )[i]
        remote(land, land, psend.at[u, i], precv.at[u, i], sib).wait_recv()

    def q_copies(cc, u):
        kh, uz = 2 * (u // 2) + cc, lax.rem(u, 2)
        me, plus, minus = (y, yp, ym) if cc == 0 else (x, xp, xm)
        to_plus, to_minus = (dyp, dym) if cc == 0 else (dxp, dxm)
        own = row(cc, kh, uz, me)
        from_minus, from_plus = row(cc, kh, uz, minus, FIRST), row(cc, kh, uz, plus, SECOND)
        return (
            remote(own, own, qsend.at[u, 0], qrecv.at[u, 0], to_plus),
            remote(own, own, qsend.at[u, 1], qrecv.at[u, 1], to_minus),
            remote(from_minus, from_minus, qsend.at[u, 2], qrecv.at[u, 2], to_plus),
            remote(from_plus, from_plus, qsend.at[u, 3], qrecv.at[u, 3], to_minus),
        )

    def q_landed(cc, u, i):
        kh, uz = 2 * (u // 2) + cc, lax.rem(u, 2)
        plus, minus, far = (yp, ym, y2) if cc == 0 else (xp, xm, x2)
        land = (
            row(cc, kh, uz, minus),
            row(cc, kh, uz, plus),
            row(cc, kh, uz, far, FIRST),
            row(cc, kh, uz, far, SECOND),
        )[i]
        remote(land, land, qsend.at[u, i], qrecv.at[u, i], sib).wait_recv()

    def d_copy(cc, u, i):
        kh, uz = 2 * (u // 2) + cc, lax.rem(u, 2)
        at = ((y, ym, yp, y2) if cc == 0 else (x, xm, xp, x2))[i]
        block = row(cc, kh, uz, at)
        return remote(block, block, dsend.at[u, i], drecv.at[u, i], sib)

    def unit(t):
        return jnp.where(t == 0, z, jnp.where(t - 1 < z, t - 1, t))

    def by_core(body):
        for cc in (0, 1):
            pl.when(c == cc)(functools.partial(body, cc))

    def stage_p1(t):
        u = unit(t)

        @pl.when(t == 0)
        def _():
            for d in (1, 7, 2, 6, 3, 5, 4):
                raw(d).start()

        @pl.when(t > 0)
        def _():
            block = wb.at[2 * (u // 2) + c, lax.rem(u, 2), y, x]
            remote(block, block, rsend.at[0], rrecv.at[u], sib).wait_recv()

        def body(cc):
            copies = p_copies(cc, u)
            copies[0].start()
            copies[1].start()

        by_core(body)

    def stage_p2(t):
        u = unit(t)

        def body(cc):
            copies = p_copies(cc, u)
            p_landed(cc, u, 0)
            copies[2].start()
            p_landed(cc, u, 1)
            copies[3].start()

        by_core(body)

    def stage_q1(t):
        u = unit(t)

        def body(cc):
            copies = q_copies(cc, u)
            p_landed(cc, u, 2)
            p_landed(cc, u, 3)
            copies[0].start()
            copies[1].start()
            d_copy(cc, u, 0).start()

        by_core(body)

    def stage_q2(t):
        u = unit(t)

        def body(cc):
            copies = q_copies(cc, u)
            q_landed(cc, u, 0)
            copies[2].start()
            q_landed(cc, u, 1)
            copies[3].start()
            d_copy(cc, u, 1).start()
            d_copy(cc, u, 2).start()

        by_core(body)

    def stage_f(t):
        u = unit(t)

        def body(cc):
            q_landed(cc, u, 2)
            q_landed(cc, u, 3)
            d_copy(cc, u, 3).start()

        by_core(body)

    def normed_copy():
        return remote(nw.at[c], nw.at[c], nsend.at[0], nrecv.at[0], sib)

    def forward(k):
        def body(cc):
            @pl.loop(0, 2)
            def _(uz):
                for i in range(4):
                    d_copy(1 - cc, 2 * k + uz, i).wait_recv()

        by_core(body)

        @pl.loop(0, ROWS // 32)
        def _(i):
            rows = pl.ds(pl.multiple_of(i * 32, 32), 32)
            xf = xs[k, rows, :].astype(F32)
            inv = lax.rsqrt(jnp.mean(xf * xf, axis=-1, keepdims=True) + EPS)
            iv[k, rows, :] = jnp.broadcast_to(inv, (32, 128))
            gp[rows, :] = (xf * inv).astype(BF16)

        @pl.when(k == s)
        def _():
            nw[c] = gp[...]
            normed_copy().start()

        @pl.loop(0, 4)
        def _(j):
            inside = pl.ds(pl.multiple_of(lax.rem(j, 2) * 512, 512), 512)
            cols = pl.ds(pl.multiple_of(j * 512, 512), 512)
            w = wb[2 * k + j // 2, :, :, :, :, inside].reshape(D, 512)
            u = jnp.dot(gp[...], w, preferred_element_type=F32)
            uu = u * u
            t = jnp.tanh((GELU_C * u) * (1.0 + GELU_A * uu))
            cdf = 0.5 * (1.0 + t)
            gd[k, :, cols] = cdf + (0.5 * GELU_C) * u * (1.0 - t * t) * (
                1.0 + (3.0 * GELU_A) * uu
            )

            @pl.when(k < 3)
            def _():
                nxt = jnp.minimum(k + 1, 3)
                xs[nxt, :, cols] = (xs[k, :, cols].astype(F32) + u * cdf).astype(BF16)

    @pl.loop(0, UNITS + 4)
    def _(i):
        pl.when(i < UNITS)(lambda: stage_p1(i))
        pl.when((i >= 1) & (i < UNITS + 1))(lambda: stage_p2(i - 1))
        pl.when((i >= 2) & (i < UNITS + 2))(lambda: stage_q1(i - 2))
        pl.when((i >= 3) & (i < UNITS + 3))(lambda: stage_q2(i - 3))
        pl.when(i >= 4)(lambda: stage_f(i - 4))
        ready = (i == 6) | (i == 8) | (i == 10) | (i == 11)
        k = jnp.where(i == 11, 3, (jnp.maximum(i, 6) - 6) // 2)
        pl.when(ready)(lambda: forward(k))

    def grad_pre(k):
        @pl.loop(0, ROWS // 32)
        def _(i):
            rows = pl.ds(pl.multiple_of(i * 32, 32), 32)
            gp[rows, :] = (gr[rows, :].astype(F32) * gd[k, rows, :]).astype(BF16)

    @pl.loop(0, 3 - s)
    def _(step):
        k = 3 - step
        grad_pre(k)

        @pl.loop(0, 4)
        def _(j):
            total = None
            for h in range(2):
                w = wb[2 * k + h, j // 2, pl.ds(lax.rem(j, 2) * 2, 2)].reshape(512, HALF)
                part = lax.dot_general(
                    gp[:, h * HALF : (h + 1) * HALF], w, (((1,), (1,)), ((), ())),
                    preferred_element_type=F32,
                )
                total = part if total is None else total + part
            gn[:, pl.ds(pl.multiple_of(j * 512, 512), 512)] = total

        @pl.loop(0, ROWS // 32)
        def _(i):
            rows = pl.ds(pl.multiple_of(i * 32, 32), 32)
            xf = xs[k, rows, :].astype(F32)
            g = gn[rows, :]
            inv = iv[k, rows, :][:, :1]
            mean = jnp.mean(g * xf, axis=-1, keepdims=True)
            gr[rows, :] = (
                gr[rows, :].astype(F32) + inv * g - xf * (inv * inv * inv * mean)
            ).astype(BF16)

    grad_pre(s)
    gw[c] = gp[:, mine]
    give_g = remote(gp.at[:, other], gw.at[c], nsend.at[1], nrecv.at[1], sib)
    give_g.start()

    give.wait_send()
    for d in range(1, 8):
        raw(d).wait_send()

    @pl.loop(0, UNITS)
    def _(u):
        def body(cc):
            for copy in p_copies(cc, u) + q_copies(cc, u):
                copy.wait_send()
            for i in range(4):
                d_copy(cc, u, i).wait_send()

        by_core(body)

    remote(nw.at[1 - c], nw.at[1 - c], nsend.at[0], nrecv.at[0], sib).wait_recv()
    remote(gw.at[1 - c], gw.at[1 - c], nsend.at[1], nrecv.at[1], sib).wait_recv()

    gb = wb.at[0]

    def weight_term(v):
        @pl.loop(0, 4)
        def _(j):
            cols = pl.ds(pl.multiple_of(v * HALF + j * 256, 256), 256)
            total = None
            for half in range(2):
                part = lax.dot_general(
                    nw[half, :, cols], gw[half], (((0,), (0,)), ((), ())),
                    preferred_element_type=F32,
                )
                total = part if total is None else total + part
            gb[v, j] = total.astype(BF16).reshape(4, 64, HALF)

    def grow(cc, v, i, part=None):
        if cc == 0:
            return gb.at[v, i] if part is None else gb.at[v, i, part]
        return gb.at[v, :, i] if part is None else gb.at[v, part, i]

    def gchip(cc, v, i, part=None):
        at = (v, y, i) if cc == 0 else (v, i, x)
        return gb.at[at] if part is None else gb.at[at + (part,)]

    def r1_copies(cc, v):
        far = y2 if cc == 0 else x2
        to_plus, to_minus = (dyp, dym) if cc == 0 else (dxp, dxm)
        return (
            remote(grow(cc, v, far, FIRST), r1.at[v, 0], r1s.at[v, 0], r1r.at[v, 0], to_plus),
            remote(grow(cc, v, far, SECOND), r1.at[v, 1], r1s.at[v, 1], r1r.at[v, 1], to_minus),
        )

    def r2_copies(cc, v):
        plus, minus = (yp, ym) if cc == 0 else (xp, xm)
        to_plus, to_minus = (dyp, dym) if cc == 0 else (dxp, dxm)
        return (
            remote(grow(cc, v, plus), r2.at[v, 0], r2s.at[v, 0], r2r.at[v, 0], to_plus),
            remote(grow(cc, v, minus), r2.at[v, 1], r2s.at[v, 1], r2r.at[v, 1], to_minus),
        )

    def t1_copies(cc, v):
        far = x2 if cc == 0 else y2
        to_plus, to_minus = (dxp, dxm) if cc == 0 else (dyp, dym)
        return (
            remote(gchip(cc, v, far, TOP), t1.at[v, 0], t1s.at[v, 0], t1r.at[v, 0], to_plus),
            remote(gchip(cc, v, far, BOTTOM), t1.at[v, 1], t1s.at[v, 1], t1r.at[v, 1], to_minus),
        )

    def t2_copies(cc, v):
        plus, minus = (xp, xm) if cc == 0 else (yp, ym)
        to_plus, to_minus = (dxp, dxm) if cc == 0 else (dyp, dym)
        return (
            remote(gchip(cc, v, plus), t2.at[v, 0], t2s.at[v, 0], t2r.at[v, 0], to_plus),
            remote(gchip(cc, v, minus), t2.at[v, 1], t2s.at[v, 1], t2r.at[v, 1], to_minus),
        )

    def add_into(ref, *others):
        total = ref[...].astype(F32)
        for more in others:
            total = total + more[...].astype(F32)
        ref[...] = total.astype(BF16)

    def rs_a(v):
        def body(cc):
            for copy in r1_copies(cc, v):
                copy.start()

        by_core(body)

    def rs_b(v):
        def body(cc):
            plus, minus = (yp, ym) if cc == 0 else (xp, xm)
            arrive, leave = r1_copies(cc, v), r2_copies(cc, v)
            arrive[0].wait_recv()
            add_into(grow(cc, v, plus, FIRST), r1.at[v, 0])
            leave[0].start()
            arrive[1].wait_recv()
            add_into(grow(cc, v, minus, SECOND), r1.at[v, 1])
            leave[1].start()

        by_core(body)

    def rs_c(v):
        def body(cc):
            me = y if cc == 0 else x
            arrive, leave = r2_copies(cc, v), t1_copies(cc, v)
            arrive[0].wait_recv()
            arrive[1].wait_recv()
            for i in range(4):
                block = gchip(cc, v, i)
                add_into(block, r2.at[v, 0, i], r2.at[v, 1, i])
            for copy in leave:
                copy.start()

        by_core(body)

    def rs_d(v):
        def body(cc):
            plus, minus = (xp, xm) if cc == 0 else (yp, ym)
            arrive, leave = t1_copies(cc, v), t2_copies(cc, v)
            arrive[0].wait_recv()
            add_into(gchip(cc, v, plus, TOP), t1.at[v, 0])
            leave[0].start()
            arrive[1].wait_recv()
            add_into(gchip(cc, v, minus, BOTTOM), t1.at[v, 1])
            leave[1].start()

        by_core(body)

    def rs_e(v):
        def body(cc):
            for copy in t2_copies(cc, v):
                copy.wait_recv()

        by_core(body)
        return (
            gb[v, y, x].astype(F32) + t2[v, 0].astype(F32) + t2[v, 1].astype(F32)
        )

    v0, v1 = 1 - zl, zl
    weight_term(v0)
    rs_a(v0)
    weight_term(v1)
    rs_a(v1)
    rs_b(v0)
    rs_b(v1)
    rs_c(v0)
    rs_c(v1)
    rs_d(v0)
    rs_d(v1)
    gb[v0, y, x] = rs_e(v0).astype(BF16)
    pair = device(x, y, 2 * s + 1 - zl, c)
    cross = remote(gb.at[v0, y, x], z1, zsend, zrecv, pair)
    cross.start()
    sf[...] = rs_e(v1)
    cross.wait_recv()
    sf[...] = sf[...] + z1[...].astype(F32)
    last = remote(sf.at[sib_rows], o1, osend, orecv, sib)
    last.start()
    out_ref[:, mine] = sf[my_rows, :]
    last.wait_recv()
    out_ref[:, other] = o1[...]

    last.wait_send()
    cross.wait_send()
    give_g.wait_send()
    normed_copy().wait_send()

    @pl.loop(0, 2)
    def _(v):
        def body(cc):
            for copies in (r1_copies, r2_copies, t1_copies, t2_copies):
                for copy in copies(cc, v):
                    copy.wait_send()

        by_core(body)


def local(inputs, weights, cotangents, lengths):
    rows = inputs.shape[0] * inputs.shape[1]
    dma = pltpu.SemaphoreType.DMA
    vmem = pl.BlockSpec(memory_space=pltpu.VMEM)
    out = pl.pallas_call(
        kernel,
        out_shape=jax.ShapeDtypeStruct((32, D), F32),
        in_specs=[
            pl.BlockSpec(memory_space=pl.ANY),
            vmem,
            vmem,
            pl.BlockSpec(memory_space=pltpu.SMEM),
        ],
        out_specs=vmem,
        scratch_shapes=[
            pltpu.VMEM((8, 2, 4, 4, 64, HALF), BF16),
            pltpu.VMEM((4, ROWS, D), BF16),
            pltpu.VMEM((4, ROWS, D), F32),
            pltpu.VMEM((4, ROWS, 128), F32),
            pltpu.VMEM((ROWS, D), BF16),
            pltpu.VMEM((2, ROWS, D), BF16),
            pltpu.VMEM((2, ROWS, HALF), BF16),
            pltpu.VMEM((ROWS, D), BF16),
            pltpu.VMEM((ROWS, D), F32),
            pltpu.VMEM((2, 2, 2, 64, HALF), BF16),
            pltpu.VMEM((2, 2, 4, 64, HALF), BF16),
            pltpu.VMEM((2, 2, 32, HALF), BF16),
            pltpu.VMEM((2, 2, 64, HALF), BF16),
            pltpu.VMEM((64, HALF), BF16),
            pltpu.VMEM((64, HALF), F32),
            pltpu.VMEM((32, HALF), F32),
            dma((2,)),
            dma,
            dma,
            dma((7,)),
            dma((8,)),
            dma((8, 4)),
            dma((8, 4)),
            dma((8, 4)),
            dma((8, 4)),
            dma((8, 4)),
            dma((8, 4)),
            dma((2,)),
            dma((2,)),
            dma((2, 2)),
            dma((2, 2)),
            dma((2, 2)),
            dma((2, 2)),
            dma((2, 2)),
            dma((2, 2)),
            dma((2, 2)),
            dma((2, 2)),
            dma,
            dma,
            dma,
            dma,
        ],
        compiler_params=pltpu.CompilerParams(
            collective_id=0, has_side_effects=True, vmem_limit_bytes=62 * 2**20
        ),
        cost_estimate=pl.CostEstimate(
            flops=9 * 2 * ROWS * D * D, bytes_accessed=36 * 2**20, transcendentals=4 * ROWS * D
        ),
    )(inputs.reshape(rows, D), weights[0], cotangents.reshape(rows, D), lengths)
    return out[None]


def solution(mesh):
    in_specs = (
        P(None, "fsdp", None),
        P("section", "fsdp", None),
        P(None, "fsdp", None),
        P(None, "fsdp"),
    )
    out_specs = P("section", "fsdp", None)
    return jax.shard_map(local, mesh=mesh, in_specs=in_specs, out_specs=out_specs, check_vma=False)
```

```python
import functools

import jax
import jax.numpy as jnp
from jax import lax
from jax.experimental import pallas as pl
from jax.experimental.pallas import tpu as pltpu
from jax.sharding import PartitionSpec as P

MESH = pl.DeviceIdType.MESH
F32 = jnp.float32
BF16 = jnp.bfloat16
EPS = 1e-06
GELU_C = 0.7978845608028654
GELU_A = 0.044715

D = 2048
ROWS = 256
HALF = 1024
XY = 768
Z = HALF - XY
UNITS = 8
READY = ((4, 6, 8, 9), (6, 7, 8, 9), (6, 7, 8, 9), (6, 8, 9, 10))
FIRST, SECOND = pl.ds(0, 2), pl.ds(2, 2)
TOP, BOTTOM = pl.ds(0, 32), pl.ds(32, 32)


def position():
    s, f = lax.axis_index("section"), lax.axis_index("fsdp")
    c = lax.rem(f, 2)
    x = lax.rem(f // 2, 4)
    y = lax.rem(f // 8, 4)
    zl = f // 32
    return s, zl, x, y, c


def device(x, y, z, c):
    return (z // 2, lax.rem(z, 2) * 32 + y * 8 + x * 2 + c)


def remote(src, dst, send, recv, dev):
    return pltpu.make_async_remote_copy(
        src_ref=src, dst_ref=dst, send_sem=send, recv_sem=recv, device_id=dev, device_id_type=MESH
    )


def kernel(
    x_ref, w_ref, cot_ref, len_ref, out_ref,
    wa, wz, xs, gd, iv, gp, nw, gw, gr, gn, r1, r2, t1, t2, z1, sf, o1,
    loc, xsend, xrecv, rsend, rrecv, usend, urecv, lsend, lrecv, esend, erecv, psend, precv, qsend, qrecv, dsend, drecv,
    nsend, nrecv, r1s, r1r, r2s, r2r, t1s, t1r, t2s, t2r, zsend, zrecv, osend, orecv,
):
    s, zl, x, y, c = position()
    z = 2 * s + zl
    sib = device(x, y, z, 1 - c)
    xp, xm = lax.rem(x + 1, 4), lax.rem(x + 3, 4)
    yp, ym = lax.rem(y + 1, 4), lax.rem(y + 3, 4)
    x2, y2 = lax.rem(x + 2, 4), lax.rem(y + 2, 4)
    dxp, dxm = device(xp, y, z, c), device(xm, y, z, c)
    dyp, dym = device(x, yp, z, c), device(x, ym, z, c)

    barrier = pltpu.get_barrier_semaphore()
    for partner in (dxp, dxm, dyp, dym, sib):
        pl.semaphore_signal(barrier, inc=1, device_id=partner, device_id_type=MESH)
    for d in range(1, 8):
        pl.semaphore_signal(
            barrier, inc=1, device_id=device(x, y, lax.rem(z + d, 8), c), device_id_type=MESH
        )

    def part(core, first, width):
        return pl.ds(pl.multiple_of(core * HALF + first, 256), width)

    in_x = [
        pltpu.make_async_copy(x_ref.at[:, :, h * HALF : (h + 1) * HALF], xs.at[h], loc.at[3 * h])
        for h in range(2)
    ]
    for copy in in_x:
        copy.start()
    mine = pl.ds(pl.multiple_of(c * HALF, HALF), HALF)
    other = pl.ds(pl.multiple_of((1 - c) * HALF, HALF), HALF)
    my_rows = pl.ds(pl.multiple_of(c * 32, 32), 32)
    sib_rows = pl.ds(pl.multiple_of((1 - c) * 32, 32), 32)
    in_w = [
        pltpu.make_async_copy(src, dst, loc.at[1 + i])
        for i, (src, dst) in enumerate(
            (
                (w_ref.at[:, part(c, 0, XY)], wa.at[2 * s + c, zl, y, x, my_rows]),
                (w_ref.at[:, part(c, XY, Z)], wz.at[2 * s + c, zl, y, x, my_rows]),
            )
        )
    ]
    for copy in in_w:
        copy.start()
    for m in range(2):
        for q in range(2):
            rows = pl.ds(128 * m + 64 * q, 64)
            live = lax.broadcasted_iota(jnp.int32, (64, D), 0) < len_ref[m, q]
            gr[rows, :] = jnp.where(live, cot_ref[rows, :].astype(F32), 0.0).astype(BF16)
    pl.semaphore_wait(barrier, 12)

    def gives(core, rows):
        kh = 2 * s + core
        return (
            remote(
                w_ref.at[:, part(core, XY, Z)], wz.at[kh, zl, y, x, rows],
                xsend.at[0], xrecv.at[0], sib,
            ),
            remote(
                w_ref.at[:, part(core, 0, XY)], wa.at[kh, zl, y, x, rows],
                xsend.at[1], xrecv.at[1], sib,
            ),
        )

    for copy in gives(1 - c, my_rows):
        copy.start()
    for copy in in_x + in_w:
        copy.wait()
    for copy in gives(c, sib_rows):
        copy.wait_recv()

    def raw(d):
        block = wa.at[2 * s + c, zl, y, x]
        dest = device(x, y, lax.rem(z + d, 8), c)
        return remote(block, block, rsend.at[d - 1], rrecv.at[z], dest)

    def row(w, cc, kh, uz, i, part=None):
        if cc == 0:
            return w.at[kh, uz, i] if part is None else w.at[kh, uz, i, part]
        return w.at[kh, uz, :, i] if part is None else w.at[kh, uz, part, i]

    def chip(w, cc, kh, uz, i, part=None):
        at = (kh, uz, y, i) if cc == 0 else (kh, uz, i, x)
        return w.at[at] if part is None else w.at[at + (part,)]

    def p_copies(w, cc, u, b):
        kh, uz = 2 * (u // 2) + cc, lax.rem(u, 2)
        me, plus, minus = (x, xp, xm) if cc == 0 else (y, yp, ym)
        to_plus, to_minus = (dxp, dxm) if cc == 0 else (dyp, dym)
        own = chip(w, cc, kh, uz, me)
        from_minus, from_plus = chip(w, cc, kh, uz, minus, TOP), chip(w, cc, kh, uz, plus, BOTTOM)
        return (
            remote(own, own, psend.at[b, 0], precv.at[b, 0], to_plus),
            remote(own, own, psend.at[b, 1], precv.at[b, 1], to_minus),
            remote(from_minus, from_minus, psend.at[b, 2], precv.at[b, 2], to_plus),
            remote(from_plus, from_plus, psend.at[b, 3], precv.at[b, 3], to_minus),
        )

    def p_landed(w, cc, u, b, i):
        kh, uz = 2 * (u // 2) + cc, lax.rem(u, 2)
        plus, minus, far = (xp, xm, x2) if cc == 0 else (yp, ym, y2)
        land = (
            chip(w, cc, kh, uz, minus),
            chip(w, cc, kh, uz, plus),
            chip(w, cc, kh, uz, far, TOP),
            chip(w, cc, kh, uz, far, BOTTOM),
        )[i]
        remote(land, land, psend.at[b, i], precv.at[b, i], sib).wait_recv()

    def q_copies(w, cc, u, b):
        kh, uz = 2 * (u // 2) + cc, lax.rem(u, 2)
        me, plus, minus = (y, yp, ym) if cc == 0 else (x, xp, xm)
        to_plus, to_minus = (dyp, dym) if cc == 0 else (dxp, dxm)
        own = row(w, cc, kh, uz, me)
        from_minus, from_plus = row(w, cc, kh, uz, minus, FIRST), row(w, cc, kh, uz, plus, SECOND)
        return (
            remote(own, own, qsend.at[b, 0], qrecv.at[b, 0], to_plus),
            remote(own, own, qsend.at[b, 1], qrecv.at[b, 1], to_minus),
            remote(from_minus, from_minus, qsend.at[b, 2], qrecv.at[b, 2], to_plus),
            remote(from_plus, from_plus, qsend.at[b, 3], qrecv.at[b, 3], to_minus),
        )

    def q_landed(w, cc, u, b, i):
        kh, uz = 2 * (u // 2) + cc, lax.rem(u, 2)
        plus, minus, far = (yp, ym, y2) if cc == 0 else (xp, xm, x2)
        land = (
            row(w, cc, kh, uz, minus),
            row(w, cc, kh, uz, plus),
            row(w, cc, kh, uz, far, FIRST),
            row(w, cc, kh, uz, far, SECOND),
        )[i]
        remote(land, land, qsend.at[b, i], qrecv.at[b, i], sib).wait_recv()

    def d_copy(w, cc, u, b, i):
        kh, uz = 2 * (u // 2) + cc, lax.rem(u, 2)
        at = ((y, ym, yp, y2) if cc == 0 else (x, xm, xp, x2))[i]
        block = row(w, cc, kh, uz, at)
        return remote(block, block, dsend.at[b, i], drecv.at[b, i], sib)

    def by_core(body):
        for cc in (0, 1):
            pl.when(c == cc)(functools.partial(body, cc))

    def unit(t):
        rest = t - 2
        rest = jnp.where(rest < 2 * s, rest, rest + 2)
        return jnp.where(t == 0, z, jnp.where(t == 1, 2 * s + 1 - zl, rest))

    def stage_p1(w, u, b):
        def body(cc):
            copies = p_copies(w, cc, u, b)
            copies[0].start()
            copies[1].start()

        by_core(body)

    def raw_landed(u):
        block = wa.at[2 * (u // 2) + c, lax.rem(u, 2), y, x]
        remote(block, block, rsend.at[0], rrecv.at[u], sib).wait_recv()

    def stage_p2(w, u, b):
        def body(cc):
            copies = p_copies(w, cc, u, b)
            p_landed(w, cc, u, b, 0)
            copies[2].start()
            p_landed(w, cc, u, b, 1)
            copies[3].start()

        by_core(body)

    def stage_q1(w, u, b):
        def body(cc):
            copies = q_copies(w, cc, u, b)
            p_landed(w, cc, u, b, 2)
            p_landed(w, cc, u, b, 3)
            copies[0].start()
            copies[1].start()
            d_copy(w, cc, u, b, 0).start()

        by_core(body)

    def stage_q2(w, u, b):
        def body(cc):
            copies = q_copies(w, cc, u, b)
            q_landed(w, cc, u, b, 0)
            copies[2].start()
            q_landed(w, cc, u, b, 1)
            copies[3].start()
            d_copy(w, cc, u, b, 1).start()
            d_copy(w, cc, u, b, 2).start()

        by_core(body)

    def stage_f(w, u, b):
        def body(cc):
            q_landed(w, cc, u, b, 2)
            q_landed(w, cc, u, b, 3)
            d_copy(w, cc, u, b, 3).start()

        by_core(body)

    PARTS = (pl.ds(0, 2), pl.ds(2, 2))
    above, below = device(x, y, lax.rem(z + 1, 8), c), device(x, y, lax.rem(z + 7, 8), c)

    def plane(d, part, core=None):
        v = lax.rem(z + 8 + d, 8)
        core = c if core is None else core
        return wz.at[2 * (v // 2) + core, lax.rem(v, 2), PARTS[part]]

    def up(r, part):
        block = plane(1 - r, part)
        return remote(block, block, usend.at[r - 1, part], urecv.at[r - 1, part], above)

    def down(r, part):
        block = plane(r - 1, part)
        return remote(block, block, lsend.at[r - 1, part], lrecv.at[r - 1, part], below)

    def up_landed(r, part):
        block = plane(-r, part)
        remote(block, block, usend.at[r - 1, part], urecv.at[r - 1, part], above).wait_recv()

    def down_landed(r, part):
        block = plane(r, part)
        remote(block, block, lsend.at[r - 1, part], lrecv.at[r - 1, part], below).wait_recv()

    def e_copy(slot, part):
        d = (-1, -2, -3, 1, 2, 3, 4)[slot]
        block = plane(d, part)
        return remote(block, block, esend.at[slot, part], erecv.at[slot, part], sib)

    def relay(r, part):
        up_landed(r, part)
        if r < 3 or part == 0:
            up(r + 1, part).start()
        down_landed(r, part)
        if r < 3 or part == 1:
            down(r + 1, part).start()
        e_copy(r - 1, part).start()
        e_copy(r + 2, part).start()

    def relay_end():
        up_landed(4, 0)
        e_copy(6, 0).start()
        down_landed(4, 1)
        e_copy(6, 1).start()

    def normed_copy():
        return remote(nw.at[c], nw.at[c], nsend.at[0], nrecv.at[0], sib)

    def section_rows(k, i):
        at = pl.ds(pl.multiple_of(lax.rem(i, 2) * 32, 32), 32)
        halves = [xs[2 * k + h, i // 2, at, :].astype(F32) for h in range(2)]
        return jnp.concatenate(halves, axis=1)

    def forward(k):
        @pl.loop(0, 2)
        def _(uz):
            u = 2 * k + uz

            def body(cc):
                for i in range(4):
                    d_copy(wa, 1 - cc, u, u, i).wait_recv()

                @pl.when(u == z)
                def _():
                    for i in range(4):
                        d_copy(wz, 1 - cc, u, UNITS, i).wait_recv()

            by_core(body)

            @pl.when(u != z)
            def _():
                d = lax.rem(u - z + 8, 8)
                slot = jnp.where(d < 4, 2 + d, jnp.where(d == 4, 6, 7 - d))
                for i in range(2):
                    block = wz.at[2 * k + 1 - c, uz, PARTS[i]]
                    remote(block, block, esend.at[slot, i], erecv.at[slot, i], sib).wait_recv()

        @pl.loop(0, ROWS // 32)
        def _(i):
            rows = pl.ds(pl.multiple_of(i * 32, 32), 32)
            xf = section_rows(k, i)
            inv = lax.rsqrt(jnp.mean(xf * xf, axis=-1, keepdims=True) + EPS)
            iv[k, rows, :] = jnp.broadcast_to(inv, (32, 128))
            gp[rows, :] = (xf * inv).astype(BF16)

        @pl.when(k == s)
        def _():
            nw[c] = gp[...]
            normed_copy().start()

        def section_columns(w, h, first, width):
            cols = part(h, first, width)
            u = jnp.dot(gp[...], w.reshape(D, width), preferred_element_type=F32)
            uu = u * u
            t = jnp.tanh((GELU_C * u) * (1.0 + GELU_A * uu))
            cdf = 0.5 * (1.0 + t)
            gd[k, :, cols] = cdf + (0.5 * GELU_C) * u * (1.0 - t * t) * (
                1.0 + (3.0 * GELU_A) * uu
            )

            @pl.when(k < 3)
            def _():
                nxt = jnp.minimum(k + 1, 3)
                inside = pl.ds(first, width)
                before = xs[2 * k + h, :, :, inside].reshape(ROWS, width)
                after = (before.astype(F32) + u * cdf).astype(BF16)
                xs[2 * nxt + h, :, :, inside] = after.reshape(4, 64, width)

        @pl.loop(0, 2)
        def _(h):
            section_columns(wa[2 * k + h], h, 0, XY)
            section_columns(wz[2 * k + h], h, XY, Z)

    own = unit(0)
    stage_p1(wz, own, UNITS)
    stage_p1(wa, own, own)
    for d in (1, 7, 2, 6, 3, 5, 4):
        raw(d).start()
    stage_p2(wz, own, UNITS)
    stage_p2(wa, own, own)
    stage_q1(wz, own, UNITS)
    stage_q1(wa, own, own)
    near = unit(1)
    raw_landed(near)
    stage_p1(wa, near, near)
    stage_q2(wz, own, UNITS)
    stage_f(wz, own, UNITS)
    for part_ in range(2):
        up(1, part_).start()
        down(1, part_).start()
    stage_p2(wa, near, near)

    @pl.loop(1, UNITS + 3)
    def _(i):
        def when_unit(ahead, stage):
            @pl.when((i + ahead >= 0) & (i + ahead < UNITS))
            def _():
                u = unit(i + ahead)
                stage(wa, u, u)

        def first_stage(w, u, b):
            raw_landed(u)
            stage_p1(w, u, b)

        when_unit(1, first_stage)
        when_unit(0, stage_q1)
        when_unit(1, stage_p2)
        when_unit(-1, stage_q2)
        when_unit(-2, stage_f)
        pl.when(i == 1)(lambda: relay(1, 0))
        pl.when(i == 2)(lambda: relay(1, 1))
        pl.when(i == 3)(lambda: relay(2, 0))
        pl.when(i == 4)(lambda: relay(2, 1))

        @pl.when(i == 5)
        def _():
            relay(3, 0)
            relay(3, 1)

        pl.when(i == 6)(relay_end)
        k = -1
        for section in range(4):
            for number in range(4):
                k = jnp.where((s == section) & (i == READY[section][number]), number, k)
        pl.when(k >= 0)(lambda: forward(jnp.maximum(k, 0)))

    def grad_pre(k):
        @pl.loop(0, ROWS // 32)
        def _(i):
            rows = pl.ds(pl.multiple_of(i * 32, 32), 32)
            gp[rows, :] = (gr[rows, :].astype(F32) * gd[k, rows, :]).astype(BF16)

    @pl.loop(0, 3 - s)
    def _(step):
        k = 3 - step
        grad_pre(k)

        @pl.loop(0, 4)
        def _(j):
            total = None
            for h in range(2):
                for w, first, width in ((wa, 0, XY), (wz, XY, Z)):
                    tile = w[2 * k + h, j // 2, pl.ds(lax.rem(j, 2) * 2, 2)].reshape(512, width)
                    term = lax.dot_general(
                        gp[:, h * HALF + first : h * HALF + first + width], tile,
                        (((1,), (1,)), ((), ())), preferred_element_type=F32,
                    )
                    total = term if total is None else total + term
            gn[:, pl.ds(pl.multiple_of(j * 512, 512), 512)] = total

        @pl.loop(0, ROWS // 32)
        def _(i):
            rows = pl.ds(pl.multiple_of(i * 32, 32), 32)
            xf = section_rows(k, i)
            g = gn[rows, :]
            inv = iv[k, rows, :][:, :1]
            mean = jnp.mean(g * xf, axis=-1, keepdims=True)
            gr[rows, :] = (
                gr[rows, :].astype(F32) + inv * g - xf * (inv * inv * inv * mean)
            ).astype(BF16)

    grad_pre(s)
    gw[c] = gp[:, mine]
    give_g = remote(gp.at[:, other], gw.at[c], nsend.at[1], nrecv.at[1], sib)
    give_g.start()

    remote(nw.at[1 - c], nw.at[1 - c], nsend.at[0], nrecv.at[0], sib).wait_recv()
    remote(gw.at[1 - c], gw.at[1 - c], nsend.at[1], nrecv.at[1], sib).wait_recv()

    def weight_term(v):
        @pl.loop(0, 4)
        def _(j):
            cols = pl.ds(pl.multiple_of(v * HALF + j * 256, 256), 256)
            total = None
            for half in range(2):
                part = lax.dot_general(
                    nw[half, :, cols], gw[half], (((0,), (0,)), ((), ())),
                    preferred_element_type=F32,
                )
                total = part if total is None else total + part
            xs[4 * v + j] = total.astype(BF16).reshape(4, 64, HALF)

    def grow(cc, v, i, first=0, count=4):
        if cc == 0:
            return xs.at[4 * v + i, pl.ds(first, count)]
        return xs.at[pl.ds(4 * v + first, count), i]

    def gchip(cc, v, i, part=None):
        at = (4 * v + y, i) if cc == 0 else (4 * v + i, x)
        return xs.at[at] if part is None else xs.at[at + (part,)]

    def r1_copies(cc, v):
        far = y2 if cc == 0 else x2
        to_plus, to_minus = (dyp, dym) if cc == 0 else (dxp, dxm)
        return (
            remote(grow(cc, v, far, 0, 2), r1.at[v, 0], r1s.at[v, 0], r1r.at[v, 0], to_plus),
            remote(grow(cc, v, far, 2, 2), r1.at[v, 1], r1s.at[v, 1], r1r.at[v, 1], to_minus),
        )

    def r2_copies(cc, v):
        plus, minus = (yp, ym) if cc == 0 else (xp, xm)
        to_plus, to_minus = (dyp, dym) if cc == 0 else (dxp, dxm)
        return (
            remote(grow(cc, v, plus), r2.at[v, 0], r2s.at[v, 0], r2r.at[v, 0], to_plus),
            remote(grow(cc, v, minus), r2.at[v, 1], r2s.at[v, 1], r2r.at[v, 1], to_minus),
        )

    def t1_copies(cc, v):
        far = x2 if cc == 0 else y2
        to_plus, to_minus = (dxp, dxm) if cc == 0 else (dyp, dym)
        return (
            remote(gchip(cc, v, far, TOP), t1.at[v, 0], t1s.at[v, 0], t1r.at[v, 0], to_plus),
            remote(gchip(cc, v, far, BOTTOM), t1.at[v, 1], t1s.at[v, 1], t1r.at[v, 1], to_minus),
        )

    def t2_copies(cc, v):
        plus, minus = (xp, xm) if cc == 0 else (yp, ym)
        to_plus, to_minus = (dxp, dxm) if cc == 0 else (dyp, dym)
        return (
            remote(gchip(cc, v, plus), t2.at[v, 0], t2s.at[v, 0], t2r.at[v, 0], to_plus),
            remote(gchip(cc, v, minus), t2.at[v, 1], t2s.at[v, 1], t2r.at[v, 1], to_minus),
        )

    def add_into(ref, *others):
        total = ref[...].astype(F32)
        for more in others:
            total = total + more[...].astype(F32)
        ref[...] = total.astype(BF16)

    def rs_a(v):
        def body(cc):
            for copy in r1_copies(cc, v):
                copy.start()

        by_core(body)

    def rs_b(v):
        def body(cc):
            plus, minus = (yp, ym) if cc == 0 else (xp, xm)
            arrive, leave = r1_copies(cc, v), r2_copies(cc, v)
            arrive[0].wait_recv()
            add_into(grow(cc, v, plus, 0, 2), r1.at[v, 0])
            leave[0].start()
            arrive[1].wait_recv()
            add_into(grow(cc, v, minus, 2, 2), r1.at[v, 1])
            leave[1].start()

        by_core(body)

    def rs_c(v):
        def body(cc):
            me = y if cc == 0 else x
            arrive, leave = r2_copies(cc, v), t1_copies(cc, v)
            arrive[0].wait_recv()
            arrive[1].wait_recv()
            for i in range(4):
                block = gchip(cc, v, i)
                add_into(block, r2.at[v, 0, i], r2.at[v, 1, i])
            for copy in leave:
                copy.start()

        by_core(body)

    def rs_d(v):
        def body(cc):
            plus, minus = (xp, xm) if cc == 0 else (yp, ym)
            arrive, leave = t1_copies(cc, v), t2_copies(cc, v)
            arrive[0].wait_recv()
            add_into(gchip(cc, v, plus, TOP), t1.at[v, 0])
            leave[0].start()
            arrive[1].wait_recv()
            add_into(gchip(cc, v, minus, BOTTOM), t1.at[v, 1])
            leave[1].start()

        by_core(body)

    def rs_e(v):
        def body(cc):
            for copy in t2_copies(cc, v):
                copy.wait_recv()

        by_core(body)
        return (
            xs[4 * v + y, x].astype(F32) + t2[v, 0].astype(F32) + t2[v, 1].astype(F32)
        )

    v0, v1 = 1 - zl, zl
    weight_term(v0)
    rs_a(v0)
    weight_term(v1)
    rs_a(v1)
    rs_b(v0)
    rs_b(v1)
    rs_c(v0)
    rs_c(v1)
    rs_d(v0)
    rs_d(v1)
    xs[4 * v0 + y, x] = rs_e(v0).astype(BF16)
    pair = device(x, y, 2 * s + 1 - zl, c)
    cross = remote(xs.at[4 * v0 + y, x], z1, zsend, zrecv, pair)
    cross.start()
    sf[...] = rs_e(v1)
    cross.wait_recv()
    sf[...] = sf[...] + z1[...].astype(F32)
    last = remote(sf.at[sib_rows], o1, osend, orecv, sib)
    last.start()
    out_ref[:, mine] = sf[my_rows, :]
    last.wait_recv()
    out_ref[:, other] = o1[...]

    for copy in gives(1 - c, my_rows):
        copy.wait_send()
    for d in range(1, 8):
        raw(d).wait_send()

    @pl.loop(0, UNITS)
    def _(u):
        def body(cc):
            for copy in p_copies(wa, cc, u, u) + q_copies(wa, cc, u, u):
                copy.wait_send()
            for i in range(4):
                d_copy(wa, cc, u, u, i).wait_send()

        by_core(body)

    def own_sent(cc):
        for copy in p_copies(wz, cc, own, UNITS) + q_copies(wz, cc, own, UNITS):
            copy.wait_send()
        for i in range(4):
            d_copy(wz, cc, own, UNITS, i).wait_send()

    by_core(own_sent)
    for i in range(2):
        for r in range(1, 4):
            up(r, i).wait_send()
            down(r, i).wait_send()
        for slot in range(7):
            e_copy(slot, i).wait_send()
    up(4, 0).wait_send()
    down(4, 1).wait_send()
    last.wait_send()
    cross.wait_send()
    give_g.wait_send()
    normed_copy().wait_send()

    @pl.loop(0, 2)
    def _(v):
        def body(cc):
            for copies in (r1_copies, r2_copies, t1_copies, t2_copies):
                for copy in copies(cc, v):
                    copy.wait_send()

        by_core(body)


def local(inputs, weights, cotangents, lengths):
    rows = inputs.shape[0] * inputs.shape[1]
    dma = pltpu.SemaphoreType.DMA
    vmem = pl.BlockSpec(memory_space=pltpu.VMEM)
    out = pl.pallas_call(
        kernel,
        out_shape=jax.ShapeDtypeStruct((32, D), F32),
        in_specs=[
            pl.BlockSpec(memory_space=pl.ANY),
            vmem,
            vmem,
            pl.BlockSpec(memory_space=pltpu.SMEM),
        ],
        out_specs=vmem,
        scratch_shapes=[
            pltpu.VMEM((8, 2, 4, 4, 64, XY), BF16),
            pltpu.VMEM((8, 2, 4, 4, 64, Z), BF16),
            pltpu.VMEM((8, 4, 64, HALF), BF16),
            pltpu.VMEM((4, ROWS, D), F32),
            pltpu.VMEM((4, ROWS, 128), F32),
            pltpu.VMEM((ROWS, D), BF16),
            pltpu.VMEM((2, ROWS, D), BF16),
            pltpu.VMEM((2, ROWS, HALF), BF16),
            pltpu.VMEM((ROWS, D), BF16),
            pltpu.VMEM((ROWS, D), F32),
            pltpu.VMEM((2, 2, 2, 64, HALF), BF16),
            pltpu.VMEM((2, 2, 4, 64, HALF), BF16),
            pltpu.VMEM((2, 2, 32, HALF), BF16),
            pltpu.VMEM((2, 2, 64, HALF), BF16),
            pltpu.VMEM((64, HALF), BF16),
            pltpu.VMEM((64, HALF), F32),
            pltpu.VMEM((32, HALF), F32),
            dma((4,)),
            dma((2,)),
            dma((2,)),
            dma((7,)),
            dma((8,)),
            dma((4, 2)),
            dma((4, 2)),
            dma((4, 2)),
            dma((4, 2)),
            dma((7, 2)),
            dma((7, 2)),
            dma((9, 4)),
            dma((9, 4)),
            dma((9, 4)),
            dma((9, 4)),
            dma((9, 4)),
            dma((9, 4)),
            dma((2,)),
            dma((2,)),
            dma((2, 2)),
            dma((2, 2)),
            dma((2, 2)),
            dma((2, 2)),
            dma((2, 2)),
            dma((2, 2)),
            dma((2, 2)),
            dma((2, 2)),
            dma,
            dma,
            dma,
            dma,
        ],
        compiler_params=pltpu.CompilerParams(
            collective_id=0, has_side_effects=True, vmem_limit_bytes=63 * 2**20
        ),
        cost_estimate=pl.CostEstimate(
            flops=9 * 2 * ROWS * D * D, bytes_accessed=36 * 2**20, transcendentals=4 * ROWS * D
        ),
    )(inputs.reshape(4, rows // 4, D), weights[0], cotangents.reshape(rows, D), lengths)
    return out[None]


def solution(mesh):
    in_specs = (
        P(None, "fsdp", None),
        P("section", "fsdp", None),
        P(None, "fsdp", None),
        P(None, "fsdp"),
    )
    out_specs = P("section", "fsdp", None)
    return jax.shard_map(local, mesh=mesh, in_specs=in_specs, out_specs=out_specs, check_vma=False)
```

```python
import functools

import jax
import jax.numpy as jnp
from jax import lax
from jax.experimental import pallas as pl
from jax.experimental.pallas import tpu as pltpu
from jax.sharding import PartitionSpec as P

MESH = pl.DeviceIdType.MESH
F32 = jnp.float32
BF16 = jnp.bfloat16
EPS = 1e-06
GELU_C = 0.7978845608028654
GELU_A = 0.044715

D = 2048
ROWS = 256
HALF = 1024
XY = 768
Z = HALF - XY
UNITS = 8
READY = ((3, 6, 7, 9), (6, 7, 8, 9), (7, 8, 9, 10), (6, 7, 9, 10))
FIRST, SECOND = pl.ds(0, 2), pl.ds(2, 2)
TOP, BOTTOM = pl.ds(0, 32), pl.ds(32, 32)


def position():
    s, f = lax.axis_index("section"), lax.axis_index("fsdp")
    c = lax.rem(f, 2)
    x = lax.rem(f // 2, 4)
    y = lax.rem(f // 8, 4)
    zl = f // 32
    return s, zl, x, y, c


def device(x, y, z, c):
    return (z // 2, lax.rem(z, 2) * 32 + y * 8 + x * 2 + c)


def remote(src, dst, send, recv, dev):
    return pltpu.make_async_remote_copy(
        src_ref=src, dst_ref=dst, send_sem=send, recv_sem=recv, device_id=dev, device_id_type=MESH
    )


def kernel(
    x_ref, w_ref, cot_ref, len_ref, out_ref,
    wa, wz, xs, gd, iv, gp, nw, gw, gr, gn, r1, r2, t1, t2, z1, sf, o1,
    loc, xsend, xrecv, rsend, rrecv, usend, urecv, lsend, lrecv, esend, erecv, psend, precv, qsend, qrecv, dsend, drecv,
    nsend, nrecv, r1s, r1r, r2s, r2r, t1s, t1r, t2s, t2r, zsend, zrecv, osend, orecv,
):
    s, zl, x, y, c = position()
    z = 2 * s + zl
    sib = device(x, y, z, 1 - c)
    xp, xm = lax.rem(x + 1, 4), lax.rem(x + 3, 4)
    yp, ym = lax.rem(y + 1, 4), lax.rem(y + 3, 4)
    x2, y2 = lax.rem(x + 2, 4), lax.rem(y + 2, 4)
    dxp, dxm = device(xp, y, z, c), device(xm, y, z, c)
    dyp, dym = device(x, yp, z, c), device(x, ym, z, c)

    barrier = pltpu.get_barrier_semaphore()
    for partner in (dxp, dxm, dyp, dym, sib):
        pl.semaphore_signal(barrier, inc=1, device_id=partner, device_id_type=MESH)
    for d in range(1, 8):
        pl.semaphore_signal(
            barrier, inc=1, device_id=device(x, y, lax.rem(z + d, 8), c), device_id_type=MESH
        )

    def part(core, first, width):
        return pl.ds(pl.multiple_of(core * HALF + first, 256), width)

    in_x = [
        pltpu.make_async_copy(x_ref.at[:, :, h * HALF : (h + 1) * HALF], xs.at[h], loc.at[3 * h])
        for h in range(2)
    ]
    for copy in in_x:
        copy.start()
    mine = pl.ds(pl.multiple_of(c * HALF, HALF), HALF)
    other = pl.ds(pl.multiple_of((1 - c) * HALF, HALF), HALF)
    my_rows = pl.ds(pl.multiple_of(c * 32, 32), 32)
    sib_rows = pl.ds(pl.multiple_of((1 - c) * 32, 32), 32)
    in_w = [
        pltpu.make_async_copy(src, dst, loc.at[1 + i])
        for i, (src, dst) in enumerate(
            (
                (w_ref.at[:, part(c, 0, XY)], wa.at[2 * s + c, zl, y, x, my_rows]),
                (w_ref.at[:, part(c, XY, Z)], wz.at[2 * s + c, zl, y, x, my_rows]),
            )
        )
    ]
    for copy in in_w:
        copy.start()
    pl.semaphore_wait(barrier, 12)

    def gives(core, rows):
        kh = 2 * s + core
        return (
            remote(
                w_ref.at[:, part(core, XY, Z)], wz.at[kh, zl, y, x, rows],
                xsend.at[0], xrecv.at[0], sib,
            ),
            remote(
                w_ref.at[:, part(core, 0, XY)], wa.at[kh, zl, y, x, rows],
                xsend.at[1], xrecv.at[1], sib,
            ),
        )

    for copy in gives(1 - c, my_rows):
        copy.start()
    for copy in in_w:
        copy.wait()
    for copy in gives(c, sib_rows):
        copy.wait_recv()

    def raw(d):
        block = wa.at[2 * s + c, zl, y, x]
        dest = device(x, y, lax.rem(z + d, 8), c)
        return remote(block, block, rsend.at[d - 1], rrecv.at[z], dest)

    def row(w, cc, kh, uz, i, part=None):
        if cc == 0:
            return w.at[kh, uz, i] if part is None else w.at[kh, uz, i, part]
        return w.at[kh, uz, :, i] if part is None else w.at[kh, uz, part, i]

    def chip(w, cc, kh, uz, i, part=None):
        at = (kh, uz, y, i) if cc == 0 else (kh, uz, i, x)
        return w.at[at] if part is None else w.at[at + (part,)]

    def p_copies(w, cc, u, b):
        kh, uz = 2 * (u // 2) + cc, lax.rem(u, 2)
        me, plus, minus = (x, xp, xm) if cc == 0 else (y, yp, ym)
        to_plus, to_minus = (dxp, dxm) if cc == 0 else (dyp, dym)
        own = chip(w, cc, kh, uz, me)
        from_minus, from_plus = chip(w, cc, kh, uz, minus, TOP), chip(w, cc, kh, uz, plus, BOTTOM)
        return (
            remote(own, own, psend.at[b, 0], precv.at[b, 0], to_plus),
            remote(own, own, psend.at[b, 1], precv.at[b, 1], to_minus),
            remote(from_minus, from_minus, psend.at[b, 2], precv.at[b, 2], to_plus),
            remote(from_plus, from_plus, psend.at[b, 3], precv.at[b, 3], to_minus),
        )

    def p_landed(w, cc, u, b, i):
        kh, uz = 2 * (u // 2) + cc, lax.rem(u, 2)
        plus, minus, far = (xp, xm, x2) if cc == 0 else (yp, ym, y2)
        land = (
            chip(w, cc, kh, uz, minus),
            chip(w, cc, kh, uz, plus),
            chip(w, cc, kh, uz, far, TOP),
            chip(w, cc, kh, uz, far, BOTTOM),
        )[i]
        remote(land, land, psend.at[b, i], precv.at[b, i], sib).wait_recv()

    def q_copies(w, cc, u, b):
        kh, uz = 2 * (u // 2) + cc, lax.rem(u, 2)
        me, plus, minus = (y, yp, ym) if cc == 0 else (x, xp, xm)
        to_plus, to_minus = (dyp, dym) if cc == 0 else (dxp, dxm)
        first, second = row(w, cc, kh, uz, me, FIRST), row(w, cc, kh, uz, me, SECOND)
        from_minus, from_plus = row(w, cc, kh, uz, minus, FIRST), row(w, cc, kh, uz, plus, SECOND)
        return (
            remote(first, first, qsend.at[b, 0], qrecv.at[b, 0], to_plus),
            remote(second, second, qsend.at[b, 1], qrecv.at[b, 1], to_minus),
            remote(second, second, qsend.at[b, 2], qrecv.at[b, 2], to_plus),
            remote(first, first, qsend.at[b, 3], qrecv.at[b, 3], to_minus),
            remote(from_minus, from_minus, qsend.at[b, 4], qrecv.at[b, 4], to_plus),
            remote(from_plus, from_plus, qsend.at[b, 5], qrecv.at[b, 5], to_minus),
        )

    def q_landed(w, cc, u, b, i):
        kh, uz = 2 * (u // 2) + cc, lax.rem(u, 2)
        plus, minus, far = (yp, ym, y2) if cc == 0 else (xp, xm, x2)
        land = (
            row(w, cc, kh, uz, minus, FIRST),
            row(w, cc, kh, uz, plus, SECOND),
            row(w, cc, kh, uz, minus, SECOND),
            row(w, cc, kh, uz, plus, FIRST),
            row(w, cc, kh, uz, far, FIRST),
            row(w, cc, kh, uz, far, SECOND),
        )[i]
        remote(land, land, qsend.at[b, i], qrecv.at[b, i], sib).wait_recv()

    def d_copy(w, cc, u, b, i):
        kh, uz = 2 * (u // 2) + cc, lax.rem(u, 2)
        at = ((y, ym, yp, y2) if cc == 0 else (x, xm, xp, x2))[i]
        block = row(w, cc, kh, uz, at)
        return remote(block, block, dsend.at[b, i], drecv.at[b, i], sib)

    def by_core(body):
        for cc in (0, 1):
            pl.when(c == cc)(functools.partial(body, cc))

    def unit(t):
        rest = t - 2
        near = jnp.where(rest < 2, rest + 2, jnp.where(rest < 4, rest - 2, rest + 2))
        rest = jnp.where(s == 2, near, jnp.where(rest < 2 * s, rest, rest + 2))
        return jnp.where(t == 0, z, jnp.where(t == 1, 2 * s + 1 - zl, rest))

    def stage_p1(w, u, b):
        def body(cc):
            copies = p_copies(w, cc, u, b)
            copies[0].start()
            copies[1].start()

        by_core(body)

    def raw_landed(u):
        block = wa.at[2 * (u // 2) + c, lax.rem(u, 2), y, x]
        remote(block, block, rsend.at[0], rrecv.at[u], sib).wait_recv()

    def stage_p2(w, u, b):
        def body(cc):
            copies = p_copies(w, cc, u, b)
            p_landed(w, cc, u, b, 0)
            copies[2].start()
            p_landed(w, cc, u, b, 1)
            copies[3].start()

        by_core(body)

    def stage_q1(w, u, b):
        def body(cc):
            copies = q_copies(w, cc, u, b)
            p_landed(w, cc, u, b, 2)
            p_landed(w, cc, u, b, 3)
            for copy in copies[:4]:
                copy.start()
            d_copy(w, cc, u, b, 0).start()

        by_core(body)

    def stage_q2(w, u, b):
        def body(cc):
            copies = q_copies(w, cc, u, b)
            q_landed(w, cc, u, b, 0)
            copies[4].start()
            q_landed(w, cc, u, b, 1)
            copies[5].start()

        by_core(body)

    def stage_f(w, u, b):
        def body(cc):
            q_landed(w, cc, u, b, 2)
            d_copy(w, cc, u, b, 1).start()
            q_landed(w, cc, u, b, 3)
            d_copy(w, cc, u, b, 2).start()
            q_landed(w, cc, u, b, 4)
            q_landed(w, cc, u, b, 5)
            d_copy(w, cc, u, b, 3).start()

        by_core(body)

    PARTS = (pl.ds(0, 2), pl.ds(2, 2))
    above, below = device(x, y, lax.rem(z + 1, 8), c), device(x, y, lax.rem(z + 7, 8), c)

    def plane(d, part, core=None):
        v = lax.rem(z + 8 + d, 8)
        core = c if core is None else core
        return wz.at[2 * (v // 2) + core, lax.rem(v, 2), PARTS[part]]

    def up(r, part):
        block = plane(1 - r, part)
        return remote(block, block, usend.at[r - 1, part], urecv.at[r - 1, part], above)

    def down(r, part):
        block = plane(r - 1, part)
        return remote(block, block, lsend.at[r - 1, part], lrecv.at[r - 1, part], below)

    def up_landed(r, part):
        block = plane(-r, part)
        remote(block, block, usend.at[r - 1, part], urecv.at[r - 1, part], above).wait_recv()

    def down_landed(r, part):
        block = plane(r, part)
        remote(block, block, lsend.at[r - 1, part], lrecv.at[r - 1, part], below).wait_recv()

    def e_copy(slot, part):
        d = (-1, -2, -3, 1, 2, 3, 4)[slot]
        block = plane(d, part)
        return remote(block, block, esend.at[slot, part], erecv.at[slot, part], sib)

    def relay(r, part):
        up_landed(r, part)
        if r < 3 or part == 0:
            up(r + 1, part).start()
        down_landed(r, part)
        if r < 3 or part == 1:
            down(r + 1, part).start()
        e_copy(r - 1, part).start()
        e_copy(r + 2, part).start()

    def relay_end():
        up_landed(4, 0)
        e_copy(6, 0).start()
        down_landed(4, 1)
        e_copy(6, 1).start()

    def normed_copy():
        return remote(nw.at[c], nw.at[c], nsend.at[0], nrecv.at[0], sib)

    def section_rows(k, i):
        at = pl.ds(pl.multiple_of(lax.rem(i, 2) * 32, 32), 32)
        halves = [xs[2 * k + h, i // 2, at, :].astype(F32) for h in range(2)]
        return jnp.concatenate(halves, axis=1)

    def forward(k):
        @pl.loop(0, 2)
        def _(uz):
            u = 2 * k + uz

            def body(cc):
                for i in range(4):
                    d_copy(wa, 1 - cc, u, u, i).wait_recv()

                @pl.when(u == z)
                def _():
                    for i in range(4):
                        d_copy(wz, 1 - cc, u, UNITS, i).wait_recv()

            by_core(body)

            @pl.when(u != z)
            def _():
                d = lax.rem(u - z + 8, 8)
                slot = jnp.where(d < 4, 2 + d, jnp.where(d == 4, 6, 7 - d))
                for i in range(2):
                    block = wz.at[2 * k + 1 - c, uz, PARTS[i]]
                    remote(block, block, esend.at[slot, i], erecv.at[slot, i], sib).wait_recv()

        @pl.loop(0, ROWS // 32)
        def _(i):
            rows = pl.ds(pl.multiple_of(i * 32, 32), 32)
            xf = section_rows(k, i)
            inv = lax.rsqrt(jnp.mean(xf * xf, axis=-1, keepdims=True) + EPS)
            iv[k, rows, :] = jnp.broadcast_to(inv, (32, 128))
            gp[rows, :] = (xf * inv).astype(BF16)

        @pl.when(k == s)
        def _():
            nw[c] = gp[...]
            normed_copy().start()

        def section_columns(w, h, first, width):
            cols = part(h, first, width)
            u = jnp.dot(gp[...], w.reshape(D, width), preferred_element_type=F32)
            uu = u * u
            t = jnp.tanh((GELU_C * u) * (1.0 + GELU_A * uu))
            cdf = 0.5 * (1.0 + t)
            gd[k, :, cols] = cdf + (0.5 * GELU_C) * u * (1.0 - t * t) * (
                1.0 + (3.0 * GELU_A) * uu
            )

            @pl.when(k < 3)
            def _():
                nxt = jnp.minimum(k + 1, 3)
                inside = pl.ds(first, width)
                before = xs[2 * k + h, :, :, inside].reshape(ROWS, width)
                after = (before.astype(F32) + u * cdf).astype(BF16)
                xs[2 * nxt + h, :, :, inside] = after.reshape(4, 64, width)

        @pl.loop(0, 2)
        def _(h):
            section_columns(wa[2 * k + h], h, 0, XY)
            section_columns(wz[2 * k + h], h, XY, Z)

    own = unit(0)
    stage_p1(wz, own, UNITS)
    stage_p1(wa, own, own)
    for d in (1, 7, 2, 6, 3, 5, 4):
        raw(d).start()
    for m in range(2):
        for q in range(2):
            rows = pl.ds(128 * m + 64 * q, 64)
            live = lax.broadcasted_iota(jnp.int32, (64, D), 0) < len_ref[m, q]
            gr[rows, :] = jnp.where(live, cot_ref[rows, :].astype(F32), 0.0).astype(BF16)
    for copy in in_x:
        copy.wait()
    stage_p2(wz, own, UNITS)
    stage_p2(wa, own, own)
    stage_q1(wz, own, UNITS)
    stage_q1(wa, own, own)
    near = unit(1)
    raw_landed(near)
    stage_p1(wa, near, near)
    stage_q2(wz, own, UNITS)
    stage_p2(wa, near, near)
    stage_q2(wa, own, own)
    stage_f(wz, own, UNITS)
    for i in range(2):
        up(1, i).start()
        down(1, i).start()
    third = unit(2)
    raw_landed(third)
    stage_p1(wa, third, third)

    @pl.loop(1, UNITS + 3)
    def _(i):
        def when_unit(ahead, stage):
            @pl.when((i + ahead >= 0) & (i + ahead < UNITS))
            def _():
                u = unit(i + ahead)
                stage(wa, u, u)

        def first_stage(w, u, b):
            raw_landed(u)
            stage_p1(w, u, b)

        when_unit(0, stage_q1)
        when_unit(2, first_stage)
        when_unit(1, stage_p2)
        k = -1
        for section in range(4):
            for number in range(4):
                k = jnp.where((s == section) & (i == READY[section][number]), number, k)
        pl.when(k >= 0)(lambda: forward(jnp.maximum(k, 0)))
        when_unit(0, stage_q2)
        when_unit(-1, stage_f)
        pl.when(i == 1)(lambda: relay(1, 0))
        pl.when(i == 2)(lambda: relay(1, 1))
        pl.when(i == 3)(lambda: relay(2, 0))
        pl.when(i == 4)(lambda: relay(2, 1))

        @pl.when(i == 5)
        def _():
            relay(3, 0)
            relay(3, 1)

        pl.when(i == 6)(relay_end)

    def grad_pre(k):
        @pl.loop(0, ROWS // 32)
        def _(i):
            rows = pl.ds(pl.multiple_of(i * 32, 32), 32)
            gp[rows, :] = (gr[rows, :].astype(F32) * gd[k, rows, :]).astype(BF16)

    @pl.loop(0, 3 - s)
    def _(step):
        k = 3 - step
        grad_pre(k)

        @pl.loop(0, 4)
        def _(j):
            total = None
            for h in range(2):
                for w, first, width in ((wa, 0, XY), (wz, XY, Z)):
                    tile = w[2 * k + h, j // 2, pl.ds(lax.rem(j, 2) * 2, 2)].reshape(512, width)
                    term = lax.dot_general(
                        gp[:, h * HALF + first : h * HALF + first + width], tile,
                        (((1,), (1,)), ((), ())), preferred_element_type=F32,
                    )
                    total = term if total is None else total + term
            gn[:, pl.ds(pl.multiple_of(j * 512, 512), 512)] = total

        @pl.loop(0, ROWS // 32)
        def _(i):
            rows = pl.ds(pl.multiple_of(i * 32, 32), 32)
            xf = section_rows(k, i)
            g = gn[rows, :]
            inv = iv[k, rows, :][:, :1]
            mean = jnp.mean(g * xf, axis=-1, keepdims=True)
            gr[rows, :] = (
                gr[rows, :].astype(F32) + inv * g - xf * (inv * inv * inv * mean)
            ).astype(BF16)

    grad_pre(s)
    gw[c] = gp[:, mine]
    give_g = remote(gp.at[:, other], gw.at[c], nsend.at[1], nrecv.at[1], sib)
    give_g.start()

    remote(nw.at[1 - c], nw.at[1 - c], nsend.at[0], nrecv.at[0], sib).wait_recv()
    remote(gw.at[1 - c], gw.at[1 - c], nsend.at[1], nrecv.at[1], sib).wait_recv()

    def weight_term(v):
        @pl.loop(0, 4)
        def _(j):
            cols = pl.ds(pl.multiple_of(v * HALF + j * 256, 256), 256)
            total = None
            for half in range(2):
                part = lax.dot_general(
                    nw[half, :, cols], gw[half], (((0,), (0,)), ((), ())),
                    preferred_element_type=F32,
                )
                total = part if total is None else total + part
            xs[4 * v + j] = total.astype(BF16).reshape(4, 64, HALF)

    def grow(cc, v, i, first=0, count=4):
        if cc == 0:
            return xs.at[4 * v + i, pl.ds(first, count)]
        return xs.at[pl.ds(4 * v + first, count), i]

    def gchip(cc, v, i, part=None):
        at = (4 * v + y, i) if cc == 0 else (4 * v + i, x)
        return xs.at[at] if part is None else xs.at[at + (part,)]

    def r1_copies(cc, v):
        far = y2 if cc == 0 else x2
        to_plus, to_minus = (dyp, dym) if cc == 0 else (dxp, dxm)
        return (
            remote(grow(cc, v, far, 0, 2), r1.at[v, 0], r1s.at[v, 0], r1r.at[v, 0], to_plus),
            remote(grow(cc, v, far, 2, 2), r1.at[v, 1], r1s.at[v, 1], r1r.at[v, 1], to_minus),
        )

    def r2_copies(cc, v):
        plus, minus = (yp, ym) if cc == 0 else (xp, xm)
        to_plus, to_minus = (dyp, dym) if cc == 0 else (dxp, dxm)
        return (
            remote(grow(cc, v, plus), r2.at[v, 0], r2s.at[v, 0], r2r.at[v, 0], to_plus),
            remote(grow(cc, v, minus), r2.at[v, 1], r2s.at[v, 1], r2r.at[v, 1], to_minus),
        )

    def t1_copies(cc, v):
        far = x2 if cc == 0 else y2
        to_plus, to_minus = (dxp, dxm) if cc == 0 else (dyp, dym)
        return (
            remote(gchip(cc, v, far, TOP), t1.at[v, 0], t1s.at[v, 0], t1r.at[v, 0], to_plus),
            remote(gchip(cc, v, far, BOTTOM), t1.at[v, 1], t1s.at[v, 1], t1r.at[v, 1], to_minus),
        )

    def t2_copies(cc, v):
        plus, minus = (xp, xm) if cc == 0 else (yp, ym)
        to_plus, to_minus = (dxp, dxm) if cc == 0 else (dyp, dym)
        return (
            remote(gchip(cc, v, plus), t2.at[v, 0], t2s.at[v, 0], t2r.at[v, 0], to_plus),
            remote(gchip(cc, v, minus), t2.at[v, 1], t2s.at[v, 1], t2r.at[v, 1], to_minus),
        )

    def add_into(ref, *others):
        total = ref[...].astype(F32)
        for more in others:
            total = total + more[...].astype(F32)
        ref[...] = total.astype(BF16)

    def rs_a(v):
        def body(cc):
            for copy in r1_copies(cc, v):
                copy.start()

        by_core(body)

    def rs_b(v):
        def body(cc):
            plus, minus = (yp, ym) if cc == 0 else (xp, xm)
            arrive, leave = r1_copies(cc, v), r2_copies(cc, v)
            arrive[0].wait_recv()
            add_into(grow(cc, v, plus, 0, 2), r1.at[v, 0])
            leave[0].start()
            arrive[1].wait_recv()
            add_into(grow(cc, v, minus, 2, 2), r1.at[v, 1])
            leave[1].start()

        by_core(body)

    def rs_c(v):
        def body(cc):
            me = y if cc == 0 else x
            arrive, leave = r2_copies(cc, v), t1_copies(cc, v)
            arrive[0].wait_recv()
            arrive[1].wait_recv()
            for i in range(4):
                block = gchip(cc, v, i)
                add_into(block, r2.at[v, 0, i], r2.at[v, 1, i])
            for copy in leave:
                copy.start()

        by_core(body)

    def rs_d(v):
        def body(cc):
            plus, minus = (xp, xm) if cc == 0 else (yp, ym)
            arrive, leave = t1_copies(cc, v), t2_copies(cc, v)
            arrive[0].wait_recv()
            add_into(gchip(cc, v, plus, TOP), t1.at[v, 0])
            leave[0].start()
            arrive[1].wait_recv()
            add_into(gchip(cc, v, minus, BOTTOM), t1.at[v, 1])
            leave[1].start()

        by_core(body)

    def rs_e(v):
        def body(cc):
            for copy in t2_copies(cc, v):
                copy.wait_recv()

        by_core(body)
        return (
            xs[4 * v + y, x].astype(F32) + t2[v, 0].astype(F32) + t2[v, 1].astype(F32)
        )

    v0, v1 = 1 - zl, zl
    weight_term(v0)
    rs_a(v0)
    weight_term(v1)
    rs_a(v1)
    rs_b(v0)
    rs_b(v1)
    rs_c(v0)
    rs_c(v1)
    rs_d(v0)
    rs_d(v1)
    xs[4 * v0 + y, x] = rs_e(v0).astype(BF16)
    pair = device(x, y, 2 * s + 1 - zl, c)
    cross = remote(xs.at[4 * v0 + y, x], z1, zsend, zrecv, pair)
    cross.start()
    sf[...] = rs_e(v1)
    cross.wait_recv()
    sf[...] = sf[...] + z1[...].astype(F32)
    last = remote(sf.at[sib_rows], o1, osend, orecv, sib)
    last.start()
    out_ref[:, mine] = sf[my_rows, :]
    last.wait_recv()
    out_ref[:, other] = o1[...]

    for copy in gives(1 - c, my_rows):
        copy.wait_send()
    for d in range(1, 8):
        raw(d).wait_send()

    @pl.loop(0, UNITS)
    def _(u):
        def body(cc):
            for copy in p_copies(wa, cc, u, u) + q_copies(wa, cc, u, u):
                copy.wait_send()
            for i in range(4):
                d_copy(wa, cc, u, u, i).wait_send()

        by_core(body)

    def own_sent(cc):
        for copy in p_copies(wz, cc, own, UNITS) + q_copies(wz, cc, own, UNITS):
            copy.wait_send()
        for i in range(4):
            d_copy(wz, cc, own, UNITS, i).wait_send()

    by_core(own_sent)
    for i in range(2):
        for r in range(1, 4):
            up(r, i).wait_send()
            down(r, i).wait_send()
        for slot in range(7):
            e_copy(slot, i).wait_send()
    up(4, 0).wait_send()
    down(4, 1).wait_send()
    last.wait_send()
    cross.wait_send()
    give_g.wait_send()
    normed_copy().wait_send()

    @pl.loop(0, 2)
    def _(v):
        def body(cc):
            for copies in (r1_copies, r2_copies, t1_copies, t2_copies):
                for copy in copies(cc, v):
                    copy.wait_send()

        by_core(body)


def local(inputs, weights, cotangents, lengths):
    rows = inputs.shape[0] * inputs.shape[1]
    dma = pltpu.SemaphoreType.DMA
    vmem = pl.BlockSpec(memory_space=pltpu.VMEM)
    out = pl.pallas_call(
        kernel,
        out_shape=jax.ShapeDtypeStruct((32, D), F32),
        in_specs=[
            pl.BlockSpec(memory_space=pl.ANY),
            vmem,
            vmem,
            pl.BlockSpec(memory_space=pltpu.SMEM),
        ],
        out_specs=vmem,
        scratch_shapes=[
            pltpu.VMEM((8, 2, 4, 4, 64, XY), BF16),
            pltpu.VMEM((8, 2, 4, 4, 64, Z), BF16),
            pltpu.VMEM((8, 4, 64, HALF), BF16),
            pltpu.VMEM((4, ROWS, D), F32),
            pltpu.VMEM((4, ROWS, 128), F32),
            pltpu.VMEM((ROWS, D), BF16),
            pltpu.VMEM((2, ROWS, D), BF16),
            pltpu.VMEM((2, ROWS, HALF), BF16),
            pltpu.VMEM((ROWS, D), BF16),
            pltpu.VMEM((ROWS, D), F32),
            pltpu.VMEM((2, 2, 2, 64, HALF), BF16),
            pltpu.VMEM((2, 2, 4, 64, HALF), BF16),
            pltpu.VMEM((2, 2, 32, HALF), BF16),
            pltpu.VMEM((2, 2, 64, HALF), BF16),
            pltpu.VMEM((64, HALF), BF16),
            pltpu.VMEM((64, HALF), F32),
            pltpu.VMEM((32, HALF), F32),
            dma((4,)),
            dma((2,)),
            dma((2,)),
            dma((7,)),
            dma((8,)),
            dma((4, 2)),
            dma((4, 2)),
            dma((4, 2)),
            dma((4, 2)),
            dma((7, 2)),
            dma((7, 2)),
            dma((9, 4)),
            dma((9, 4)),
            dma((9, 6)),
            dma((9, 6)),
            dma((9, 4)),
            dma((9, 4)),
            dma((2,)),
            dma((2,)),
            dma((2, 2)),
            dma((2, 2)),
            dma((2, 2)),
            dma((2, 2)),
            dma((2, 2)),
            dma((2, 2)),
            dma((2, 2)),
            dma((2, 2)),
            dma,
            dma,
            dma,
            dma,
        ],
        compiler_params=pltpu.CompilerParams(
            collective_id=0, has_side_effects=True, vmem_limit_bytes=63 * 2**20
        ),
        cost_estimate=pl.CostEstimate(
            flops=9 * 2 * ROWS * D * D, bytes_accessed=36 * 2**20, transcendentals=4 * ROWS * D
        ),
    )(inputs.reshape(4, rows // 4, D), weights[0], cotangents.reshape(rows, D), lengths)
    return out[None]


def solution(mesh):
    in_specs = (
        P(None, "fsdp", None),
        P("section", "fsdp", None),
        P(None, "fsdp", None),
        P(None, "fsdp"),
    )
    out_specs = P("section", "fsdp", None)
    return jax.shard_map(local, mesh=mesh, in_specs=in_specs, out_specs=out_specs, check_vma=False)
```

```python
import functools

import jax
import jax.numpy as jnp
from jax import lax
from jax.experimental import pallas as pl
from jax.experimental.pallas import tpu as pltpu
from jax.sharding import PartitionSpec as P

MESH = pl.DeviceIdType.MESH
F32 = jnp.float32
BF16 = jnp.bfloat16
EPS = 1e-06
GELU_C = 0.7978845608028654
GELU_A = 0.044715

D = 2048
ROWS = 256
HALF = 1024
XY = 768
Z = HALF - XY
UNITS = 8
READY = ((3, 6, 7, 9), (6, 7, 8, 9), (7, 8, 9, 10), (6, 7, 9, 10))
FIRST, SECOND = pl.ds(0, 2), pl.ds(2, 2)
TOP, BOTTOM = pl.ds(0, 32), pl.ds(32, 32)


def position():
    s, f = lax.axis_index("section"), lax.axis_index("fsdp")
    c = lax.rem(f, 2)
    x = lax.rem(f // 2, 4)
    y = lax.rem(f // 8, 4)
    zl = f // 32
    return s, zl, x, y, c


def device(x, y, z, c):
    return (z // 2, lax.rem(z, 2) * 32 + y * 8 + x * 2 + c)


def remote(src, dst, send, recv, dev):
    return pltpu.make_async_remote_copy(
        src_ref=src, dst_ref=dst, send_sem=send, recv_sem=recv, device_id=dev, device_id_type=MESH
    )


def kernel(
    x_ref, w_ref, cot_ref, len_ref, out_ref,
    wa, wz, xs, gd, iv, gp, nw, gw, gr, gn, r1, r2, t1, t2, z1, sf, o1,
    loc, xsend, xrecv, rsend, rrecv, usend, urecv, lsend, lrecv, esend, erecv, psend, precv, qsend, qrecv, dsend, drecv,
    nsend, nrecv, r1s, r1r, r2s, r2r, t1s, t1r, t2s, t2r, zsend, zrecv, osend, orecv,
):
    s, zl, x, y, c = position()
    z = 2 * s + zl
    sib = device(x, y, z, 1 - c)
    xp, xm = lax.rem(x + 1, 4), lax.rem(x + 3, 4)
    yp, ym = lax.rem(y + 1, 4), lax.rem(y + 3, 4)
    x2, y2 = lax.rem(x + 2, 4), lax.rem(y + 2, 4)
    dxp, dxm = device(xp, y, z, c), device(xm, y, z, c)
    dyp, dym = device(x, yp, z, c), device(x, ym, z, c)

    barrier = pltpu.get_barrier_semaphore()
    pair_other = device(x, y, 2 * s + 1 - zl, 1 - c)
    for partner in (dxp, dxm, dyp, dym, sib, pair_other):
        pl.semaphore_signal(barrier, inc=1, device_id=partner, device_id_type=MESH)
    for d in range(1, 8):
        pl.semaphore_signal(
            barrier, inc=1, device_id=device(x, y, lax.rem(z + d, 8), c), device_id_type=MESH
        )

    def part(core, first, width):
        return pl.ds(pl.multiple_of(core * HALF + first, 256), width)

    in_x = [
        pltpu.make_async_copy(x_ref.at[:, :, h * HALF : (h + 1) * HALF], xs.at[h], loc.at[3 * h])
        for h in range(2)
    ]
    for copy in in_x:
        copy.start()
    mine = pl.ds(pl.multiple_of(c * HALF, HALF), HALF)
    other = pl.ds(pl.multiple_of((1 - c) * HALF, HALF), HALF)
    my_rows = pl.ds(pl.multiple_of(c * 32, 32), 32)
    sib_rows = pl.ds(pl.multiple_of((1 - c) * 32, 32), 32)
    in_w = [
        pltpu.make_async_copy(src, dst, loc.at[1 + i])
        for i, (src, dst) in enumerate(
            (
                (w_ref.at[:, part(c, 0, XY)], wa.at[2 * s + c, zl, y, x, my_rows]),
                (w_ref.at[:, part(c, XY, Z)], wz.at[2 * s + c, zl, y, x, my_rows]),
            )
        )
    ]
    for copy in in_w:
        copy.start()
    pl.semaphore_wait(barrier, 13)

    def gives(core, rows):
        kh = 2 * s + core
        return (
            remote(
                w_ref.at[:, part(core, XY, Z)], wz.at[kh, zl, y, x, rows],
                xsend.at[0], xrecv.at[0], sib,
            ),
            remote(
                w_ref.at[:, part(core, 0, XY)], wa.at[kh, zl, y, x, rows],
                xsend.at[1], xrecv.at[1], sib,
            ),
        )

    for copy in gives(1 - c, my_rows):
        copy.start()
    for copy in in_w:
        copy.wait()
    for copy in gives(c, sib_rows):
        copy.wait_recv()

    def raw(d):
        block = wa.at[2 * s + c, zl, y, x]
        dest = device(x, y, lax.rem(z + d, 8), c)
        return remote(block, block, rsend.at[d - 1], rrecv.at[z], dest)

    def row(w, cc, kh, uz, i, part=None):
        if cc == 0:
            return w.at[kh, uz, i] if part is None else w.at[kh, uz, i, part]
        return w.at[kh, uz, :, i] if part is None else w.at[kh, uz, part, i]

    def chip(w, cc, kh, uz, i, part=None):
        at = (kh, uz, y, i) if cc == 0 else (kh, uz, i, x)
        return w.at[at] if part is None else w.at[at + (part,)]

    def p_copies(w, cc, u, b):
        kh, uz = 2 * (u // 2) + cc, lax.rem(u, 2)
        me, plus, minus = (x, xp, xm) if cc == 0 else (y, yp, ym)
        to_plus, to_minus = (dxp, dxm) if cc == 0 else (dyp, dym)
        own = chip(w, cc, kh, uz, me)
        from_minus, from_plus = chip(w, cc, kh, uz, minus, TOP), chip(w, cc, kh, uz, plus, BOTTOM)
        return (
            remote(own, own, psend.at[b, 0], precv.at[b, 0], to_plus),
            remote(own, own, psend.at[b, 1], precv.at[b, 1], to_minus),
            remote(from_minus, from_minus, psend.at[b, 2], precv.at[b, 2], to_plus),
            remote(from_plus, from_plus, psend.at[b, 3], precv.at[b, 3], to_minus),
        )

    def p_landed(w, cc, u, b, i):
        kh, uz = 2 * (u // 2) + cc, lax.rem(u, 2)
        plus, minus, far = (xp, xm, x2) if cc == 0 else (yp, ym, y2)
        land = (
            chip(w, cc, kh, uz, minus),
            chip(w, cc, kh, uz, plus),
            chip(w, cc, kh, uz, far, TOP),
            chip(w, cc, kh, uz, far, BOTTOM),
        )[i]
        remote(land, land, psend.at[b, i], precv.at[b, i], sib).wait_recv()

    def q_copies(w, cc, u, b):
        kh, uz = 2 * (u // 2) + cc, lax.rem(u, 2)
        me, plus, minus = (y, yp, ym) if cc == 0 else (x, xp, xm)
        to_plus, to_minus = (dyp, dym) if cc == 0 else (dxp, dxm)
        first, second = row(w, cc, kh, uz, me, FIRST), row(w, cc, kh, uz, me, SECOND)
        from_minus, from_plus = row(w, cc, kh, uz, minus, FIRST), row(w, cc, kh, uz, plus, SECOND)
        return (
            remote(first, first, qsend.at[b, 0], qrecv.at[b, 0], to_plus),
            remote(second, second, qsend.at[b, 1], qrecv.at[b, 1], to_minus),
            remote(second, second, qsend.at[b, 2], qrecv.at[b, 2], to_plus),
            remote(first, first, qsend.at[b, 3], qrecv.at[b, 3], to_minus),
            remote(from_minus, from_minus, qsend.at[b, 4], qrecv.at[b, 4], to_plus),
            remote(from_plus, from_plus, qsend.at[b, 5], qrecv.at[b, 5], to_minus),
        )

    def q_landed(w, cc, u, b, i):
        kh, uz = 2 * (u // 2) + cc, lax.rem(u, 2)
        plus, minus, far = (yp, ym, y2) if cc == 0 else (xp, xm, x2)
        land = (
            row(w, cc, kh, uz, minus, FIRST),
            row(w, cc, kh, uz, plus, SECOND),
            row(w, cc, kh, uz, minus, SECOND),
            row(w, cc, kh, uz, plus, FIRST),
            row(w, cc, kh, uz, far, FIRST),
            row(w, cc, kh, uz, far, SECOND),
        )[i]
        remote(land, land, qsend.at[b, i], qrecv.at[b, i], sib).wait_recv()

    def d_copy(w, cc, u, b, i):
        kh, uz = 2 * (u // 2) + cc, lax.rem(u, 2)
        at = ((y, ym, yp, y2) if cc == 0 else (x, xm, xp, x2))[i]
        block = row(w, cc, kh, uz, at)
        return remote(block, block, dsend.at[b, i], drecv.at[b, i], sib)

    def by_core(body):
        for cc in (0, 1):
            pl.when(c == cc)(functools.partial(body, cc))

    def unit(t):
        rest = t - 2
        near = jnp.where(rest < 2, rest + 2, jnp.where(rest < 4, rest - 2, rest + 2))
        rest = jnp.where(s == 2, near, jnp.where(rest < 2 * s, rest, rest + 2))
        return jnp.where(t == 0, z, jnp.where(t == 1, 2 * s + 1 - zl, rest))

    def stage_p1(w, u, b):
        def body(cc):
            copies = p_copies(w, cc, u, b)
            copies[0].start()
            copies[1].start()

        by_core(body)

    def raw_landed(u):
        block = wa.at[2 * (u // 2) + c, lax.rem(u, 2), y, x]
        remote(block, block, rsend.at[0], rrecv.at[u], sib).wait_recv()

    def stage_p2(w, u, b):
        def body(cc):
            copies = p_copies(w, cc, u, b)
            p_landed(w, cc, u, b, 0)
            copies[2].start()
            p_landed(w, cc, u, b, 1)
            copies[3].start()

        by_core(body)

    def stage_q1(w, u, b):
        def body(cc):
            copies = q_copies(w, cc, u, b)
            p_landed(w, cc, u, b, 2)
            p_landed(w, cc, u, b, 3)
            for copy in copies[:4]:
                copy.start()
            d_copy(w, cc, u, b, 0).start()

        by_core(body)

    def stage_q2(w, u, b):
        def body(cc):
            copies = q_copies(w, cc, u, b)
            q_landed(w, cc, u, b, 0)
            copies[4].start()
            q_landed(w, cc, u, b, 1)
            copies[5].start()

        by_core(body)

    def stage_f(w, u, b):
        def body(cc):
            q_landed(w, cc, u, b, 2)
            d_copy(w, cc, u, b, 1).start()
            q_landed(w, cc, u, b, 3)
            d_copy(w, cc, u, b, 2).start()
            q_landed(w, cc, u, b, 4)
            q_landed(w, cc, u, b, 5)
            d_copy(w, cc, u, b, 3).start()

        by_core(body)

    PARTS = (pl.ds(0, 2), pl.ds(2, 2))
    above, below = device(x, y, lax.rem(z + 1, 8), c), device(x, y, lax.rem(z + 7, 8), c)

    def plane(d, part, core=None):
        v = lax.rem(z + 8 + d, 8)
        core = c if core is None else core
        return wz.at[2 * (v // 2) + core, lax.rem(v, 2), PARTS[part]]

    def up(r, part):
        block = plane(1 - r, part)
        return remote(block, block, usend.at[r - 1, part], urecv.at[r - 1, part], above)

    def down(r, part):
        block = plane(r - 1, part)
        return remote(block, block, lsend.at[r - 1, part], lrecv.at[r - 1, part], below)

    def up_landed(r, part):
        block = plane(-r, part)
        remote(block, block, usend.at[r - 1, part], urecv.at[r - 1, part], above).wait_recv()

    def down_landed(r, part):
        block = plane(r, part)
        remote(block, block, lsend.at[r - 1, part], lrecv.at[r - 1, part], below).wait_recv()

    def e_copy(slot, part):
        d = (-1, -2, -3, 1, 2, 3, 4)[slot]
        block = plane(d, part)
        return remote(block, block, esend.at[slot, part], erecv.at[slot, part], sib)

    def relay(r, part):
        up_landed(r, part)
        if r < 3 or part == 0:
            up(r + 1, part).start()
        down_landed(r, part)
        if r < 3 or part == 1:
            down(r + 1, part).start()
        e_copy(r - 1, part).start()
        e_copy(r + 2, part).start()

    def relay_end():
        up_landed(4, 0)
        e_copy(6, 0).start()
        down_landed(4, 1)
        e_copy(6, 1).start()

    def normed_copy():
        return remote(nw.at[c], nw.at[c], nsend.at[0], nrecv.at[0], sib)

    def section_rows(k, i):
        at = pl.ds(pl.multiple_of(lax.rem(i, 2) * 32, 32), 32)
        halves = [xs[2 * k + h, i // 2, at, :].astype(F32) for h in range(2)]
        return jnp.concatenate(halves, axis=1)

    def forward(k):
        @pl.loop(0, 2)
        def _(uz):
            u = 2 * k + uz

            def body(cc):
                for i in range(4):
                    d_copy(wa, 1 - cc, u, u, i).wait_recv()

                @pl.when(u == z)
                def _():
                    for i in range(4):
                        d_copy(wz, 1 - cc, u, UNITS, i).wait_recv()

            by_core(body)

            @pl.when(u != z)
            def _():
                d = lax.rem(u - z + 8, 8)
                slot = jnp.where(d < 4, 2 + d, jnp.where(d == 4, 6, 7 - d))
                for i in range(2):
                    block = wz.at[2 * k + 1 - c, uz, PARTS[i]]
                    remote(block, block, esend.at[slot, i], erecv.at[slot, i], sib).wait_recv()

        @pl.loop(0, ROWS // 32)
        def _(i):
            rows = pl.ds(pl.multiple_of(i * 32, 32), 32)
            xf = section_rows(k, i)
            inv = lax.rsqrt(jnp.mean(xf * xf, axis=-1, keepdims=True) + EPS)
            iv[k, rows, :] = jnp.broadcast_to(inv, (32, 128))
            gp[rows, :] = (xf * inv).astype(BF16)

        @pl.when(k == s)
        def _():
            nw[c] = gp[...]
            normed_copy().start()

        @pl.loop(0, 2)
        def _(h):
            cols = part(h, 0, HALF)
            w = jnp.concatenate(
                [wa[2 * k + h].reshape(D, XY), wz[2 * k + h].reshape(D, Z)], axis=1
            )
            u = jnp.dot(gp[...], w, preferred_element_type=F32)
            uu = u * u
            t = jnp.tanh((GELU_C * u) * (1.0 + GELU_A * uu))
            cdf = 0.5 * (1.0 + t)
            gd[k, :, cols] = cdf + (0.5 * GELU_C) * u * (1.0 - t * t) * (
                1.0 + (3.0 * GELU_A) * uu
            )

            @pl.when(k < 3)
            def _():
                nxt = jnp.minimum(k + 1, 3)
                before = xs[2 * k + h].reshape(ROWS, HALF)
                after = (before.astype(F32) + u * cdf).astype(BF16)
                xs[2 * nxt + h] = after.reshape(4, 64, HALF)

    own = unit(0)
    stage_p1(wz, own, UNITS)
    stage_p1(wa, own, own)
    for d in (1, 7, 2, 6, 3, 5, 4):
        raw(d).start()
    for m in range(2):
        for q in range(2):
            rows = pl.ds(128 * m + 64 * q, 64)
            live = lax.broadcasted_iota(jnp.int32, (64, D), 0) < len_ref[m, q]
            gr[rows, :] = jnp.where(live, cot_ref[rows, :].astype(F32), 0.0).astype(BF16)
    for copy in in_x:
        copy.wait()
    stage_p2(wz, own, UNITS)
    stage_p2(wa, own, own)
    stage_q1(wz, own, UNITS)
    stage_q1(wa, own, own)
    near = unit(1)
    raw_landed(near)
    stage_p1(wa, near, near)
    stage_q2(wz, own, UNITS)
    stage_p2(wa, near, near)
    stage_q2(wa, own, own)
    stage_f(wz, own, UNITS)
    for i in range(2):
        up(1, i).start()
        down(1, i).start()
    third = unit(2)
    raw_landed(third)
    stage_p1(wa, third, third)

    @pl.loop(1, UNITS + 3)
    def _(i):
        def when_unit(ahead, stage):
            @pl.when((i + ahead >= 0) & (i + ahead < UNITS))
            def _():
                u = unit(i + ahead)
                stage(wa, u, u)

        def first_stage(w, u, b):
            raw_landed(u)
            stage_p1(w, u, b)

        when_unit(0, stage_q1)
        when_unit(2, first_stage)
        when_unit(1, stage_p2)
        k = -1
        for section in range(4):
            for number in range(4):
                k = jnp.where((s == section) & (i == READY[section][number]), number, k)
        pl.when(k >= 0)(lambda: forward(jnp.maximum(k, 0)))
        when_unit(0, stage_q2)
        when_unit(-1, stage_f)
        pl.when(i == 1)(lambda: relay(1, 0))
        pl.when(i == 2)(lambda: relay(1, 1))
        pl.when(i == 3)(lambda: relay(2, 0))
        pl.when(i == 4)(lambda: relay(2, 1))

        @pl.when(i == 5)
        def _():
            relay(3, 0)
            relay(3, 1)

        pl.when(i == 6)(relay_end)

    @pl.loop(0, ROWS // 32)
    def _(i):
        rows = pl.ds(pl.multiple_of(i * 32, 32), 32)
        gp[rows, :] = (gr[rows, :].astype(F32) * gd[3, rows, :]).astype(BF16)

    @pl.loop(0, 3 - s)
    def _(step):
        k = 3 - step

        @pl.loop(0, 2)
        def _(j):
            tile = jnp.concatenate(
                [
                    w[2 * k + h, j].reshape(HALF, width)
                    for h in range(2)
                    for w, width in ((wa, XY), (wz, Z))
                ],
                axis=1,
            )
            gn[:, part(j, 0, HALF)] = lax.dot_general(
                gp[...], tile, (((1,), (1,)), ((), ())), preferred_element_type=F32
            )

        @pl.loop(0, ROWS // 32)
        def _(i):
            rows = pl.ds(pl.multiple_of(i * 32, 32), 32)
            xf = section_rows(k, i)
            g = gn[rows, :]
            inv = iv[k, rows, :][:, :1]
            mean = jnp.mean(g * xf, axis=-1, keepdims=True)
            grad = gr[rows, :].astype(F32) + inv * g - xf * (inv * inv * inv * mean)
            grad = grad.astype(BF16)
            gr[rows, :] = grad
            gp[rows, :] = (grad.astype(F32) * gd[k - 1, rows, :]).astype(BF16)

    gw[c] = gp[:, mine]
    give_g = remote(gp.at[:, other], gw.at[c], nsend.at[1], nrecv.at[1], sib)
    give_g.start()

    remote(nw.at[1 - c], nw.at[1 - c], nsend.at[0], nrecv.at[0], sib).wait_recv()
    remote(gw.at[1 - c], gw.at[1 - c], nsend.at[1], nrecv.at[1], sib).wait_recv()

    def weight_term(v):
        @pl.loop(0, 4)
        def _(j):
            cols = pl.ds(pl.multiple_of(v * HALF + j * 256, 256), 256)
            total = None
            for half in range(2):
                part = lax.dot_general(
                    nw[half, :, cols], gw[half], (((0,), (0,)), ((), ())),
                    preferred_element_type=F32,
                )
                total = part if total is None else total + part
            xs[4 * v + j] = total.astype(BF16).reshape(4, 64, HALF)

    def grow(cc, v, i, first=0, count=4):
        if cc == 0:
            return xs.at[4 * v + i, pl.ds(first, count)]
        return xs.at[pl.ds(4 * v + first, count), i]

    def gchip(cc, v, i, part=None):
        at = (4 * v + y, i) if cc == 0 else (4 * v + i, x)
        return xs.at[at] if part is None else xs.at[at + (part,)]

    def r1_copies(cc, v):
        far = y2 if cc == 0 else x2
        to_plus, to_minus = (dyp, dym) if cc == 0 else (dxp, dxm)
        return (
            remote(grow(cc, v, far, 0, 2), r1.at[v, 0], r1s.at[v, 0], r1r.at[v, 0], to_plus),
            remote(grow(cc, v, far, 2, 2), r1.at[v, 1], r1s.at[v, 1], r1r.at[v, 1], to_minus),
        )

    def r2_copies(cc, v):
        plus, minus = (yp, ym) if cc == 0 else (xp, xm)
        to_plus, to_minus = (dyp, dym) if cc == 0 else (dxp, dxm)
        return (
            remote(grow(cc, v, plus), r2.at[v, 0], r2s.at[v, 0], r2r.at[v, 0], to_plus),
            remote(grow(cc, v, minus), r2.at[v, 1], r2s.at[v, 1], r2r.at[v, 1], to_minus),
        )

    def t1_copies(cc, v):
        far = x2 if cc == 0 else y2
        to_plus, to_minus = (dxp, dxm) if cc == 0 else (dyp, dym)
        return (
            remote(gchip(cc, v, far, TOP), t1.at[v, 0], t1s.at[v, 0], t1r.at[v, 0], to_plus),
            remote(gchip(cc, v, far, BOTTOM), t1.at[v, 1], t1s.at[v, 1], t1r.at[v, 1], to_minus),
        )

    def t2_copies(cc, v):
        plus, minus = (xp, xm) if cc == 0 else (yp, ym)
        to_plus, to_minus = (dxp, dxm) if cc == 0 else (dyp, dym)
        return (
            remote(gchip(cc, v, plus), t2.at[v, 0], t2s.at[v, 0], t2r.at[v, 0], to_plus),
            remote(gchip(cc, v, minus), t2.at[v, 1], t2s.at[v, 1], t2r.at[v, 1], to_minus),
        )

    def add_into(ref, *others):
        total = ref[...].astype(F32)
        for more in others:
            total = total + more[...].astype(F32)
        ref[...] = total.astype(BF16)

    def rs_a(v):
        def body(cc):
            for copy in r1_copies(cc, v):
                copy.start()

        by_core(body)

    def rs_b(v):
        def body(cc):
            plus, minus = (yp, ym) if cc == 0 else (xp, xm)
            arrive, leave = r1_copies(cc, v), r2_copies(cc, v)
            arrive[0].wait_recv()
            add_into(grow(cc, v, plus, 0, 2), r1.at[v, 0])
            leave[0].start()
            arrive[1].wait_recv()
            add_into(grow(cc, v, minus, 2, 2), r1.at[v, 1])
            leave[1].start()

        by_core(body)

    def rs_c(v):
        def body(cc):
            me = y if cc == 0 else x
            arrive, leave = r2_copies(cc, v), t1_copies(cc, v)
            arrive[0].wait_recv()
            arrive[1].wait_recv()
            for i in range(4):
                block = gchip(cc, v, i)
                add_into(block, r2.at[v, 0, i], r2.at[v, 1, i])
            for copy in leave:
                copy.start()

        by_core(body)

    def rs_d(v):
        def body(cc):
            plus, minus = (xp, xm) if cc == 0 else (yp, ym)
            arrive, leave = t1_copies(cc, v), t2_copies(cc, v)
            arrive[0].wait_recv()
            add_into(gchip(cc, v, plus, TOP), t1.at[v, 0])
            leave[0].start()
            arrive[1].wait_recv()
            add_into(gchip(cc, v, minus, BOTTOM), t1.at[v, 1])
            leave[1].start()

        by_core(body)

    def rs_e(v):
        def body(cc):
            for copy in t2_copies(cc, v):
                copy.wait_recv()

        by_core(body)
        return (
            xs[4 * v + y, x].astype(F32) + t2[v, 0].astype(F32) + t2[v, 1].astype(F32)
        )

    v0, v1 = 1 - zl, zl
    weight_term(v0)
    rs_a(v0)
    weight_term(v1)
    rs_a(v1)
    rs_b(v0)
    rs_b(v1)
    rs_c(v0)
    rs_c(v1)
    rs_d(v0)
    rs_d(v1)
    xs[4 * v0 + y, x] = rs_e(v0).astype(BF16)
    def cross(core):
        rows = pl.ds(pl.multiple_of(core * 32, 32), 32)
        dest = device(x, y, 2 * s + 1 - zl, core)
        return remote(xs.at[4 * v0 + y, x, rows], z1.at[c], zsend.at[core], zrecv.at[c], dest)

    cross(0).start()
    cross(1).start()
    sf[...] = rs_e(v1)
    last = remote(sf.at[sib_rows], o1, osend, orecv, sib)
    last.start()
    for core in range(2):
        remote(z1.at[core], z1.at[core], zsend.at[core], zrecv.at[core], sib).wait_recv()
    out_ref[:, mine] = sf[my_rows, :] + z1[c].astype(F32)
    last.wait_recv()
    out_ref[:, other] = o1[...] + z1[1 - c].astype(F32)

    for copy in gives(1 - c, my_rows):
        copy.wait_send()
    for d in range(1, 8):
        raw(d).wait_send()

    @pl.loop(0, UNITS)
    def _(u):
        def body(cc):
            for copy in p_copies(wa, cc, u, u) + q_copies(wa, cc, u, u):
                copy.wait_send()
            for i in range(4):
                d_copy(wa, cc, u, u, i).wait_send()

        by_core(body)

    def own_sent(cc):
        for copy in p_copies(wz, cc, own, UNITS) + q_copies(wz, cc, own, UNITS):
            copy.wait_send()
        for i in range(4):
            d_copy(wz, cc, own, UNITS, i).wait_send()

    by_core(own_sent)
    for i in range(2):
        for r in range(1, 4):
            up(r, i).wait_send()
            down(r, i).wait_send()
        for slot in range(7):
            e_copy(slot, i).wait_send()
    up(4, 0).wait_send()
    down(4, 1).wait_send()
    last.wait_send()
    cross(0).wait_send()
    cross(1).wait_send()
    give_g.wait_send()
    normed_copy().wait_send()

    @pl.loop(0, 2)
    def _(v):
        def body(cc):
            for copies in (r1_copies, r2_copies, t1_copies, t2_copies):
                for copy in copies(cc, v):
                    copy.wait_send()

        by_core(body)


def local(inputs, weights, cotangents, lengths):
    rows = inputs.shape[0] * inputs.shape[1]
    dma = pltpu.SemaphoreType.DMA
    vmem = pl.BlockSpec(memory_space=pltpu.VMEM)
    out = pl.pallas_call(
        kernel,
        out_shape=jax.ShapeDtypeStruct((32, D), F32),
        in_specs=[
            pl.BlockSpec(memory_space=pl.ANY),
            vmem,
            vmem,
            pl.BlockSpec(memory_space=pltpu.SMEM),
        ],
        out_specs=vmem,
        scratch_shapes=[
            pltpu.VMEM((8, 2, 4, 4, 64, XY), BF16),
            pltpu.VMEM((8, 2, 4, 4, 64, Z), BF16),
            pltpu.VMEM((8, 4, 64, HALF), BF16),
            pltpu.VMEM((4, ROWS, D), F32),
            pltpu.VMEM((4, ROWS, 128), F32),
            pltpu.VMEM((ROWS, D), BF16),
            pltpu.VMEM((2, ROWS, D), BF16),
            pltpu.VMEM((2, ROWS, HALF), BF16),
            pltpu.VMEM((ROWS, D), BF16),
            pltpu.VMEM((ROWS, D), F32),
            pltpu.VMEM((2, 2, 2, 64, HALF), BF16),
            pltpu.VMEM((2, 2, 4, 64, HALF), BF16),
            pltpu.VMEM((2, 2, 32, HALF), BF16),
            pltpu.VMEM((2, 2, 64, HALF), BF16),
            pltpu.VMEM((2, 32, HALF), BF16),
            pltpu.VMEM((64, HALF), F32),
            pltpu.VMEM((32, HALF), F32),
            dma((4,)),
            dma((2,)),
            dma((2,)),
            dma((7,)),
            dma((8,)),
            dma((4, 2)),
            dma((4, 2)),
            dma((4, 2)),
            dma((4, 2)),
            dma((7, 2)),
            dma((7, 2)),
            dma((9, 4)),
            dma((9, 4)),
            dma((9, 6)),
            dma((9, 6)),
            dma((9, 4)),
            dma((9, 4)),
            dma((2,)),
            dma((2,)),
            dma((2, 2)),
            dma((2, 2)),
            dma((2, 2)),
            dma((2, 2)),
            dma((2, 2)),
            dma((2, 2)),
            dma((2, 2)),
            dma((2, 2)),
            dma((2,)),
            dma((2,)),
            dma,
            dma,
        ],
        compiler_params=pltpu.CompilerParams(
            collective_id=0, has_side_effects=True, vmem_limit_bytes=63 * 2**20
        ),
        cost_estimate=pl.CostEstimate(
            flops=9 * 2 * ROWS * D * D, bytes_accessed=36 * 2**20, transcendentals=4 * ROWS * D
        ),
    )(inputs.reshape(4, rows // 4, D), weights[0], cotangents.reshape(rows, D), lengths)
    return out[None]


def solution(mesh):
    in_specs = (
        P(None, "fsdp", None),
        P("section", "fsdp", None),
        P(None, "fsdp", None),
        P(None, "fsdp"),
    )
    out_specs = P("section", "fsdp", None)
    return jax.shard_map(local, mesh=mesh, in_specs=in_specs, out_specs=out_specs, check_vma=False)
```

```python
import functools

import jax
import jax.numpy as jnp
from jax import lax
from jax.experimental import pallas as pl
from jax.experimental.pallas import tpu as pltpu
from jax.sharding import PartitionSpec as P

MESH = pl.DeviceIdType.MESH
F32 = jnp.float32
BF16 = jnp.bfloat16
EPS = 1e-06
GELU_C = 0.7978845608028654
GELU_A = 0.044715

D = 2048
ROWS = 256
HALF = 1024
XY = 768
Z = HALF - XY
UNITS = 8
READY = ((4, 6, 8, 10), (6, 7, 8, 10), (8, 9, 10, 11), (6, 8, 10, 11))
FIRST, SECOND = pl.ds(0, 2), pl.ds(2, 2)
TOP, BOTTOM = pl.ds(0, 32), pl.ds(32, 32)


def position():
    s, f = lax.axis_index("section"), lax.axis_index("fsdp")
    c = lax.rem(f, 2)
    x = lax.rem(f // 2, 4)
    y = lax.rem(f // 8, 4)
    zl = f // 32
    return s, zl, x, y, c


def device(x, y, z, c):
    return (z // 2, lax.rem(z, 2) * 32 + y * 8 + x * 2 + c)


def remote(src, dst, send, recv, dev):
    return pltpu.make_async_remote_copy(
        src_ref=src, dst_ref=dst, send_sem=send, recv_sem=recv, device_id=dev, device_id_type=MESH
    )


def kernel(
    x_ref, w_ref, cot_ref, len_ref, out_ref,
    wa, wz, xs, gd, iv, gp, nw, gw, gr, gn, r1, r2, t1, t2, z1, sf, o1,
    loc, xsend, xrecv, rsend, rrecv, usend, urecv, lsend, lrecv, esend, erecv, psend, precv, qsend, qrecv, dsend, drecv,
    nsend, nrecv, r1s, r1r, r2s, r2r, t1s, t1r, t2s, t2r, zsend, zrecv, osend, orecv,
):
    s, zl, x, y, c = position()
    z = 2 * s + zl
    sib = device(x, y, z, 1 - c)
    xp, xm = lax.rem(x + 1, 4), lax.rem(x + 3, 4)
    yp, ym = lax.rem(y + 1, 4), lax.rem(y + 3, 4)
    x2, y2 = lax.rem(x + 2, 4), lax.rem(y + 2, 4)
    dxp, dxm = device(xp, y, z, c), device(xm, y, z, c)
    dyp, dym = device(x, yp, z, c), device(x, ym, z, c)

    barrier = pltpu.get_barrier_semaphore()
    pair_other = device(x, y, 2 * s + 1 - zl, 1 - c)
    for partner in (dxp, dxm, dyp, dym, sib, pair_other):
        pl.semaphore_signal(barrier, inc=1, device_id=partner, device_id_type=MESH)
    for d in range(1, 8):
        pl.semaphore_signal(
            barrier, inc=1, device_id=device(x, y, lax.rem(z + d, 8), c), device_id_type=MESH
        )

    def part(core, first, width):
        return pl.ds(pl.multiple_of(core * HALF + first, 256), width)

    in_x = [
        pltpu.make_async_copy(x_ref.at[:, :, h * HALF : (h + 1) * HALF], xs.at[h], loc.at[3 * h])
        for h in range(2)
    ]
    for copy in in_x:
        copy.start()
    mine = pl.ds(pl.multiple_of(c * HALF, HALF), HALF)
    other = pl.ds(pl.multiple_of((1 - c) * HALF, HALF), HALF)
    my_rows = pl.ds(pl.multiple_of(c * 32, 32), 32)
    sib_rows = pl.ds(pl.multiple_of((1 - c) * 32, 32), 32)
    in_w = [
        pltpu.make_async_copy(src, dst, loc.at[1 + i])
        for i, (src, dst) in enumerate(
            (
                (w_ref.at[:, part(c, 0, XY)], wa.at[2 * s + c, zl, y, x, my_rows]),
                (w_ref.at[:, part(c, XY, Z)], wz.at[2 * s + c, zl, y, x, my_rows]),
            )
        )
    ]
    for copy in in_w:
        copy.start()
    pl.semaphore_wait(barrier, 13)

    def gives(core, rows):
        kh = 2 * s + core
        return (
            remote(
                w_ref.at[:, part(core, XY, Z)], wz.at[kh, zl, y, x, rows],
                xsend.at[0], xrecv.at[0], sib,
            ),
            remote(
                w_ref.at[:, part(core, 0, XY)], wa.at[kh, zl, y, x, rows],
                xsend.at[1], xrecv.at[1], sib,
            ),
        )

    for copy in gives(1 - c, my_rows):
        copy.start()
    for copy in in_w:
        copy.wait()
    for copy in gives(c, sib_rows):
        copy.wait_recv()

    def raw(d):
        block = wa.at[2 * s + c, zl, y, x]
        dest = device(x, y, lax.rem(z + d, 8), c)
        return remote(block, block, rsend.at[d - 1], rrecv.at[z], dest)

    def row(w, cc, kh, uz, i, part=None):
        if cc == 0:
            return w.at[kh, uz, i] if part is None else w.at[kh, uz, i, part]
        return w.at[kh, uz, :, i] if part is None else w.at[kh, uz, part, i]

    def chip(w, cc, kh, uz, i, part=None):
        at = (kh, uz, y, i) if cc == 0 else (kh, uz, i, x)
        return w.at[at] if part is None else w.at[at + (part,)]

    def p_copies(w, cc, u, b):
        kh, uz = 2 * (u // 2) + cc, lax.rem(u, 2)
        me, plus, minus = (x, xp, xm) if cc == 0 else (y, yp, ym)
        to_plus, to_minus = (dxp, dxm) if cc == 0 else (dyp, dym)
        own = chip(w, cc, kh, uz, me)
        from_minus, from_plus = chip(w, cc, kh, uz, minus, TOP), chip(w, cc, kh, uz, plus, BOTTOM)
        return (
            remote(own, own, psend.at[b, 0], precv.at[b, 0], to_plus),
            remote(own, own, psend.at[b, 1], precv.at[b, 1], to_minus),
            remote(from_minus, from_minus, psend.at[b, 2], precv.at[b, 2], to_plus),
            remote(from_plus, from_plus, psend.at[b, 3], precv.at[b, 3], to_minus),
        )

    def p_landed(w, cc, u, b, i):
        kh, uz = 2 * (u // 2) + cc, lax.rem(u, 2)
        plus, minus, far = (xp, xm, x2) if cc == 0 else (yp, ym, y2)
        land = (
            chip(w, cc, kh, uz, minus),
            chip(w, cc, kh, uz, plus),
            chip(w, cc, kh, uz, far, TOP),
            chip(w, cc, kh, uz, far, BOTTOM),
        )[i]
        remote(land, land, psend.at[b, i], precv.at[b, i], sib).wait_recv()

    def q_copies(w, cc, u, b):
        kh, uz = 2 * (u // 2) + cc, lax.rem(u, 2)
        me, plus, minus = (y, yp, ym) if cc == 0 else (x, xp, xm)
        to_plus, to_minus = (dyp, dym) if cc == 0 else (dxp, dxm)
        first, second = row(w, cc, kh, uz, me, FIRST), row(w, cc, kh, uz, me, SECOND)
        from_minus, from_plus = row(w, cc, kh, uz, minus, FIRST), row(w, cc, kh, uz, plus, SECOND)
        return (
            remote(first, first, qsend.at[b, 0], qrecv.at[b, 0], to_plus),
            remote(second, second, qsend.at[b, 1], qrecv.at[b, 1], to_minus),
            remote(second, second, qsend.at[b, 2], qrecv.at[b, 2], to_plus),
            remote(first, first, qsend.at[b, 3], qrecv.at[b, 3], to_minus),
            remote(from_minus, from_minus, qsend.at[b, 4], qrecv.at[b, 4], to_plus),
            remote(from_plus, from_plus, qsend.at[b, 5], qrecv.at[b, 5], to_minus),
        )

    def q_landed(w, cc, u, b, i):
        kh, uz = 2 * (u // 2) + cc, lax.rem(u, 2)
        plus, minus, far = (yp, ym, y2) if cc == 0 else (xp, xm, x2)
        land = (
            row(w, cc, kh, uz, minus, FIRST),
            row(w, cc, kh, uz, plus, SECOND),
            row(w, cc, kh, uz, minus, SECOND),
            row(w, cc, kh, uz, plus, FIRST),
            row(w, cc, kh, uz, far, FIRST),
            row(w, cc, kh, uz, far, SECOND),
        )[i]
        remote(land, land, qsend.at[b, i], qrecv.at[b, i], sib).wait_recv()

    def o_block(w, cc, ahead, off):
        qs = ((y, yp, y2, ym) if cc == 0 else (x, xp, x2, xm))[ahead]
        ps = ((x, xp, x2, xm) if cc == 0 else (y, yp, y2, ym))[off]
        at = (qs, ps) if cc == 0 else (ps, qs)
        return w.at[(2 * s + cc, zl) + at]

    def o_copies(w, cc, b):
        plus, minus = (dyp, dym) if cc == 0 else (dxp, dxm)
        moves = [(0, off, way) for off in (0, -1, 1, 2) for way in (True, False)]
        moves += [(-1, 0, True), (1, -1, False), (1, 1, False), (-1, 2, True)]
        copies = []
        for i, (ahead, off, way) in enumerate(moves):
            block = o_block(w, cc, ahead, off)
            copies.append(
                remote(block, block, qsend.at[b, i], qrecv.at[b, i], plus if way else minus)
            )
        return copies

    def o_landed(w, cc, b, *which):
        lands = [(-1 if way else 1, off) for off in (0, -1, 1, 2) for way in (True, False)]
        lands += [(2, 0), (2, -1), (2, 1), (2, 2)]
        for i in which:
            block = o_block(w, cc, *lands[i])
            remote(block, block, qsend.at[b, i], qrecv.at[b, i], sib).wait_recv()

    def d_copy(w, cc, u, b, i):
        kh, uz = 2 * (u // 2) + cc, lax.rem(u, 2)
        at = ((y, ym, yp, y2) if cc == 0 else (x, xm, xp, x2))[i]
        block = row(w, cc, kh, uz, at)
        return remote(block, block, dsend.at[b, i], drecv.at[b, i], sib)

    def by_core(body):
        for cc in (0, 1):
            pl.when(c == cc)(functools.partial(body, cc))

    def unit(t):
        rest = t - 2
        near = jnp.where(rest < 2, rest + 2, jnp.where(rest < 4, rest - 2, rest + 2))
        rest = jnp.where(s == 2, near, jnp.where(rest < 2 * s, rest, rest + 2))
        return jnp.where(t == 0, z, jnp.where(t == 1, 2 * s + 1 - zl, rest))

    def stage_p1(w, u, b):
        def body(cc):
            copies = p_copies(w, cc, u, b)
            copies[0].start()
            copies[1].start()

        by_core(body)

    def raw_landed(u):
        block = wa.at[2 * (u // 2) + c, lax.rem(u, 2), y, x]
        remote(block, block, rsend.at[0], rrecv.at[u], sib).wait_recv()

    def stage_p2(w, u, b):
        def body(cc):
            copies = p_copies(w, cc, u, b)
            p_landed(w, cc, u, b, 0)
            copies[2].start()
            p_landed(w, cc, u, b, 1)
            copies[3].start()

        by_core(body)

    def stage_q1(w, u, b):
        def body(cc):
            copies = q_copies(w, cc, u, b)
            p_landed(w, cc, u, b, 2)
            p_landed(w, cc, u, b, 3)
            for copy in copies[:4]:
                copy.start()
            d_copy(w, cc, u, b, 0).start()

        by_core(body)

    def stage_q2(w, u, b):
        def body(cc):
            copies = q_copies(w, cc, u, b)
            q_landed(w, cc, u, b, 0)
            copies[4].start()
            q_landed(w, cc, u, b, 1)
            copies[5].start()

        by_core(body)

    def stage_f(w, u, b):
        def body(cc):
            q_landed(w, cc, u, b, 2)
            d_copy(w, cc, u, b, 1).start()
            q_landed(w, cc, u, b, 3)
            d_copy(w, cc, u, b, 2).start()
            q_landed(w, cc, u, b, 4)
            q_landed(w, cc, u, b, 5)
            d_copy(w, cc, u, b, 3).start()

        by_core(body)

    def own_0(w, b):
        def body(cc):
            for copy in p_copies(w, cc, z, b)[:2] + tuple(o_copies(w, cc, b)[:2]):
                copy.start()

        by_core(body)

    def own_1(w, b):
        def body(cc):
            first, row_ = p_copies(w, cc, z, b), o_copies(w, cc, b)
            p_landed(w, cc, z, b, 0)
            first[2].start()
            row_[2].start()
            row_[3].start()
            p_landed(w, cc, z, b, 1)
            first[3].start()
            row_[4].start()
            row_[5].start()

        by_core(body)

    def own_2(w, b):
        def body(cc):
            row_ = o_copies(w, cc, b)
            p_landed(w, cc, z, b, 2)
            p_landed(w, cc, z, b, 3)
            row_[6].start()
            row_[7].start()
            d_copy(w, cc, z, b, 0).start()

        by_core(body)

    def own_3(w, b):
        def body(cc):
            row_ = o_copies(w, cc, b)
            o_landed(w, cc, b, 0)
            row_[8].start()
            o_landed(w, cc, b, 3)
            row_[9].start()
            o_landed(w, cc, b, 5)
            row_[10].start()

        by_core(body)

    def own_4(w, b):
        def body(cc):
            o_landed(w, cc, b, 6)
            o_copies(w, cc, b)[11].start()
            o_landed(w, cc, b, 2, 4)
            d_copy(w, cc, z, b, 1).start()
            o_landed(w, cc, b, 1, 7)
            d_copy(w, cc, z, b, 2).start()

        by_core(body)

    def own_5(w, b):
        def body(cc):
            o_landed(w, cc, b, 8, 9, 10, 11)
            d_copy(w, cc, z, b, 3).start()

        by_core(body)

    PARTS = (pl.ds(0, 2), pl.ds(2, 2))
    above, below = device(x, y, lax.rem(z + 1, 8), c), device(x, y, lax.rem(z + 7, 8), c)

    def plane(d, part, core=None):
        v = lax.rem(z + 8 + d, 8)
        core = c if core is None else core
        return wz.at[2 * (v // 2) + core, lax.rem(v, 2), PARTS[part]]

    def up(r, part):
        block = plane(1 - r, part)
        return remote(block, block, usend.at[r - 1, part], urecv.at[r - 1, part], above)

    def down(r, part):
        block = plane(r - 1, part)
        return remote(block, block, lsend.at[r - 1, part], lrecv.at[r - 1, part], below)

    def up_landed(r, part):
        block = plane(-r, part)
        remote(block, block, usend.at[r - 1, part], urecv.at[r - 1, part], above).wait_recv()

    def down_landed(r, part):
        block = plane(r, part)
        remote(block, block, lsend.at[r - 1, part], lrecv.at[r - 1, part], below).wait_recv()

    def e_copy(slot, part):
        d = (-1, -2, -3, 1, 2, 3, 4)[slot]
        block = plane(d, part)
        return remote(block, block, esend.at[slot, part], erecv.at[slot, part], sib)

    def relay(r, part):
        up_landed(r, part)
        if r < 3 or part == 0:
            up(r + 1, part).start()
        down_landed(r, part)
        if r < 3 or part == 1:
            down(r + 1, part).start()
        e_copy(r - 1, part).start()
        e_copy(r + 2, part).start()

    def relay_end():
        up_landed(4, 0)
        e_copy(6, 0).start()
        down_landed(4, 1)
        e_copy(6, 1).start()

    def normed_copy():
        return remote(nw.at[c], nw.at[c], nsend.at[0], nrecv.at[0], sib)

    def section_rows(k, i):
        at = pl.ds(pl.multiple_of(lax.rem(i, 2) * 32, 32), 32)
        halves = [xs[2 * k + h, i // 2, at, :].astype(F32) for h in range(2)]
        return jnp.concatenate(halves, axis=1)

    def forward(k):
        @pl.loop(0, 2)
        def _(uz):
            u = 2 * k + uz

            def body(cc):
                for i in range(4):
                    d_copy(wa, 1 - cc, u, u, i).wait_recv()

                @pl.when(u == z)
                def _():
                    for i in range(4):
                        d_copy(wz, 1 - cc, u, UNITS, i).wait_recv()

            by_core(body)

            @pl.when(u != z)
            def _():
                d = lax.rem(u - z + 8, 8)
                slot = jnp.where(d < 4, 2 + d, jnp.where(d == 4, 6, 7 - d))
                for i in range(2):
                    block = wz.at[2 * k + 1 - c, uz, PARTS[i]]
                    remote(block, block, esend.at[slot, i], erecv.at[slot, i], sib).wait_recv()

        @pl.loop(0, ROWS // 32)
        def _(i):
            rows = pl.ds(pl.multiple_of(i * 32, 32), 32)
            xf = section_rows(k, i)
            inv = lax.rsqrt(jnp.mean(xf * xf, axis=-1, keepdims=True) + EPS)
            iv[k, rows, :] = jnp.broadcast_to(inv, (32, 128))
            gp[rows, :] = (xf * inv).astype(BF16)

        @pl.when(k == s)
        def _():
            nw[c] = gp[...]
            normed_copy().start()

        @pl.loop(0, 2)
        def _(h):
            cols = part(h, 0, HALF)
            w = jnp.concatenate(
                [wa[2 * k + h].reshape(D, XY), wz[2 * k + h].reshape(D, Z)], axis=1
            )
            u = jnp.dot(gp[...], w, preferred_element_type=F32)
            uu = u * u
            t = jnp.tanh((GELU_C * u) * (1.0 + GELU_A * uu))
            cdf = 0.5 * (1.0 + t)
            gd[k, :, cols] = cdf + (0.5 * GELU_C) * u * (1.0 - t * t) * (
                1.0 + (3.0 * GELU_A) * uu
            )

            @pl.when(k < 3)
            def _():
                nxt = jnp.minimum(k + 1, 3)
                before = xs[2 * k + h].reshape(ROWS, HALF)
                after = (before.astype(F32) + u * cdf).astype(BF16)
                xs[2 * nxt + h] = after.reshape(4, 64, HALF)

    own_0(wz, UNITS)
    own_0(wa, z)
    for d in (1, 7, 2, 6, 3, 5, 4):
        raw(d).start()
    for m in range(2):
        for q in range(2):
            rows = pl.ds(128 * m + 64 * q, 64)
            live = lax.broadcasted_iota(jnp.int32, (64, D), 0) < len_ref[m, q]
            gr[rows, :] = jnp.where(live, cot_ref[rows, :].astype(F32), 0.0).astype(BF16)
    for copy in in_x:
        copy.wait()
    own_1(wz, UNITS)
    own_1(wa, z)
    own_2(wz, UNITS)
    near = unit(1)
    raw_landed(near)
    stage_p1(wa, near, near)
    own_2(wa, z)
    own_3(wz, UNITS)
    stage_p2(wa, near, near)
    own_3(wa, z)
    own_4(wz, UNITS)
    own_5(wz, UNITS)
    for i in range(2):
        up(1, i).start()
        down(1, i).start()
    third = unit(2)
    raw_landed(third)
    stage_p1(wa, third, third)

    @pl.loop(1, UNITS + 4)
    def _(i):
        def when_unit(ahead, stage):
            @pl.when((i + ahead >= 1) & (i + ahead < UNITS))
            def _():
                u = unit(i + ahead)
                stage(wa, u, u)

        def first_stage(w, u, b):
            raw_landed(u)
            stage_p1(w, u, b)

        when_unit(2, first_stage)
        when_unit(1, stage_p2)
        when_unit(0, stage_q1)
        k = -1
        for section in range(4):
            for number in range(4):
                k = jnp.where((s == section) & (i == READY[section][number]), number, k)
        pl.when(k >= 0)(lambda: forward(jnp.maximum(k, 0)))
        when_unit(-1, stage_q2)
        when_unit(-2, stage_f)

        @pl.when(i == 1)
        def _():
            own_4(wa, z)
            own_5(wa, z)

        pl.when(i == 2)(lambda: relay(1, 0))

        @pl.when(i == 3)
        def _():
            relay(1, 1)
            relay(2, 0)

        pl.when(i == 4)(lambda: relay(2, 1))

        @pl.when(i == 5)
        def _():
            relay(3, 0)
            relay(3, 1)

        pl.when(i == 6)(relay_end)

    @pl.loop(0, ROWS // 32)
    def _(i):
        rows = pl.ds(pl.multiple_of(i * 32, 32), 32)
        gp[rows, :] = (gr[rows, :].astype(F32) * gd[3, rows, :]).astype(BF16)

    @pl.loop(0, 3 - s)
    def _(step):
        k = 3 - step

        @pl.loop(0, 2)
        def _(j):
            tile = jnp.concatenate(
                [
                    w[2 * k + h, j].reshape(HALF, width)
                    for h in range(2)
                    for w, width in ((wa, XY), (wz, Z))
                ],
                axis=1,
            )
            gn[:, part(j, 0, HALF)] = lax.dot_general(
                gp[...], tile, (((1,), (1,)), ((), ())), preferred_element_type=F32
            )

        @pl.loop(0, ROWS // 32)
        def _(i):
            rows = pl.ds(pl.multiple_of(i * 32, 32), 32)
            xf = section_rows(k, i)
            g = gn[rows, :]
            inv = iv[k, rows, :][:, :1]
            mean = jnp.mean(g * xf, axis=-1, keepdims=True)
            grad = gr[rows, :].astype(F32) + inv * g - xf * (inv * inv * inv * mean)
            grad = grad.astype(BF16)
            gr[rows, :] = grad
            gp[rows, :] = (grad.astype(F32) * gd[k - 1, rows, :]).astype(BF16)

    gw[c] = gp[:, mine]
    give_g = remote(gp.at[:, other], gw.at[c], nsend.at[1], nrecv.at[1], sib)
    give_g.start()

    remote(nw.at[1 - c], nw.at[1 - c], nsend.at[0], nrecv.at[0], sib).wait_recv()
    remote(gw.at[1 - c], gw.at[1 - c], nsend.at[1], nrecv.at[1], sib).wait_recv()

    def weight_term(v):
        @pl.loop(0, 4)
        def _(j):
            cols = pl.ds(pl.multiple_of(v * HALF + j * 256, 256), 256)
            total = None
            for half in range(2):
                part = lax.dot_general(
                    nw[half, :, cols], gw[half], (((0,), (0,)), ((), ())),
                    preferred_element_type=F32,
                )
                total = part if total is None else total + part
            xs[4 * v + j] = total.astype(BF16).reshape(4, 64, HALF)

    def grow(cc, v, i, first=0, count=4):
        if cc == 0:
            return xs.at[4 * v + i, pl.ds(first, count)]
        return xs.at[pl.ds(4 * v + first, count), i]

    def gchip(cc, v, i, part=None):
        at = (4 * v + y, i) if cc == 0 else (4 * v + i, x)
        return xs.at[at] if part is None else xs.at[at + (part,)]

    def r1_copies(cc, v):
        far = y2 if cc == 0 else x2
        to_plus, to_minus = (dyp, dym) if cc == 0 else (dxp, dxm)
        return (
            remote(grow(cc, v, far, 0, 2), r1.at[v, 0], r1s.at[v, 0], r1r.at[v, 0], to_plus),
            remote(grow(cc, v, far, 2, 2), r1.at[v, 1], r1s.at[v, 1], r1r.at[v, 1], to_minus),
        )

    def r2_copies(cc, v):
        plus, minus = (yp, ym) if cc == 0 else (xp, xm)
        to_plus, to_minus = (dyp, dym) if cc == 0 else (dxp, dxm)
        return (
            remote(grow(cc, v, plus), r2.at[v, 0], r2s.at[v, 0], r2r.at[v, 0], to_plus),
            remote(grow(cc, v, minus), r2.at[v, 1], r2s.at[v, 1], r2r.at[v, 1], to_minus),
        )

    def t1_copies(cc, v):
        far = x2 if cc == 0 else y2
        to_plus, to_minus = (dxp, dxm) if cc == 0 else (dyp, dym)
        return (
            remote(gchip(cc, v, far, TOP), t1.at[v, 0], t1s.at[v, 0], t1r.at[v, 0], to_plus),
            remote(gchip(cc, v, far, BOTTOM), t1.at[v, 1], t1s.at[v, 1], t1r.at[v, 1], to_minus),
        )

    def t2_copies(cc, v):
        plus, minus = (xp, xm) if cc == 0 else (yp, ym)
        to_plus, to_minus = (dxp, dxm) if cc == 0 else (dyp, dym)
        return (
            remote(gchip(cc, v, plus), t2.at[v, 0], t2s.at[v, 0], t2r.at[v, 0], to_plus),
            remote(gchip(cc, v, minus), t2.at[v, 1], t2s.at[v, 1], t2r.at[v, 1], to_minus),
        )

    def add_into(ref, *others):
        total = ref[...].astype(F32)
        for more in others:
            total = total + more[...].astype(F32)
        ref[...] = total.astype(BF16)

    def rs_a(v):
        def body(cc):
            for copy in r1_copies(cc, v):
                copy.start()

        by_core(body)

    def rs_b(v):
        def body(cc):
            plus, minus = (yp, ym) if cc == 0 else (xp, xm)
            arrive, leave = r1_copies(cc, v), r2_copies(cc, v)
            arrive[0].wait_recv()
            add_into(grow(cc, v, plus, 0, 2), r1.at[v, 0])
            leave[0].start()
            arrive[1].wait_recv()
            add_into(grow(cc, v, minus, 2, 2), r1.at[v, 1])
            leave[1].start()

        by_core(body)

    def rs_c(v):
        def body(cc):
            me = y if cc == 0 else x
            arrive, leave = r2_copies(cc, v), t1_copies(cc, v)
            arrive[0].wait_recv()
            arrive[1].wait_recv()
            for i in range(4):
                block = gchip(cc, v, i)
                add_into(block, r2.at[v, 0, i], r2.at[v, 1, i])
            for copy in leave:
                copy.start()

        by_core(body)

    def rs_d(v):
        def body(cc):
            plus, minus = (xp, xm) if cc == 0 else (yp, ym)
            arrive, leave = t1_copies(cc, v), t2_copies(cc, v)
            arrive[0].wait_recv()
            add_into(gchip(cc, v, plus, TOP), t1.at[v, 0])
            leave[0].start()
            arrive[1].wait_recv()
            add_into(gchip(cc, v, minus, BOTTOM), t1.at[v, 1])
            leave[1].start()

        by_core(body)

    def rs_e(v):
        def body(cc):
            for copy in t2_copies(cc, v):
                copy.wait_recv()

        by_core(body)
        return (
            xs[4 * v + y, x].astype(F32) + t2[v, 0].astype(F32) + t2[v, 1].astype(F32)
        )

    v0, v1 = 1 - zl, zl
    weight_term(v0)
    rs_a(v0)
    weight_term(v1)
    rs_a(v1)
    rs_b(v0)
    rs_b(v1)
    rs_c(v0)
    rs_c(v1)
    rs_d(v0)
    rs_d(v1)
    xs[4 * v0 + y, x] = rs_e(v0).astype(BF16)
    def cross(core):
        rows = pl.ds(pl.multiple_of(core * 32, 32), 32)
        dest = device(x, y, 2 * s + 1 - zl, core)
        return remote(xs.at[4 * v0 + y, x, rows], z1.at[c], zsend.at[core], zrecv.at[c], dest)

    cross(0).start()
    cross(1).start()
    sf[...] = rs_e(v1)
    last = remote(sf.at[sib_rows], o1, osend, orecv, sib)
    last.start()
    for core in range(2):
        remote(z1.at[core], z1.at[core], zsend.at[core], zrecv.at[core], sib).wait_recv()
    out_ref[:, mine] = sf[my_rows, :] + z1[c].astype(F32)
    last.wait_recv()
    out_ref[:, other] = o1[...] + z1[1 - c].astype(F32)

    for copy in gives(1 - c, my_rows):
        copy.wait_send()
    for d in range(1, 8):
        raw(d).wait_send()

    @pl.loop(0, UNITS)
    def _(u):
        def body(cc):
            for copy in p_copies(wa, cc, u, u):
                copy.wait_send()
            for i in range(4):
                d_copy(wa, cc, u, u, i).wait_send()

            @pl.when(u != z)
            def _():
                for copy in q_copies(wa, cc, u, u):
                    copy.wait_send()

        by_core(body)

    def own_sent(cc):
        for copy in p_copies(wz, cc, z, UNITS):
            copy.wait_send()
        for copy in o_copies(wz, cc, UNITS) + o_copies(wa, cc, z):
            copy.wait_send()
        for i in range(4):
            d_copy(wz, cc, z, UNITS, i).wait_send()

    by_core(own_sent)
    for i in range(2):
        for r in range(1, 4):
            up(r, i).wait_send()
            down(r, i).wait_send()
        for slot in range(7):
            e_copy(slot, i).wait_send()
    up(4, 0).wait_send()
    down(4, 1).wait_send()
    last.wait_send()
    cross(0).wait_send()
    cross(1).wait_send()
    give_g.wait_send()
    normed_copy().wait_send()

    @pl.loop(0, 2)
    def _(v):
        def body(cc):
            for copies in (r1_copies, r2_copies, t1_copies, t2_copies):
                for copy in copies(cc, v):
                    copy.wait_send()

        by_core(body)


def local(inputs, weights, cotangents, lengths):
    rows = inputs.shape[0] * inputs.shape[1]
    dma = pltpu.SemaphoreType.DMA
    vmem = pl.BlockSpec(memory_space=pltpu.VMEM)
    out = pl.pallas_call(
        kernel,
        out_shape=jax.ShapeDtypeStruct((32, D), F32),
        in_specs=[
            pl.BlockSpec(memory_space=pl.ANY),
            vmem,
            vmem,
            pl.BlockSpec(memory_space=pltpu.SMEM),
        ],
        out_specs=vmem,
        scratch_shapes=[
            pltpu.VMEM((8, 2, 4, 4, 64, XY), BF16),
            pltpu.VMEM((8, 2, 4, 4, 64, Z), BF16),
            pltpu.VMEM((8, 4, 64, HALF), BF16),
            pltpu.VMEM((4, ROWS, D), F32),
            pltpu.VMEM((4, ROWS, 128), F32),
            pltpu.VMEM((ROWS, D), BF16),
            pltpu.VMEM((2, ROWS, D), BF16),
            pltpu.VMEM((2, ROWS, HALF), BF16),
            pltpu.VMEM((ROWS, D), BF16),
            pltpu.VMEM((ROWS, D), F32),
            pltpu.VMEM((2, 2, 2, 64, HALF), BF16),
            pltpu.VMEM((2, 2, 4, 64, HALF), BF16),
            pltpu.VMEM((2, 2, 32, HALF), BF16),
            pltpu.VMEM((2, 2, 64, HALF), BF16),
            pltpu.VMEM((2, 32, HALF), BF16),
            pltpu.VMEM((64, HALF), F32),
            pltpu.VMEM((32, HALF), F32),
            dma((4,)),
            dma((2,)),
            dma((2,)),
            dma((7,)),
            dma((8,)),
            dma((4, 2)),
            dma((4, 2)),
            dma((4, 2)),
            dma((4, 2)),
            dma((7, 2)),
            dma((7, 2)),
            dma((9, 4)),
            dma((9, 4)),
            dma((9, 12)),
            dma((9, 12)),
            dma((9, 4)),
            dma((9, 4)),
            dma((2,)),
            dma((2,)),
            dma((2, 2)),
            dma((2, 2)),
            dma((2, 2)),
            dma((2, 2)),
            dma((2, 2)),
            dma((2, 2)),
            dma((2, 2)),
            dma((2, 2)),
            dma((2,)),
            dma((2,)),
            dma,
            dma,
        ],
        compiler_params=pltpu.CompilerParams(
            collective_id=0, has_side_effects=True, vmem_limit_bytes=63 * 2**20
        ),
        cost_estimate=pl.CostEstimate(
            flops=9 * 2 * ROWS * D * D, bytes_accessed=36 * 2**20, transcendentals=4 * ROWS * D
        ),
    )(inputs.reshape(4, rows // 4, D), weights[0], cotangents.reshape(rows, D), lengths)
    return out[None]


def solution(mesh):
    in_specs = (
        P(None, "fsdp", None),
        P("section", "fsdp", None),
        P(None, "fsdp", None),
        P(None, "fsdp"),
    )
    out_specs = P("section", "fsdp", None)
    return jax.shard_map(local, mesh=mesh, in_specs=in_specs, out_specs=out_specs, check_vma=False)
```

```python
import functools

import jax
import jax.numpy as jnp
from jax import lax
from jax.experimental import pallas as pl
from jax.experimental.pallas import tpu as pltpu
from jax.sharding import PartitionSpec as P

MESH = pl.DeviceIdType.MESH
F32 = jnp.float32
BF16 = jnp.bfloat16
EPS = 1e-06
GELU_C = 0.7978845608028654
GELU_A = 0.044715

D = 2048
ROWS = 256
HALF = 1024
XY = 768
Z = HALF - XY
UNITS = 8
READY = ((4, 6, 7, 9), (6, 7, 8, 9), (7, 8, 9, 10), (6, 7, 9, 10))
FIRST, SECOND = pl.ds(0, 2), pl.ds(2, 2)
TOP, BOTTOM = pl.ds(0, 32), pl.ds(32, 32)


def position():
    s, f = lax.axis_index("section"), lax.axis_index("fsdp")
    c = lax.rem(f, 2)
    x = lax.rem(f // 2, 4)
    y = lax.rem(f // 8, 4)
    zl = f // 32
    return s, zl, x, y, c


def device(x, y, z, c):
    return (z // 2, lax.rem(z, 2) * 32 + y * 8 + x * 2 + c)


def remote(src, dst, send, recv, dev):
    return pltpu.make_async_remote_copy(
        src_ref=src, dst_ref=dst, send_sem=send, recv_sem=recv, device_id=dev, device_id_type=MESH
    )


def kernel(
    x_ref, w_ref, cot_ref, len_ref, out_ref,
    wa, wz, xs, gd, iv, gp, nw, gw, gr, gn, r1, r2, t1, t2, z1, sf, o1,
    loc, xsend, xrecv, rsend, rrecv, usend, urecv, lsend, lrecv, esend, erecv, psend, precv, qsend, qrecv, dsend, drecv,
    nsend, nrecv, r1s, r1r, r2s, r2r, t1s, t1r, t2s, t2r, zsend, zrecv, osend, orecv,
):
    s, zl, x, y, c = position()
    z = 2 * s + zl
    sib = device(x, y, z, 1 - c)
    xp, xm = lax.rem(x + 1, 4), lax.rem(x + 3, 4)
    yp, ym = lax.rem(y + 1, 4), lax.rem(y + 3, 4)
    x2, y2 = lax.rem(x + 2, 4), lax.rem(y + 2, 4)
    dxp, dxm = device(xp, y, z, c), device(xm, y, z, c)
    dyp, dym = device(x, yp, z, c), device(x, ym, z, c)

    barrier = pltpu.get_barrier_semaphore()
    pair_other = device(x, y, 2 * s + 1 - zl, 1 - c)
    for partner in (dxp, dxm, dyp, dym, sib, pair_other):
        pl.semaphore_signal(barrier, inc=1, device_id=partner, device_id_type=MESH)
    for d in range(1, 8):
        pl.semaphore_signal(
            barrier, inc=1, device_id=device(x, y, lax.rem(z + d, 8), c), device_id_type=MESH
        )

    def part(core, first, width):
        return pl.ds(pl.multiple_of(core * HALF + first, 256), width)

    in_x = [
        pltpu.make_async_copy(x_ref.at[:, :, h * HALF : (h + 1) * HALF], xs.at[h], loc.at[3 * h])
        for h in range(2)
    ]
    for copy in in_x:
        copy.start()
    mine = pl.ds(pl.multiple_of(c * HALF, HALF), HALF)
    other = pl.ds(pl.multiple_of((1 - c) * HALF, HALF), HALF)
    my_rows = pl.ds(pl.multiple_of(c * 32, 32), 32)
    sib_rows = pl.ds(pl.multiple_of((1 - c) * 32, 32), 32)
    in_w = [
        pltpu.make_async_copy(src, dst, loc.at[1 + i])
        for i, (src, dst) in enumerate(
            (
                (w_ref.at[:, part(c, 0, XY)], wa.at[2 * s + c, zl, y, x, my_rows]),
                (w_ref.at[:, part(c, XY, Z)], wz.at[2 * s + c, zl, y, x, my_rows]),
            )
        )
    ]
    for copy in in_w:
        copy.start()
    pl.semaphore_wait(barrier, 13)

    def gives(core, rows):
        kh = 2 * s + core
        return (
            remote(
                w_ref.at[:, part(core, XY, Z)], wz.at[kh, zl, y, x, rows],
                xsend.at[0], xrecv.at[0], sib,
            ),
            remote(
                w_ref.at[:, part(core, 0, XY)], wa.at[kh, zl, y, x, rows],
                xsend.at[1], xrecv.at[1], sib,
            ),
        )

    for copy in gives(1 - c, my_rows):
        copy.start()
    for copy in in_w:
        copy.wait()
    for copy in gives(c, sib_rows):
        copy.wait_recv()

    def raw(d):
        block = wa.at[2 * s + c, zl, y, x]
        dest = device(x, y, lax.rem(z + d, 8), c)
        return remote(block, block, rsend.at[d - 1], rrecv.at[z], dest)

    def row(w, cc, kh, uz, i, part=None):
        if cc == 0:
            return w.at[kh, uz, i] if part is None else w.at[kh, uz, i, part]
        return w.at[kh, uz, :, i] if part is None else w.at[kh, uz, part, i]

    def chip(w, cc, kh, uz, i, part=None):
        at = (kh, uz, y, i) if cc == 0 else (kh, uz, i, x)
        return w.at[at] if part is None else w.at[at + (part,)]

    def p_copies(w, cc, u, b):
        kh, uz = 2 * (u // 2) + cc, lax.rem(u, 2)
        me, plus, minus = (x, xp, xm) if cc == 0 else (y, yp, ym)
        to_plus, to_minus = (dxp, dxm) if cc == 0 else (dyp, dym)
        own = chip(w, cc, kh, uz, me)
        from_minus, from_plus = chip(w, cc, kh, uz, minus, TOP), chip(w, cc, kh, uz, plus, BOTTOM)
        return (
            remote(own, own, psend.at[b, 0], precv.at[b, 0], to_plus),
            remote(own, own, psend.at[b, 1], precv.at[b, 1], to_minus),
            remote(from_minus, from_minus, psend.at[b, 2], precv.at[b, 2], to_plus),
            remote(from_plus, from_plus, psend.at[b, 3], precv.at[b, 3], to_minus),
        )

    def p_landed(w, cc, u, b, i):
        kh, uz = 2 * (u // 2) + cc, lax.rem(u, 2)
        plus, minus, far = (xp, xm, x2) if cc == 0 else (yp, ym, y2)
        land = (
            chip(w, cc, kh, uz, minus),
            chip(w, cc, kh, uz, plus),
            chip(w, cc, kh, uz, far, TOP),
            chip(w, cc, kh, uz, far, BOTTOM),
        )[i]
        remote(land, land, psend.at[b, i], precv.at[b, i], sib).wait_recv()

    def q_copies(w, cc, u, b):
        kh, uz = 2 * (u // 2) + cc, lax.rem(u, 2)
        me, plus, minus = (y, yp, ym) if cc == 0 else (x, xp, xm)
        to_plus, to_minus = (dyp, dym) if cc == 0 else (dxp, dxm)
        first, second = row(w, cc, kh, uz, me, FIRST), row(w, cc, kh, uz, me, SECOND)
        from_minus, from_plus = row(w, cc, kh, uz, minus, FIRST), row(w, cc, kh, uz, plus, SECOND)
        return (
            remote(first, first, qsend.at[b, 0], qrecv.at[b, 0], to_plus),
            remote(second, second, qsend.at[b, 1], qrecv.at[b, 1], to_minus),
            remote(second, second, qsend.at[b, 2], qrecv.at[b, 2], to_plus),
            remote(first, first, qsend.at[b, 3], qrecv.at[b, 3], to_minus),
            remote(from_minus, from_minus, qsend.at[b, 4], qrecv.at[b, 4], to_plus),
            remote(from_plus, from_plus, qsend.at[b, 5], qrecv.at[b, 5], to_minus),
        )

    def q_landed(w, cc, u, b, i):
        kh, uz = 2 * (u // 2) + cc, lax.rem(u, 2)
        plus, minus, far = (yp, ym, y2) if cc == 0 else (xp, xm, x2)
        land = (
            row(w, cc, kh, uz, minus, FIRST),
            row(w, cc, kh, uz, plus, SECOND),
            row(w, cc, kh, uz, minus, SECOND),
            row(w, cc, kh, uz, plus, FIRST),
            row(w, cc, kh, uz, far, FIRST),
            row(w, cc, kh, uz, far, SECOND),
        )[i]
        remote(land, land, qsend.at[b, i], qrecv.at[b, i], sib).wait_recv()

    def o_block(w, cc, ahead, off):
        qs = ((y, yp, y2, ym) if cc == 0 else (x, xp, x2, xm))[ahead]
        ps = ((x, xp, x2, xm) if cc == 0 else (y, yp, y2, ym))[off]
        at = (qs, ps) if cc == 0 else (ps, qs)
        return w.at[(2 * s + cc, zl) + at]

    def o_copies(w, cc, b):
        plus, minus = (dyp, dym) if cc == 0 else (dxp, dxm)
        moves = [(0, off, way) for off in (0, -1, 1, 2) for way in (True, False)]
        moves += [(-1, 0, True), (1, -1, False), (1, 1, False), (-1, 2, True)]
        copies = []
        for i, (ahead, off, way) in enumerate(moves):
            block = o_block(w, cc, ahead, off)
            copies.append(
                remote(block, block, qsend.at[b, i], qrecv.at[b, i], plus if way else minus)
            )
        return copies

    def o_landed(w, cc, b, *which):
        lands = [(-1 if way else 1, off) for off in (0, -1, 1, 2) for way in (True, False)]
        lands += [(2, 0), (2, -1), (2, 1), (2, 2)]
        for i in which:
            block = o_block(w, cc, *lands[i])
            remote(block, block, qsend.at[b, i], qrecv.at[b, i], sib).wait_recv()

    def d_copy(w, cc, u, b, i):
        kh, uz = 2 * (u // 2) + cc, lax.rem(u, 2)
        at = ((y, ym, yp, y2) if cc == 0 else (x, xm, xp, x2))[i]
        block = row(w, cc, kh, uz, at)
        return remote(block, block, dsend.at[b, i], drecv.at[b, i], sib)

    def by_core(body):
        for cc in (0, 1):
            pl.when(c == cc)(functools.partial(body, cc))

    def unit(t):
        rest = t - 2
        near = jnp.where(rest < 2, rest + 2, jnp.where(rest < 4, rest - 2, rest + 2))
        rest = jnp.where(s == 2, near, jnp.where(rest < 2 * s, rest, rest + 2))
        return jnp.where(t == 0, z, jnp.where(t == 1, 2 * s + 1 - zl, rest))

    def stage_p1(w, u, b):
        def body(cc):
            copies = p_copies(w, cc, u, b)
            copies[0].start()
            copies[1].start()

        by_core(body)

    def raw_landed(u):
        block = wa.at[2 * (u // 2) + c, lax.rem(u, 2), y, x]
        remote(block, block, rsend.at[0], rrecv.at[u], sib).wait_recv()

    def stage_p2(w, u, b):
        def body(cc):
            copies = p_copies(w, cc, u, b)
            p_landed(w, cc, u, b, 0)
            copies[2].start()
            p_landed(w, cc, u, b, 1)
            copies[3].start()

        by_core(body)

    def stage_q1(w, u, b):
        def body(cc):
            copies = q_copies(w, cc, u, b)
            p_landed(w, cc, u, b, 2)
            p_landed(w, cc, u, b, 3)
            for copy in copies[:4]:
                copy.start()
            d_copy(w, cc, u, b, 0).start()

        by_core(body)

    def stage_q2(w, u, b):
        def body(cc):
            copies = q_copies(w, cc, u, b)
            q_landed(w, cc, u, b, 0)
            copies[4].start()
            q_landed(w, cc, u, b, 1)
            copies[5].start()

        by_core(body)

    def stage_f(w, u, b):
        def body(cc):
            q_landed(w, cc, u, b, 2)
            d_copy(w, cc, u, b, 1).start()
            q_landed(w, cc, u, b, 3)
            d_copy(w, cc, u, b, 2).start()
            q_landed(w, cc, u, b, 4)
            q_landed(w, cc, u, b, 5)
            d_copy(w, cc, u, b, 3).start()

        by_core(body)

    def own_0(w, b):
        def body(cc):
            for copy in p_copies(w, cc, z, b)[:2] + tuple(o_copies(w, cc, b)[:2]):
                copy.start()

        by_core(body)

    def own_1(w, b):
        def body(cc):
            first, row_ = p_copies(w, cc, z, b), o_copies(w, cc, b)
            p_landed(w, cc, z, b, 0)
            first[2].start()
            row_[2].start()
            row_[3].start()
            p_landed(w, cc, z, b, 1)
            first[3].start()
            row_[4].start()
            row_[5].start()

        by_core(body)

    def own_2(w, b):
        def body(cc):
            row_ = o_copies(w, cc, b)
            p_landed(w, cc, z, b, 2)
            p_landed(w, cc, z, b, 3)
            row_[6].start()
            row_[7].start()
            d_copy(w, cc, z, b, 0).start()

        by_core(body)

    def own_3(w, b):
        def body(cc):
            row_ = o_copies(w, cc, b)
            o_landed(w, cc, b, 0)
            row_[8].start()
            o_landed(w, cc, b, 3)
            row_[9].start()
            o_landed(w, cc, b, 5)
            row_[10].start()

        by_core(body)

    def own_4(w, b):
        def body(cc):
            o_landed(w, cc, b, 6)
            o_copies(w, cc, b)[11].start()
            o_landed(w, cc, b, 2, 4)
            d_copy(w, cc, z, b, 1).start()
            o_landed(w, cc, b, 1, 7)
            d_copy(w, cc, z, b, 2).start()

        by_core(body)

    def own_5(w, b):
        def body(cc):
            o_landed(w, cc, b, 8, 9, 10, 11)
            d_copy(w, cc, z, b, 3).start()

        by_core(body)

    PARTS = (pl.ds(0, 2), pl.ds(2, 2))
    above, below = device(x, y, lax.rem(z + 1, 8), c), device(x, y, lax.rem(z + 7, 8), c)

    def plane(d, part, core=None):
        v = lax.rem(z + 8 + d, 8)
        core = c if core is None else core
        return wz.at[2 * (v // 2) + core, lax.rem(v, 2), PARTS[part]]

    def up(r, part):
        block = plane(1 - r, part)
        return remote(block, block, usend.at[r - 1, part], urecv.at[r - 1, part], above)

    def down(r, part):
        block = plane(r - 1, part)
        return remote(block, block, lsend.at[r - 1, part], lrecv.at[r - 1, part], below)

    def up_landed(r, part):
        block = plane(-r, part)
        remote(block, block, usend.at[r - 1, part], urecv.at[r - 1, part], above).wait_recv()

    def down_landed(r, part):
        block = plane(r, part)
        remote(block, block, lsend.at[r - 1, part], lrecv.at[r - 1, part], below).wait_recv()

    def e_copy(slot, part):
        d = (-1, -2, -3, 1, 2, 3, 4)[slot]
        block = plane(d, part)
        return remote(block, block, esend.at[slot, part], erecv.at[slot, part], sib)

    def relay(r, part):
        up_landed(r, part)
        if r < 3 or part == 0:
            up(r + 1, part).start()
        down_landed(r, part)
        if r < 3 or part == 1:
            down(r + 1, part).start()
        e_copy(r - 1, part).start()
        e_copy(r + 2, part).start()

    def relay_end():
        up_landed(4, 0)
        e_copy(6, 0).start()
        down_landed(4, 1)
        e_copy(6, 1).start()

    def normed_copy():
        return remote(nw.at[c], nw.at[c], nsend.at[0], nrecv.at[0], sib)

    def section_rows(k, i):
        at = pl.ds(pl.multiple_of(lax.rem(i, 2) * 32, 32), 32)
        halves = [xs[2 * k + h, i // 2, at, :].astype(F32) for h in range(2)]
        return jnp.concatenate(halves, axis=1)

    def forward(k):
        @pl.loop(0, 2)
        def _(uz):
            u = 2 * k + uz

            def body(cc):
                for i in range(4):
                    d_copy(wa, 1 - cc, u, u, i).wait_recv()

                @pl.when(u == z)
                def _():
                    for i in range(4):
                        d_copy(wz, 1 - cc, u, UNITS, i).wait_recv()

            by_core(body)

            @pl.when(u != z)
            def _():
                d = lax.rem(u - z + 8, 8)
                slot = jnp.where(d < 4, 2 + d, jnp.where(d == 4, 6, 7 - d))
                for i in range(2):
                    block = wz.at[2 * k + 1 - c, uz, PARTS[i]]
                    remote(block, block, esend.at[slot, i], erecv.at[slot, i], sib).wait_recv()

        @pl.loop(0, ROWS // 32)
        def _(i):
            rows = pl.ds(pl.multiple_of(i * 32, 32), 32)
            xf = section_rows(k, i)
            inv = lax.rsqrt(jnp.mean(xf * xf, axis=-1, keepdims=True) + EPS)
            iv[k, rows, :] = jnp.broadcast_to(inv, (32, 128))
            gp[rows, :] = (xf * inv).astype(BF16)

        @pl.when(k == s)
        def _():
            nw[c] = gp[...]
            normed_copy().start()

        @pl.loop(0, 2)
        def _(h):
            cols = part(h, 0, HALF)
            w = jnp.concatenate(
                [wa[2 * k + h].reshape(D, XY), wz[2 * k + h].reshape(D, Z)], axis=1
            )
            u = jnp.dot(gp[...], w, preferred_element_type=F32)
            uu = u * u
            t = jnp.tanh((GELU_C * u) * (1.0 + GELU_A * uu))
            cdf = 0.5 * (1.0 + t)
            gd[k, :, cols] = cdf + (0.5 * GELU_C) * u * (1.0 - t * t) * (
                1.0 + (3.0 * GELU_A) * uu
            )

            @pl.when(k < 3)
            def _():
                nxt = jnp.minimum(k + 1, 3)
                before = xs[2 * k + h].reshape(ROWS, HALF)
                after = (before.astype(F32) + u * cdf).astype(BF16)
                xs[2 * nxt + h] = after.reshape(4, 64, HALF)

    own_0(wz, UNITS)
    own_0(wa, z)
    raw(1).start()
    raw(7).start()
    for m in range(2):
        for q in range(2):
            rows = pl.ds(128 * m + 64 * q, 64)
            live = lax.broadcasted_iota(jnp.int32, (64, D), 0) < len_ref[m, q]
            gr[rows, :] = jnp.where(live, cot_ref[rows, :].astype(F32), 0.0).astype(BF16)
    for copy in in_x:
        copy.wait()
    own_1(wz, UNITS)
    own_1(wa, z)
    raw(2).start()
    raw(6).start()
    own_2(wz, UNITS)
    near = unit(1)
    raw_landed(near)
    stage_p1(wa, near, near)
    own_2(wa, z)
    raw(3).start()
    raw(5).start()
    own_3(wz, UNITS)
    stage_p2(wa, near, near)
    own_3(wa, z)
    own_4(wz, UNITS)
    own_5(wz, UNITS)
    raw(4).start()
    for i in range(2):
        up(1, i).start()
        down(1, i).start()
    third = unit(2)
    raw_landed(third)
    stage_p1(wa, third, third)

    @pl.loop(1, UNITS + 3)
    def _(i):
        def when_unit(ahead, stage):
            @pl.when((i + ahead >= 1) & (i + ahead < UNITS))
            def _():
                u = unit(i + ahead)
                stage(wa, u, u)

        def first_stage(w, u, b):
            raw_landed(u)
            stage_p1(w, u, b)

        when_unit(0, stage_q1)
        when_unit(2, first_stage)
        when_unit(1, stage_p2)
        k = -1
        for section in range(4):
            for number in range(4):
                k = jnp.where((s == section) & (i == READY[section][number]), number, k)
        pl.when(k >= 0)(lambda: forward(jnp.maximum(k, 0)))
        when_unit(0, stage_q2)
        when_unit(-1, stage_f)

        @pl.when(i == 1)
        def _():
            own_4(wa, z)
            own_5(wa, z)

        pl.when(i == 2)(lambda: relay(1, 0))

        @pl.when(i == 3)
        def _():
            relay(1, 1)
            relay(2, 0)

        @pl.when(i == 4)
        def _():
            relay(2, 1)
            relay(3, 0)

        pl.when(i == 5)(lambda: relay(3, 1))
        pl.when(i == 6)(relay_end)

    @pl.loop(0, ROWS // 32)
    def _(i):
        rows = pl.ds(pl.multiple_of(i * 32, 32), 32)
        gp[rows, :] = (gr[rows, :].astype(F32) * gd[3, rows, :]).astype(BF16)

    @pl.loop(0, 3 - s)
    def _(step):
        k = 3 - step

        @pl.loop(0, 2)
        def _(j):
            tile = jnp.concatenate(
                [
                    w[2 * k + h, j].reshape(HALF, width)
                    for h in range(2)
                    for w, width in ((wa, XY), (wz, Z))
                ],
                axis=1,
            )
            gn[:, part(j, 0, HALF)] = lax.dot_general(
                gp[...], tile, (((1,), (1,)), ((), ())), preferred_element_type=F32
            )

        @pl.loop(0, ROWS // 32)
        def _(i):
            rows = pl.ds(pl.multiple_of(i * 32, 32), 32)
            xf = section_rows(k, i)
            g = gn[rows, :]
            inv = iv[k, rows, :][:, :1]
            mean = jnp.mean(g * xf, axis=-1, keepdims=True)
            grad = gr[rows, :].astype(F32) + inv * g - xf * (inv * inv * inv * mean)
            grad = grad.astype(BF16)
            gr[rows, :] = grad
            gp[rows, :] = (grad.astype(F32) * gd[k - 1, rows, :]).astype(BF16)

    gw[c] = gp[:, mine]
    give_g = remote(gp.at[:, other], gw.at[c], nsend.at[1], nrecv.at[1], sib)
    give_g.start()

    remote(nw.at[1 - c], nw.at[1 - c], nsend.at[0], nrecv.at[0], sib).wait_recv()
    remote(gw.at[1 - c], gw.at[1 - c], nsend.at[1], nrecv.at[1], sib).wait_recv()

    def weight_term(v):
        @pl.loop(0, 4)
        def _(j):
            cols = pl.ds(pl.multiple_of(v * HALF + j * 256, 256), 256)
            total = None
            for half in range(2):
                part = lax.dot_general(
                    nw[half, :, cols], gw[half], (((0,), (0,)), ((), ())),
                    preferred_element_type=F32,
                )
                total = part if total is None else total + part
            xs[4 * v + j] = total.astype(BF16).reshape(4, 64, HALF)

    def grow(cc, v, i, first=0, count=4):
        if cc == 0:
            return xs.at[4 * v + i, pl.ds(first, count)]
        return xs.at[pl.ds(4 * v + first, count), i]

    def gchip(cc, v, i, part=None):
        at = (4 * v + y, i) if cc == 0 else (4 * v + i, x)
        return xs.at[at] if part is None else xs.at[at + (part,)]

    def r1_copies(cc, v):
        far = y2 if cc == 0 else x2
        to_plus, to_minus = (dyp, dym) if cc == 0 else (dxp, dxm)
        return (
            remote(grow(cc, v, far, 0, 2), r1.at[v, 0], r1s.at[v, 0], r1r.at[v, 0], to_plus),
            remote(grow(cc, v, far, 2, 2), r1.at[v, 1], r1s.at[v, 1], r1r.at[v, 1], to_minus),
        )

    def r2_copies(cc, v):
        plus, minus = (yp, ym) if cc == 0 else (xp, xm)
        to_plus, to_minus = (dyp, dym) if cc == 0 else (dxp, dxm)
        return (
            remote(grow(cc, v, plus), r2.at[v, 0], r2s.at[v, 0], r2r.at[v, 0], to_plus),
            remote(grow(cc, v, minus), r2.at[v, 1], r2s.at[v, 1], r2r.at[v, 1], to_minus),
        )

    def t1_copies(cc, v):
        far = x2 if cc == 0 else y2
        to_plus, to_minus = (dxp, dxm) if cc == 0 else (dyp, dym)
        return (
            remote(gchip(cc, v, far, TOP), t1.at[v, 0], t1s.at[v, 0], t1r.at[v, 0], to_plus),
            remote(gchip(cc, v, far, BOTTOM), t1.at[v, 1], t1s.at[v, 1], t1r.at[v, 1], to_minus),
        )

    def t2_copies(cc, v):
        plus, minus = (xp, xm) if cc == 0 else (yp, ym)
        to_plus, to_minus = (dxp, dxm) if cc == 0 else (dyp, dym)
        return (
            remote(gchip(cc, v, plus), t2.at[v, 0], t2s.at[v, 0], t2r.at[v, 0], to_plus),
            remote(gchip(cc, v, minus), t2.at[v, 1], t2s.at[v, 1], t2r.at[v, 1], to_minus),
        )

    def add_into(ref, *others):
        total = ref[...].astype(F32)
        for more in others:
            total = total + more[...].astype(F32)
        ref[...] = total.astype(BF16)

    def rs_a(v):
        def body(cc):
            for copy in r1_copies(cc, v):
                copy.start()

        by_core(body)

    def rs_b(v):
        def body(cc):
            plus, minus = (yp, ym) if cc == 0 else (xp, xm)
            arrive, leave = r1_copies(cc, v), r2_copies(cc, v)
            arrive[0].wait_recv()
            add_into(grow(cc, v, plus, 0, 2), r1.at[v, 0])
            leave[0].start()
            arrive[1].wait_recv()
            add_into(grow(cc, v, minus, 2, 2), r1.at[v, 1])
            leave[1].start()

        by_core(body)

    def rs_c(v):
        def body(cc):
            me = y if cc == 0 else x
            arrive, leave = r2_copies(cc, v), t1_copies(cc, v)
            arrive[0].wait_recv()
            arrive[1].wait_recv()
            for i in range(4):
                block = gchip(cc, v, i)
                add_into(block, r2.at[v, 0, i], r2.at[v, 1, i])
            for copy in leave:
                copy.start()

        by_core(body)

    def rs_d(v):
        def body(cc):
            plus, minus = (xp, xm) if cc == 0 else (yp, ym)
            arrive, leave = t1_copies(cc, v), t2_copies(cc, v)
            arrive[0].wait_recv()
            add_into(gchip(cc, v, plus, TOP), t1.at[v, 0])
            leave[0].start()
            arrive[1].wait_recv()
            add_into(gchip(cc, v, minus, BOTTOM), t1.at[v, 1])
            leave[1].start()

        by_core(body)

    def rs_e(v):
        def body(cc):
            for copy in t2_copies(cc, v):
                copy.wait_recv()

        by_core(body)
        return (
            xs[4 * v + y, x].astype(F32) + t2[v, 0].astype(F32) + t2[v, 1].astype(F32)
        )

    v0, v1 = 1 - zl, zl
    weight_term(v0)
    rs_a(v0)
    weight_term(v1)
    rs_a(v1)
    rs_b(v0)
    rs_b(v1)
    rs_c(v0)
    rs_c(v1)
    rs_d(v0)
    rs_d(v1)
    xs[4 * v0 + y, x] = rs_e(v0).astype(BF16)
    def cross(core):
        rows = pl.ds(pl.multiple_of(core * 32, 32), 32)
        dest = device(x, y, 2 * s + 1 - zl, core)
        return remote(xs.at[4 * v0 + y, x, rows], z1.at[c], zsend.at[core], zrecv.at[c], dest)

    cross(0).start()
    cross(1).start()
    sf[...] = rs_e(v1)
    last = remote(sf.at[sib_rows], o1, osend, orecv, sib)
    last.start()
    for core in range(2):
        remote(z1.at[core], z1.at[core], zsend.at[core], zrecv.at[core], sib).wait_recv()
    out_ref[:, mine] = sf[my_rows, :] + z1[c].astype(F32)
    last.wait_recv()
    out_ref[:, other] = o1[...] + z1[1 - c].astype(F32)

    for copy in gives(1 - c, my_rows):
        copy.wait_send()
    for d in range(1, 8):
        raw(d).wait_send()

    @pl.loop(0, UNITS)
    def _(u):
        def body(cc):
            for copy in p_copies(wa, cc, u, u):
                copy.wait_send()
            for i in range(4):
                d_copy(wa, cc, u, u, i).wait_send()

            @pl.when(u != z)
            def _():
                for copy in q_copies(wa, cc, u, u):
                    copy.wait_send()

        by_core(body)

    def own_sent(cc):
        for copy in p_copies(wz, cc, z, UNITS):
            copy.wait_send()
        for copy in o_copies(wz, cc, UNITS) + o_copies(wa, cc, z):
            copy.wait_send()
        for i in range(4):
            d_copy(wz, cc, z, UNITS, i).wait_send()

    by_core(own_sent)
    for i in range(2):
        for r in range(1, 4):
            up(r, i).wait_send()
            down(r, i).wait_send()
        for slot in range(7):
            e_copy(slot, i).wait_send()
    up(4, 0).wait_send()
    down(4, 1).wait_send()
    last.wait_send()
    cross(0).wait_send()
    cross(1).wait_send()
    give_g.wait_send()
    normed_copy().wait_send()

    @pl.loop(0, 2)
    def _(v):
        def body(cc):
            for copies in (r1_copies, r2_copies, t1_copies, t2_copies):
                for copy in copies(cc, v):
                    copy.wait_send()

        by_core(body)


def local(inputs, weights, cotangents, lengths):
    rows = inputs.shape[0] * inputs.shape[1]
    dma = pltpu.SemaphoreType.DMA
    vmem = pl.BlockSpec(memory_space=pltpu.VMEM)
    out = pl.pallas_call(
        kernel,
        out_shape=jax.ShapeDtypeStruct((32, D), F32),
        in_specs=[
            pl.BlockSpec(memory_space=pl.ANY),
            vmem,
            vmem,
            pl.BlockSpec(memory_space=pltpu.SMEM),
        ],
        out_specs=vmem,
        scratch_shapes=[
            pltpu.VMEM((8, 2, 4, 4, 64, XY), BF16),
            pltpu.VMEM((8, 2, 4, 4, 64, Z), BF16),
            pltpu.VMEM((8, 4, 64, HALF), BF16),
            pltpu.VMEM((4, ROWS, D), F32),
            pltpu.VMEM((4, ROWS, 128), F32),
            pltpu.VMEM((ROWS, D), BF16),
            pltpu.VMEM((2, ROWS, D), BF16),
            pltpu.VMEM((2, ROWS, HALF), BF16),
            pltpu.VMEM((ROWS, D), BF16),
            pltpu.VMEM((ROWS, D), F32),
            pltpu.VMEM((2, 2, 2, 64, HALF), BF16),
            pltpu.VMEM((2, 2, 4, 64, HALF), BF16),
            pltpu.VMEM((2, 2, 32, HALF), BF16),
            pltpu.VMEM((2, 2, 64, HALF), BF16),
            pltpu.VMEM((2, 32, HALF), BF16),
            pltpu.VMEM((64, HALF), F32),
            pltpu.VMEM((32, HALF), F32),
            dma((4,)),
            dma((2,)),
            dma((2,)),
            dma((7,)),
            dma((8,)),
            dma((4, 2)),
            dma((4, 2)),
            dma((4, 2)),
            dma((4, 2)),
            dma((7, 2)),
            dma((7, 2)),
            dma((9, 4)),
            dma((9, 4)),
            dma((9, 12)),
            dma((9, 12)),
            dma((9, 4)),
            dma((9, 4)),
            dma((2,)),
            dma((2,)),
            dma((2, 2)),
            dma((2, 2)),
            dma((2, 2)),
            dma((2, 2)),
            dma((2, 2)),
            dma((2, 2)),
            dma((2, 2)),
            dma((2, 2)),
            dma((2,)),
            dma((2,)),
            dma,
            dma,
        ],
        compiler_params=pltpu.CompilerParams(
            collective_id=0, has_side_effects=True, vmem_limit_bytes=63 * 2**20
        ),
        cost_estimate=pl.CostEstimate(
            flops=9 * 2 * ROWS * D * D, bytes_accessed=36 * 2**20, transcendentals=4 * ROWS * D
        ),
    )(inputs.reshape(4, rows // 4, D), weights[0], cotangents.reshape(rows, D), lengths)
    return out[None]


def solution(mesh):
    in_specs = (
        P(None, "fsdp", None),
        P("section", "fsdp", None),
        P(None, "fsdp", None),
        P(None, "fsdp"),
    )
    out_specs = P("section", "fsdp", None)
    return jax.shard_map(local, mesh=mesh, in_specs=in_specs, out_specs=out_specs, check_vma=False)
```

```python
import functools

import jax
import jax.numpy as jnp
from jax import lax
from jax.experimental import pallas as pl
from jax.experimental.pallas import tpu as pltpu
from jax.sharding import PartitionSpec as P

MESH = pl.DeviceIdType.MESH
F32 = jnp.float32
BF16 = jnp.bfloat16
EPS = 1e-06
GELU_C = 0.7978845608028654
GELU_A = 0.044715

D = 2048
ROWS = 256
HALF = 1024
XY = 768
Z = HALF - XY
UNITS = 8
READY = ((3, 6, 7, 9), (6, 7, 8, 9), (7, 8, 9, 10), (6, 7, 9, 10))
FIRST, SECOND = pl.ds(0, 2), pl.ds(2, 2)
TOP, BOTTOM = pl.ds(0, 32), pl.ds(32, 32)


def position():
    s, f = lax.axis_index("section"), lax.axis_index("fsdp")
    c = lax.rem(f, 2)
    x = lax.rem(f // 2, 4)
    y = lax.rem(f // 8, 4)
    zl = f // 32
    return s, zl, x, y, c


def device(x, y, z, c):
    return (z // 2, lax.rem(z, 2) * 32 + y * 8 + x * 2 + c)


def remote(src, dst, send, recv, dev):
    return pltpu.make_async_remote_copy(
        src_ref=src, dst_ref=dst, send_sem=send, recv_sem=recv, device_id=dev, device_id_type=MESH
    )


def kernel(
    x_ref, w_ref, cot_ref, len_ref, out_ref,
    wa, wz, xs, gd, iv, gp, nw, gw, gr, gn, r1, r2, t1, t2, z1, sf, o1,
    lens, loc, xsend, xrecv, rsend, rrecv, usend, urecv, lsend, lrecv, esend, erecv,
    psend, precv, qsend, qrecv, dsend, drecv,
    nsend, nrecv, gsend, r1r, r2r, t1r, t2r, zsend, zrecv, osend, orecv,
):
    s, zl, x, y, c = position()
    z = 2 * s + zl
    sib = device(x, y, z, 1 - c)
    xp, xm = lax.rem(x + 1, 4), lax.rem(x + 3, 4)
    yp, ym = lax.rem(y + 1, 4), lax.rem(y + 3, 4)
    x2, y2 = lax.rem(x + 2, 4), lax.rem(y + 2, 4)
    dxp, dxm = device(xp, y, z, c), device(xm, y, z, c)
    dyp, dym = device(x, yp, z, c), device(x, ym, z, c)

    barrier = pltpu.get_barrier_semaphore()
    above, below = device(x, y, lax.rem(z + 1, 8), c), device(x, y, lax.rem(z + 7, 8), c)
    pair_other = device(x, y, 2 * s + 1 - zl, 1 - c)
    for partner in (dxp, dxm, dyp, dym, above, below, sib, pair_other):
        pl.semaphore_signal(barrier, inc=1, device_id=partner, device_id_type=MESH)

    def part(core, first, width):
        return pl.ds(pl.multiple_of(core * HALF + first, 256), width)

    in_x = [
        pltpu.make_async_copy(x_ref.at[:, :, h * HALF : (h + 1) * HALF], xs.at[h], loc.at[3 * h])
        for h in range(2)
    ]
    in_x.append(pltpu.make_async_copy(cot_ref, gr, loc.at[4]))
    in_x.append(pltpu.make_async_copy(len_ref, lens, loc.at[5]))
    for copy in in_x:
        copy.start()
    mine = pl.ds(pl.multiple_of(c * HALF, HALF), HALF)
    other = pl.ds(pl.multiple_of((1 - c) * HALF, HALF), HALF)
    my_rows = pl.ds(pl.multiple_of(c * 32, 32), 32)
    sib_rows = pl.ds(pl.multiple_of((1 - c) * 32, 32), 32)
    in_w = [
        pltpu.make_async_copy(src, dst, loc.at[1 + i])
        for i, (src, dst) in enumerate(
            (
                (w_ref.at[:, part(c, 0, XY)], wa.at[2 * s + c, zl, y, x, my_rows]),
                (w_ref.at[:, part(c, XY, Z)], wz.at[2 * s + c, zl, y, x, my_rows]),
            )
        )
    ]
    for copy in in_w:
        copy.start()
    pl.semaphore_wait(barrier, 8)

    def gives(core, rows):
        kh = 2 * s + core
        return (
            remote(
                w_ref.at[:, part(core, XY, Z)], wz.at[kh, zl, y, x, rows],
                xsend.at[0], xrecv.at[0], sib,
            ),
            remote(
                w_ref.at[:, part(core, 0, XY)], wa.at[kh, zl, y, x, rows],
                xsend.at[1], xrecv.at[1], sib,
            ),
        )

    for copy in gives(1 - c, my_rows):
        copy.start()
    for copy in in_w:
        copy.wait()
    for copy in gives(c, sib_rows):
        copy.wait_recv()

    def raw_block(d, half=None):
        v = lax.rem(z + 8 + d, 8)
        at = (2 * (v // 2) + c, lax.rem(v, 2), y, x)
        return wa.at[at] if half is None else wa.at[at + (half,)]

    def raw_up(r, half=None):
        block = raw_block(1 - r, half)
        return remote(block, block, rsend.at[0], rrecv.at[0, r - 1], above)

    def raw_down(r, half=None):
        block = raw_block(r - 1, half)
        return remote(block, block, rsend.at[1], rrecv.at[1, r - 1], below)

    def raw_landed(r):
        ups, downs = raw_block(-r, TOP if r == 4 else None), raw_block(r, BOTTOM if r == 4 else None)
        remote(ups, ups, rsend.at[0], rrecv.at[0, r - 1], above).wait_recv()
        remote(downs, downs, rsend.at[1], rrecv.at[1, r - 1], below).wait_recv()

    def raw_step(r):
        if r > 1:
            raw_landed(r - 1)
        raw_up(r, TOP if r == 4 else None).start()
        raw_down(r, BOTTOM if r == 4 else None).start()

    def row(w, cc, kh, uz, i, part=None):
        if cc == 0:
            return w.at[kh, uz, i] if part is None else w.at[kh, uz, i, part]
        return w.at[kh, uz, :, i] if part is None else w.at[kh, uz, part, i]

    def chip(w, cc, kh, uz, i, part=None):
        at = (kh, uz, y, i) if cc == 0 else (kh, uz, i, x)
        return w.at[at] if part is None else w.at[at + (part,)]

    def p_copies(w, cc, u, b):
        fam = 0 if w is wa else 1
        kh, uz = 2 * (u // 2) + cc, lax.rem(u, 2)
        me, plus, minus = (x, xp, xm) if cc == 0 else (y, yp, ym)
        to_plus, to_minus = (dxp, dxm) if cc == 0 else (dyp, dym)
        own = chip(w, cc, kh, uz, me)
        from_minus, from_plus = chip(w, cc, kh, uz, minus, TOP), chip(w, cc, kh, uz, plus, BOTTOM)
        return (
            remote(own, own, psend.at[fam], precv.at[b, 0], to_plus),
            remote(own, own, psend.at[fam], precv.at[b, 1], to_minus),
            remote(from_minus, from_minus, psend.at[fam], precv.at[b, 2], to_plus),
            remote(from_plus, from_plus, psend.at[fam], precv.at[b, 2], to_minus),
        )

    def p_landed(w, cc, u, b, i):
        kh, uz = 2 * (u // 2) + cc, lax.rem(u, 2)
        plus, minus, far = (xp, xm, x2) if cc == 0 else (yp, ym, y2)
        land = (
            chip(w, cc, kh, uz, minus),
            chip(w, cc, kh, uz, plus),
            chip(w, cc, kh, uz, far),
        )[i]
        remote(land, land, psend.at[0], precv.at[b, i], sib).wait_recv()

    def q_copies(w, cc, u, b):
        fam = 0 if w is wa else 1
        kh, uz = 2 * (u // 2) + cc, lax.rem(u, 2)
        me, plus, minus = (y, yp, ym) if cc == 0 else (x, xp, xm)
        to_plus, to_minus = (dyp, dym) if cc == 0 else (dxp, dxm)
        first, second = row(w, cc, kh, uz, me, FIRST), row(w, cc, kh, uz, me, SECOND)
        from_minus, from_plus = row(w, cc, kh, uz, minus, FIRST), row(w, cc, kh, uz, plus, SECOND)
        return (
            remote(first, first, qsend.at[fam], qrecv.at[b, 0], to_plus),
            remote(second, second, qsend.at[fam], qrecv.at[b, 1], to_minus),
            remote(second, second, qsend.at[fam], qrecv.at[b, 2], to_plus),
            remote(first, first, qsend.at[fam], qrecv.at[b, 2], to_minus),
            remote(from_minus, from_minus, qsend.at[fam], qrecv.at[b, 3], to_plus),
            remote(from_plus, from_plus, qsend.at[fam], qrecv.at[b, 3], to_minus),
        )

    def q_landed(w, cc, u, b, i):
        kh, uz = 2 * (u // 2) + cc, lax.rem(u, 2)
        plus, minus, far = (yp, ym, y2) if cc == 0 else (xp, xm, x2)
        land = (
            row(w, cc, kh, uz, minus, FIRST),
            row(w, cc, kh, uz, plus, SECOND),
            row(w, cc, kh, uz, far),
            row(w, cc, kh, uz, far),
        )[i]
        remote(land, land, qsend.at[0], qrecv.at[b, i], sib).wait_recv()

    def d_copy(w, cc, u, b, i):
        kh, uz = 2 * (u // 2) + cc, lax.rem(u, 2)
        at = ((y, ym, yp, y2) if cc == 0 else (x, xm, xp, x2))[i]
        block = row(w, cc, kh, uz, at)
        return remote(block, block, dsend.at[0 if w is wa else 1], drecv.at[b], sib)

    def by_core(body):
        for cc in (0, 1):
            pl.when(c == cc)(functools.partial(body, cc))

    def unit(t):
        rest = t - 2
        near = jnp.where(rest < 2, rest + 2, jnp.where(rest < 4, rest - 2, rest + 2))
        rest = jnp.where(s == 2, near, jnp.where(rest < 2 * s, rest, rest + 2))
        return jnp.where(t == 0, z, jnp.where(t == 1, 2 * s + 1 - zl, rest))

    def stage_p1(w, u, b):
        def body(cc):
            copies = p_copies(w, cc, u, b)
            copies[0].start()
            copies[1].start()

        by_core(body)

    def stage_p2(w, u, b):
        def body(cc):
            copies = p_copies(w, cc, u, b)
            p_landed(w, cc, u, b, 0)
            copies[2].start()
            p_landed(w, cc, u, b, 1)
            copies[3].start()

        by_core(body)

    def stage_q1(w, u, b):
        def body(cc):
            copies = q_copies(w, cc, u, b)
            p_landed(w, cc, u, b, 2)
            for copy in copies[:4]:
                copy.start()
            d_copy(w, cc, u, b, 0).start()

        by_core(body)

    def stage_q2(w, u, b):
        def body(cc):
            copies = q_copies(w, cc, u, b)
            q_landed(w, cc, u, b, 0)
            copies[4].start()
            q_landed(w, cc, u, b, 1)
            copies[5].start()

        by_core(body)

    def stage_f(w, u, b):
        def body(cc):
            q_landed(w, cc, u, b, 2)
            d_copy(w, cc, u, b, 1).start()
            d_copy(w, cc, u, b, 2).start()
            q_landed(w, cc, u, b, 3)
            d_copy(w, cc, u, b, 3).start()

        by_core(body)

    PARTS = (pl.ds(0, 2), pl.ds(2, 2))
    def plane(d, part, core=None):
        v = lax.rem(z + 8 + d, 8)
        core = c if core is None else core
        return wz.at[2 * (v // 2) + core, lax.rem(v, 2), PARTS[part]]

    def up(r, part):
        block = plane(1 - r, part)
        return remote(block, block, usend, urecv.at[r - 1, part], above)

    def down(r, part):
        block = plane(r - 1, part)
        return remote(block, block, lsend, lrecv.at[r - 1, part], below)

    def up_landed(r, part):
        block = plane(-r, part)
        remote(block, block, usend, urecv.at[r - 1, part], above).wait_recv()

    def down_landed(r, part):
        block = plane(r, part)
        remote(block, block, lsend, lrecv.at[r - 1, part], below).wait_recv()

    def e_copy(slot, part):
        d = (-1, -2, -3, 1, 2, 3, 4)[slot]
        block = plane(d, part)
        return remote(block, block, esend, erecv.at[slot], sib)

    def relay(r, part):
        up_landed(r, part)
        if r < 3 or part == 0:
            up(r + 1, part).start()
        down_landed(r, part)
        if r < 3 or part == 1:
            down(r + 1, part).start()
        e_copy(r - 1, part).start()
        e_copy(r + 2, part).start()

    def relay_end():
        up_landed(4, 0)
        e_copy(6, 0).start()
        down_landed(4, 1)
        e_copy(6, 1).start()

    def normed_copy():
        return remote(nw.at[c], nw.at[c], nsend.at[0], nrecv.at[0], sib)

    def section_rows(k, i):
        at = pl.ds(pl.multiple_of(lax.rem(i, 2) * 32, 32), 32)
        halves = [xs[2 * k + h, i // 2, at, :].astype(F32) for h in range(2)]
        return jnp.concatenate(halves, axis=1)

    def forward(k):
        @pl.loop(0, 2)
        def _(uz):
            u = 2 * k + uz

            block = wa.at[2 * k + 1 - c, uz]
            remote(block, block, dsend.at[0], drecv.at[u], sib).wait_recv()
            z_block = wz.at[2 * k + 1 - c, uz]

            @pl.when(u == z)
            def _():
                remote(z_block, z_block, dsend.at[1], drecv.at[UNITS], sib).wait_recv()

            @pl.when(u != z)
            def _():
                d = lax.rem(u - z + 8, 8)
                slot = jnp.where(d < 4, 2 + d, jnp.where(d == 4, 6, 7 - d))
                remote(z_block, z_block, esend, erecv.at[slot], sib).wait_recv()

        @pl.loop(0, ROWS // 32)
        def _(i):
            rows = pl.ds(pl.multiple_of(i * 32, 32), 32)
            xf = section_rows(k, i)
            inv = lax.rsqrt(jnp.mean(xf * xf, axis=-1, keepdims=True) + EPS)
            iv[k, rows, :] = jnp.broadcast_to(inv, (32, 128))
            gp[rows, :] = (xf * inv).astype(BF16)

        @pl.when(k == s)
        def _():
            nw[c] = gp[...]
            normed_copy().start()

        @pl.loop(0, 2)
        def _(h):
            cols = part(h, 0, HALF)
            w = jnp.concatenate(
                [wa[2 * k + h].reshape(D, XY), wz[2 * k + h].reshape(D, Z)], axis=1
            )
            u = jnp.dot(gp[...], w, preferred_element_type=F32)
            uu = u * u
            t = jnp.tanh((GELU_C * u) * (1.0 + GELU_A * uu))
            cdf = 0.5 * (1.0 + t)
            gd[k, :, cols] = cdf + (0.5 * GELU_C) * u * (1.0 - t * t) * (
                1.0 + (3.0 * GELU_A) * uu
            )

            @pl.when(k < 3)
            def _():
                nxt = jnp.minimum(k + 1, 3)
                before = xs[2 * k + h].reshape(ROWS, HALF)
                after = (before.astype(F32) + u * cdf).astype(BF16)
                xs[2 * nxt + h] = after.reshape(4, 64, HALF)

    own = unit(0)
    stage_p1(wz, own, UNITS)
    stage_p1(wa, own, own)
    raw_step(1)
    stage_p2(wz, own, UNITS)
    stage_p2(wa, own, own)
    raw_step(2)
    stage_q1(wz, own, UNITS)
    stage_q1(wa, own, own)
    for copy in in_x:
        copy.wait()
    for m in range(2):
        for q in range(2):
            rows = pl.ds(128 * m + 64 * q, 64)
            live = lax.broadcasted_iota(jnp.int32, (64, D), 0) < lens[m, q]
            gr[rows, :] = jnp.where(live, gr[rows, :].astype(F32), 0.0).astype(BF16)
    near = unit(1)
    stage_p1(wa, near, near)
    raw_step(3)
    stage_q2(wz, own, UNITS)
    stage_p2(wa, near, near)
    stage_q2(wa, own, own)
    stage_f(wz, own, UNITS)
    for i in range(2):
        up(1, i).start()
        down(1, i).start()
    raw_step(4)
    third = unit(2)
    stage_p1(wa, third, third)

    @pl.loop(1, UNITS + 3)
    def _(i):
        def when_unit(ahead, stage):
            @pl.when((i + ahead >= 0) & (i + ahead < UNITS))
            def _():
                u = unit(i + ahead)
                stage(wa, u, u)

        when_unit(0, stage_q1)
        pl.when(i == 2)(lambda: raw_landed(4))
        when_unit(2, stage_p1)
        when_unit(1, stage_p2)
        k = -1
        for section in range(4):
            for number in range(4):
                k = jnp.where((s == section) & (i == READY[section][number]), number, k)
        pl.when(k >= 0)(lambda: forward(jnp.maximum(k, 0)))
        when_unit(0, stage_q2)
        when_unit(-1, stage_f)
        pl.when(i == 1)(lambda: relay(1, 0))
        pl.when(i == 2)(lambda: relay(1, 1))
        pl.when(i == 3)(lambda: relay(2, 0))
        pl.when(i == 4)(lambda: relay(2, 1))

        @pl.when(i == 5)
        def _():
            relay(3, 0)
            relay(3, 1)

        pl.when(i == 6)(relay_end)

    @pl.loop(0, ROWS // 32)
    def _(i):
        rows = pl.ds(pl.multiple_of(i * 32, 32), 32)
        gp[rows, :] = (gr[rows, :].astype(F32) * gd[3, rows, :]).astype(BF16)

    @pl.loop(0, 3 - s)
    def _(step):
        k = 3 - step

        @pl.loop(0, 2)
        def _(j):
            tile = jnp.concatenate(
                [
                    w[2 * k + h, j].reshape(HALF, width)
                    for h in range(2)
                    for w, width in ((wa, XY), (wz, Z))
                ],
                axis=1,
            )
            gn[:, part(j, 0, HALF)] = lax.dot_general(
                gp[...], tile, (((1,), (1,)), ((), ())), preferred_element_type=F32
            )

        @pl.loop(0, ROWS // 32)
        def _(i):
            rows = pl.ds(pl.multiple_of(i * 32, 32), 32)
            xf = section_rows(k, i)
            g = gn[rows, :]
            inv = iv[k, rows, :][:, :1]
            mean = jnp.mean(g * xf, axis=-1, keepdims=True)
            grad = gr[rows, :].astype(F32) + inv * g - xf * (inv * inv * inv * mean)
            grad = grad.astype(BF16)
            gr[rows, :] = grad
            gp[rows, :] = (grad.astype(F32) * gd[k - 1, rows, :]).astype(BF16)

    gw[c] = gp[:, mine]
    give_g = remote(gp.at[:, other], gw.at[c], nsend.at[1], nrecv.at[1], sib)
    give_g.start()

    remote(nw.at[1 - c], nw.at[1 - c], nsend.at[0], nrecv.at[0], sib).wait_recv()
    remote(gw.at[1 - c], gw.at[1 - c], nsend.at[1], nrecv.at[1], sib).wait_recv()

    def weight_term(v):
        @pl.loop(0, 4)
        def _(j):
            cols = pl.ds(pl.multiple_of(v * HALF + j * 256, 256), 256)
            total = None
            for half in range(2):
                part = lax.dot_general(
                    nw[half, :, cols], gw[half], (((0,), (0,)), ((), ())),
                    preferred_element_type=F32,
                )
                total = part if total is None else total + part
            xs[4 * v + j] = total.astype(BF16).reshape(4, 64, HALF)

    def grow(cc, v, i, first=0, count=4):
        if cc == 0:
            return xs.at[4 * v + i, pl.ds(first, count)]
        return xs.at[pl.ds(4 * v + first, count), i]

    def gchip(cc, v, i, part=None):
        at = (4 * v + y, i) if cc == 0 else (4 * v + i, x)
        return xs.at[at] if part is None else xs.at[at + (part,)]

    def r1_copies(cc, v):
        far = y2 if cc == 0 else x2
        to_plus, to_minus = (dyp, dym) if cc == 0 else (dxp, dxm)
        return (
            remote(grow(cc, v, far, 0, 2), r1.at[v, 0], gsend.at[0], r1r.at[v, 0], to_plus),
            remote(grow(cc, v, far, 2, 2), r1.at[v, 1], gsend.at[0], r1r.at[v, 1], to_minus),
        )

    def r2_copies(cc, v):
        plus, minus = (yp, ym) if cc == 0 else (xp, xm)
        to_plus, to_minus = (dyp, dym) if cc == 0 else (dxp, dxm)
        return (
            remote(grow(cc, v, plus), r2.at[v, 0], gsend.at[1], r2r.at[v], to_plus),
            remote(grow(cc, v, minus), r2.at[v, 1], gsend.at[1], r2r.at[v], to_minus),
        )

    def t1_copies(cc, v):
        far = x2 if cc == 0 else y2
        to_plus, to_minus = (dxp, dxm) if cc == 0 else (dyp, dym)
        return (
            remote(gchip(cc, v, far, TOP), t1.at[v, 0], gsend.at[2], t1r.at[v, 0], to_plus),
            remote(gchip(cc, v, far, BOTTOM), t1.at[v, 1], gsend.at[2], t1r.at[v, 1], to_minus),
        )

    def t2_copies(cc, v):
        plus, minus = (xp, xm) if cc == 0 else (yp, ym)
        to_plus, to_minus = (dxp, dxm) if cc == 0 else (dyp, dym)
        return (
            remote(gchip(cc, v, plus), t2.at[v, 0], gsend.at[3], t2r.at[v], to_plus),
            remote(gchip(cc, v, minus), t2.at[v, 1], gsend.at[3], t2r.at[v], to_minus),
        )

    def add_into(ref, *others):
        total = ref[...].astype(F32)
        for more in others:
            total = total + more[...].astype(F32)
        ref[...] = total.astype(BF16)

    def rs_a(v):
        def body(cc):
            for copy in r1_copies(cc, v):
                copy.start()

        by_core(body)

    def rs_b(v):
        def body(cc):
            plus, minus = (yp, ym) if cc == 0 else (xp, xm)
            arrive, leave = r1_copies(cc, v), r2_copies(cc, v)
            arrive[0].wait_recv()
            add_into(grow(cc, v, plus, 0, 2), r1.at[v, 0])
            leave[0].start()
            arrive[1].wait_recv()
            add_into(grow(cc, v, minus, 2, 2), r1.at[v, 1])
            leave[1].start()

        by_core(body)

    def rs_c(v):
        def body(cc):
            leave = t1_copies(cc, v)
            remote(r2.at[v], r2.at[v], gsend.at[1], r2r.at[v], sib).wait_recv()

            def add(i):
                add_into(gchip(cc, v, i), r2.at[v, 0, i], r2.at[v, 1, i])

            me, plus, minus, far = (x, xp, xm, x2) if cc == 0 else (y, yp, ym, y2)
            add(far)
            for copy in leave:
                copy.start()
            for i in (plus, minus, me):
                add(i)

        by_core(body)

    def rs_d(v):
        def body(cc):
            plus, minus = (xp, xm) if cc == 0 else (yp, ym)
            arrive, leave = t1_copies(cc, v), t2_copies(cc, v)
            arrive[0].wait_recv()
            add_into(gchip(cc, v, plus, TOP), t1.at[v, 0])
            leave[0].start()
            arrive[1].wait_recv()
            add_into(gchip(cc, v, minus, BOTTOM), t1.at[v, 1])
            leave[1].start()

        by_core(body)

    def rs_e(v):
        remote(t2.at[v], t2.at[v], gsend.at[3], t2r.at[v], sib).wait_recv()
        return (
            xs[4 * v + y, x].astype(F32) + t2[v, 0].astype(F32) + t2[v, 1].astype(F32)
        )

    v0, v1 = 1 - zl, zl
    weight_term(v0)
    rs_a(v0)
    weight_term(v1)
    rs_a(v1)

    def sent(block, sem):
        remote(block, block, sem, sem, sib).wait_send()

    for copy in gives(1 - c, my_rows):
        copy.wait_send()
    for way in range(2):
        sent(wa.at[pl.ds(0, 7), 0, 0, 0, TOP], rsend.at[way])
    sent(wa.at[0, :, pl.ds(0, 3)], psend.at[0])
    sent(wz.at[0, 0, 0, pl.ds(0, 3)], psend.at[1])
    sent(wa.at[pl.ds(0, 3)], qsend.at[0])
    sent(wz.at[0, 0, pl.ds(0, 3)], qsend.at[1])
    sent(wa.at[pl.ds(0, 4)], dsend.at[0])
    sent(wz.at[0, 0], dsend.at[1])
    sent(wz.at[pl.ds(0, 7), 0, pl.ds(0, 2)], usend)
    sent(wz.at[pl.ds(0, 7), 0, pl.ds(0, 2)], lsend)
    sent(wz.at[pl.ds(0, 7), :, pl.ds(0, 2)], esend)

    rs_b(v0)
    rs_b(v1)
    rs_c(v0)
    rs_c(v1)
    rs_d(v0)
    rs_d(v1)
    xs[4 * v0 + y, x] = rs_e(v0).astype(BF16)
    def cross(core):
        rows = pl.ds(pl.multiple_of(core * 32, 32), 32)
        dest = device(x, y, 2 * s + 1 - zl, core)
        return remote(xs.at[4 * v0 + y, x, rows], z1.at[c], zsend, zrecv, dest)

    cross(0).start()
    cross(1).start()
    sf[...] = rs_e(v1)
    last = remote(sf.at[sib_rows], o1, osend, orecv, sib)
    last.start()
    remote(z1, z1, zsend, zrecv, sib).wait_recv()
    out_ref[:, mine] = sf[my_rows, :] + z1[c].astype(F32)
    last.wait_recv()
    out_ref[:, other] = o1[...] + z1[1 - c].astype(F32)

    last.wait_send()
    sent(z1, zsend)
    give_g.wait_send()
    normed_copy().wait_send()
    sent(r1, gsend.at[0])
    sent(r2, gsend.at[1])
    sent(t1, gsend.at[2])
    sent(t2, gsend.at[3])


def local(inputs, weights, cotangents, lengths):
    rows = inputs.shape[0] * inputs.shape[1]
    dma = pltpu.SemaphoreType.DMA
    vmem = pl.BlockSpec(memory_space=pltpu.VMEM)
    out = pl.pallas_call(
        kernel,
        out_shape=jax.ShapeDtypeStruct((32, D), F32),
        in_specs=[
            pl.BlockSpec(memory_space=pl.ANY),
            vmem,
            pl.BlockSpec(memory_space=pl.ANY),
            pl.BlockSpec(memory_space=pl.ANY),
        ],
        out_specs=vmem,
        scratch_shapes=[
            pltpu.VMEM((8, 2, 4, 4, 64, XY), BF16),
            pltpu.VMEM((8, 2, 4, 4, 64, Z), BF16),
            pltpu.VMEM((8, 4, 64, HALF), BF16),
            pltpu.VMEM((4, ROWS, D), F32),
            pltpu.VMEM((4, ROWS, 128), F32),
            pltpu.VMEM((ROWS, D), BF16),
            pltpu.VMEM((2, ROWS, D), BF16),
            pltpu.VMEM((2, ROWS, HALF), BF16),
            pltpu.VMEM((ROWS, D), BF16),
            pltpu.VMEM((ROWS, D), F32),
            pltpu.VMEM((2, 2, 2, 64, HALF), BF16),
            pltpu.VMEM((2, 2, 4, 64, HALF), BF16),
            pltpu.VMEM((2, 2, 32, HALF), BF16),
            pltpu.VMEM((2, 2, 64, HALF), BF16),
            pltpu.VMEM((2, 32, HALF), BF16),
            pltpu.VMEM((64, HALF), F32),
            pltpu.VMEM((32, HALF), F32),
            pltpu.SMEM((2, 2), jnp.int32),
            dma((6,)),
            dma((2,)),
            dma((2,)),
            dma((2,)),
            dma((2, 4)),
            dma,
            dma((4, 2)),
            dma,
            dma((4, 2)),
            dma,
            dma((7,)),
            dma((2,)),
            dma((9, 3)),
            dma((2,)),
            dma((9, 4)),
            dma((2,)),
            dma((9,)),
            dma((2,)),
            dma((2,)),
            dma((4,)),
            dma((2, 2)),
            dma((2,)),
            dma((2, 2)),
            dma((2,)),
            dma,
            dma,
            dma,
            dma,
        ],
        compiler_params=pltpu.CompilerParams(
            collective_id=0, has_side_effects=True, vmem_limit_bytes=63 * 2**20
        ),
        cost_estimate=pl.CostEstimate(
            flops=9 * 2 * ROWS * D * D, bytes_accessed=36 * 2**20, transcendentals=4 * ROWS * D
        ),
    )(inputs.reshape(4, rows // 4, D), weights[0], cotangents.reshape(rows, D), lengths)
    return out[None]


def solution(mesh):
    in_specs = (
        P(None, "fsdp", None),
        P("section", "fsdp", None),
        P(None, "fsdp", None),
        P(None, "fsdp"),
    )
    out_specs = P("section", "fsdp", None)
    return jax.shard_map(local, mesh=mesh, in_specs=in_specs, out_specs=out_specs, check_vma=False)
```

```python
import functools

import jax
import jax.numpy as jnp
from jax import lax
from jax.experimental import pallas as pl
from jax.experimental.pallas import tpu as pltpu
from jax.sharding import PartitionSpec as P

MESH = pl.DeviceIdType.MESH
F32 = jnp.float32
BF16 = jnp.bfloat16
EPS = 1e-06
GELU_C = 0.7978845608028654
GELU_A = 0.044715

D = 2048
ROWS = 256
HALF = 1024
XY = 768
Z = HALF - XY
UNITS = 8
READY = ((3, 6, 7, 9), (6, 7, 8, 9), (7, 8, 9, 10), (6, 7, 9, 10))
FIRST, SECOND = pl.ds(0, 2), pl.ds(2, 2)
TOP, BOTTOM = pl.ds(0, 32), pl.ds(32, 32)


def position():
    s, f = lax.axis_index("section"), lax.axis_index("fsdp")
    c = lax.rem(f, 2)
    x = lax.rem(f // 2, 4)
    y = lax.rem(f // 8, 4)
    zl = f // 32
    return s, zl, x, y, c


def device(x, y, z, c):
    return (z // 2, lax.rem(z, 2) * 32 + y * 8 + x * 2 + c)


def remote(src, dst, send, recv, dev):
    return pltpu.make_async_remote_copy(
        src_ref=src, dst_ref=dst, send_sem=send, recv_sem=recv, device_id=dev, device_id_type=MESH
    )


def kernel(
    x_ref, w_ref, cot_ref, len_ref, out_ref,
    wa, wz, xs, gd, ub, iv, gp, nw, gw, gr, ms, r1, r2, t1, t2, z1, sf, o1,
    lens, loc, xsend, xrecv, rsend, rrecv, usend, urecv, lsend, lrecv, esend, erecv,
    psend, precv, qsend, qrecv, dsend, drecv,
    nsend, nrecv, gsend, r1r, r2r, t1r, t2r, zsend, zrecv, osend, orecv,
):
    s, zl, x, y, c = position()
    z = 2 * s + zl
    sib = device(x, y, z, 1 - c)
    xp, xm = lax.rem(x + 1, 4), lax.rem(x + 3, 4)
    yp, ym = lax.rem(y + 1, 4), lax.rem(y + 3, 4)
    x2, y2 = lax.rem(x + 2, 4), lax.rem(y + 2, 4)
    dxp, dxm = device(xp, y, z, c), device(xm, y, z, c)
    dyp, dym = device(x, yp, z, c), device(x, ym, z, c)

    barrier = pltpu.get_barrier_semaphore()
    above, below = device(x, y, lax.rem(z + 1, 8), c), device(x, y, lax.rem(z + 7, 8), c)
    pair_other = device(x, y, 2 * s + 1 - zl, 1 - c)
    for partner in (dxp, dxm, dyp, dym, above, below, sib, pair_other):
        pl.semaphore_signal(barrier, inc=1, device_id=partner, device_id_type=MESH)

    def part(core, first, width):
        return pl.ds(pl.multiple_of(core * HALF + first, 256), width)

    in_x = [
        pltpu.make_async_copy(x_ref.at[:, :, h * HALF : (h + 1) * HALF], xs.at[h], loc.at[3 * h])
        for h in range(2)
    ]
    in_x.append(pltpu.make_async_copy(cot_ref, gr, loc.at[4]))
    in_x.append(pltpu.make_async_copy(len_ref, lens, loc.at[5]))
    for copy in in_x:
        copy.start()
    mine = pl.ds(pl.multiple_of(c * HALF, HALF), HALF)
    other = pl.ds(pl.multiple_of((1 - c) * HALF, HALF), HALF)
    my_rows = pl.ds(pl.multiple_of(c * 32, 32), 32)
    sib_rows = pl.ds(pl.multiple_of((1 - c) * 32, 32), 32)
    in_w = [
        pltpu.make_async_copy(src, dst, loc.at[1 + i])
        for i, (src, dst) in enumerate(
            (
                (w_ref.at[:, part(c, 0, XY)], wa.at[2 * s + c, zl, y, x, my_rows]),
                (w_ref.at[:, part(c, XY, Z)], wz.at[2 * s + c, zl, y, x, my_rows]),
            )
        )
    ]
    for copy in in_w:
        copy.start()
    pl.semaphore_wait(barrier, 8)

    def gives(core, rows):
        kh = 2 * s + core
        return (
            remote(
                w_ref.at[:, part(core, XY, Z)], wz.at[kh, zl, y, x, rows],
                xsend.at[0], xrecv.at[0], sib,
            ),
            remote(
                w_ref.at[:, part(core, 0, XY)], wa.at[kh, zl, y, x, rows],
                xsend.at[1], xrecv.at[1], sib,
            ),
        )

    for copy in gives(1 - c, my_rows):
        copy.start()
    for copy in in_w:
        copy.wait()
    for copy in gives(c, sib_rows):
        copy.wait_recv()

    def raw_block(d, half=None):
        v = lax.rem(z + 8 + d, 8)
        at = (2 * (v // 2) + c, lax.rem(v, 2), y, x)
        return wa.at[at] if half is None else wa.at[at + (half,)]

    def raw_up(r, half=None):
        block = raw_block(1 - r, half)
        return remote(block, block, rsend.at[0], rrecv.at[0, r - 1], above)

    def raw_down(r, half=None):
        block = raw_block(r - 1, half)
        return remote(block, block, rsend.at[1], rrecv.at[1, r - 1], below)

    def raw_landed(r):
        ups, downs = raw_block(-r, TOP if r == 4 else None), raw_block(r, BOTTOM if r == 4 else None)
        remote(ups, ups, rsend.at[0], rrecv.at[0, r - 1], above).wait_recv()
        remote(downs, downs, rsend.at[1], rrecv.at[1, r - 1], below).wait_recv()

    def raw_step(r):
        if r > 1:
            raw_landed(r - 1)
        raw_up(r, TOP if r == 4 else None).start()
        raw_down(r, BOTTOM if r == 4 else None).start()

    def row(w, cc, kh, uz, i, part=None):
        if cc == 0:
            return w.at[kh, uz, i] if part is None else w.at[kh, uz, i, part]
        return w.at[kh, uz, :, i] if part is None else w.at[kh, uz, part, i]

    def chip(w, cc, kh, uz, i, part=None):
        at = (kh, uz, y, i) if cc == 0 else (kh, uz, i, x)
        return w.at[at] if part is None else w.at[at + (part,)]

    def p_copies(w, cc, u, b):
        fam = 0 if w is wa else 1
        kh, uz = 2 * (u // 2) + cc, lax.rem(u, 2)
        me, plus, minus = (x, xp, xm) if cc == 0 else (y, yp, ym)
        to_plus, to_minus = (dxp, dxm) if cc == 0 else (dyp, dym)
        own = chip(w, cc, kh, uz, me)
        from_minus, from_plus = chip(w, cc, kh, uz, minus, TOP), chip(w, cc, kh, uz, plus, BOTTOM)
        return (
            remote(own, own, psend.at[fam], precv.at[b, 0], to_plus),
            remote(own, own, psend.at[fam], precv.at[b, 1], to_minus),
            remote(from_minus, from_minus, psend.at[fam], precv.at[b, 2], to_plus),
            remote(from_plus, from_plus, psend.at[fam], precv.at[b, 2], to_minus),
        )

    def p_landed(w, cc, u, b, i):
        kh, uz = 2 * (u // 2) + cc, lax.rem(u, 2)
        plus, minus, far = (xp, xm, x2) if cc == 0 else (yp, ym, y2)
        land = (
            chip(w, cc, kh, uz, minus),
            chip(w, cc, kh, uz, plus),
            chip(w, cc, kh, uz, far),
        )[i]
        remote(land, land, psend.at[0], precv.at[b, i], sib).wait_recv()

    def q_copies(w, cc, u, b):
        fam = 0 if w is wa else 1
        kh, uz = 2 * (u // 2) + cc, lax.rem(u, 2)
        me, plus, minus = (y, yp, ym) if cc == 0 else (x, xp, xm)
        to_plus, to_minus = (dyp, dym) if cc == 0 else (dxp, dxm)
        first, second = row(w, cc, kh, uz, me, FIRST), row(w, cc, kh, uz, me, SECOND)
        from_minus, from_plus = row(w, cc, kh, uz, minus, FIRST), row(w, cc, kh, uz, plus, SECOND)
        return (
            remote(first, first, qsend.at[fam], qrecv.at[b, 0], to_plus),
            remote(second, second, qsend.at[fam], qrecv.at[b, 1], to_minus),
            remote(second, second, qsend.at[fam], qrecv.at[b, 2], to_plus),
            remote(first, first, qsend.at[fam], qrecv.at[b, 2], to_minus),
            remote(from_minus, from_minus, qsend.at[fam], qrecv.at[b, 3], to_plus),
            remote(from_plus, from_plus, qsend.at[fam], qrecv.at[b, 3], to_minus),
        )

    def q_landed(w, cc, u, b, i):
        kh, uz = 2 * (u // 2) + cc, lax.rem(u, 2)
        plus, minus, far = (yp, ym, y2) if cc == 0 else (xp, xm, x2)
        land = (
            row(w, cc, kh, uz, minus, FIRST),
            row(w, cc, kh, uz, plus, SECOND),
            row(w, cc, kh, uz, far),
            row(w, cc, kh, uz, far),
        )[i]
        remote(land, land, qsend.at[0], qrecv.at[b, i], sib).wait_recv()

    def d_copy(w, cc, u, b, i):
        kh, uz = 2 * (u // 2) + cc, lax.rem(u, 2)
        at = ((y, ym, yp, y2) if cc == 0 else (x, xm, xp, x2))[i]
        block = row(w, cc, kh, uz, at)
        return remote(block, block, dsend.at[0 if w is wa else 1], drecv.at[b], sib)

    def by_core(body):
        for cc in (0, 1):
            pl.when(c == cc)(functools.partial(body, cc))

    def unit(t):
        rest = t - 2
        near = jnp.where(rest < 2, rest + 2, jnp.where(rest < 4, rest - 2, rest + 2))
        rest = jnp.where(s == 2, near, jnp.where(rest < 2 * s, rest, rest + 2))
        return jnp.where(t == 0, z, jnp.where(t == 1, 2 * s + 1 - zl, rest))

    def stage_p1(w, u, b):
        def body(cc):
            copies = p_copies(w, cc, u, b)
            copies[0].start()
            copies[1].start()

        by_core(body)

    def stage_p2(w, u, b):
        def body(cc):
            copies = p_copies(w, cc, u, b)
            p_landed(w, cc, u, b, 0)
            copies[2].start()
            p_landed(w, cc, u, b, 1)
            copies[3].start()

        by_core(body)

    def stage_q1(w, u, b):
        def body(cc):
            copies = q_copies(w, cc, u, b)
            p_landed(w, cc, u, b, 2)
            for copy in copies[:4]:
                copy.start()
            d_copy(w, cc, u, b, 0).start()

        by_core(body)

    def stage_q2(w, u, b):
        def body(cc):
            copies = q_copies(w, cc, u, b)
            q_landed(w, cc, u, b, 0)
            copies[4].start()
            q_landed(w, cc, u, b, 1)
            copies[5].start()

        by_core(body)

    def stage_f(w, u, b):
        def body(cc):
            q_landed(w, cc, u, b, 2)
            d_copy(w, cc, u, b, 1).start()
            d_copy(w, cc, u, b, 2).start()
            q_landed(w, cc, u, b, 3)
            d_copy(w, cc, u, b, 3).start()

        by_core(body)

    PARTS = (pl.ds(0, 2), pl.ds(2, 2))
    def plane(d, part, core=None):
        v = lax.rem(z + 8 + d, 8)
        core = c if core is None else core
        return wz.at[2 * (v // 2) + core, lax.rem(v, 2), PARTS[part]]

    def up(r, part):
        block = plane(1 - r, part)
        return remote(block, block, usend, urecv.at[r - 1, part], above)

    def down(r, part):
        block = plane(r - 1, part)
        return remote(block, block, lsend, lrecv.at[r - 1, part], below)

    def up_landed(r, part):
        block = plane(-r, part)
        remote(block, block, usend, urecv.at[r - 1, part], above).wait_recv()

    def down_landed(r, part):
        block = plane(r, part)
        remote(block, block, lsend, lrecv.at[r - 1, part], below).wait_recv()

    def e_copy(slot, part):
        d = (-1, -2, -3, 1, 2, 3, 4)[slot]
        block = plane(d, part)
        return remote(block, block, esend, erecv.at[slot], sib)

    def relay(r, part):
        up_landed(r, part)
        if r < 3 or part == 0:
            up(r + 1, part).start()
        down_landed(r, part)
        if r < 3 or part == 1:
            down(r + 1, part).start()
        e_copy(r - 1, part).start()
        e_copy(r + 2, part).start()

    def relay_end():
        up_landed(4, 0)
        e_copy(6, 0).start()
        down_landed(4, 1)
        e_copy(6, 1).start()

    def normed_copy():
        return remote(nw.at[c], nw.at[c], nsend.at[0], nrecv.at[0], sib)

    def section_rows(k, i):
        at = pl.ds(pl.multiple_of(lax.rem(i, 2) * 32, 32), 32)
        halves = [xs[2 * k + h, i // 2, at, :].astype(F32) for h in range(2)]
        return jnp.concatenate(halves, axis=1)

    def lane_sums(v):
        total = v[:, :128]
        for i in range(1, HALF // 128):
            total = total + v[:, i * 128 : (i + 1) * 128]
        return total

    def forward(k):
        @pl.loop(0, 2)
        def _(uz):
            u = 2 * k + uz

            block = wa.at[2 * k + 1 - c, uz]
            remote(block, block, dsend.at[0], drecv.at[u], sib).wait_recv()
            z_block = wz.at[2 * k + 1 - c, uz]

            @pl.when(u == z)
            def _():
                remote(z_block, z_block, dsend.at[1], drecv.at[UNITS], sib).wait_recv()

            @pl.when(u != z)
            def _():
                d = lax.rem(u - z + 8, 8)
                slot = jnp.where(d < 4, 2 + d, jnp.where(d == 4, 6, 7 - d))
                remote(z_block, z_block, esend, erecv.at[slot], sib).wait_recv()

        @pl.loop(0, ROWS // 32)
        def _(i):
            rows = pl.ds(pl.multiple_of(i * 32, 32), 32)
            xf = section_rows(k, i)
            inv = lax.rsqrt(jnp.mean(xf * xf, axis=-1, keepdims=True) + EPS)
            iv[k, rows, :] = jnp.broadcast_to(inv, (32, 128))
            gp[0, rows, :] = (xf * inv).astype(BF16)

        @pl.when(k == s)
        def _():
            nw[c] = gp[0]
            normed_copy().start()

        @pl.loop(0, 2)
        def _(h):
            cols = part(h, 0, HALF)
            w = jnp.concatenate(
                [wa[2 * k + h].reshape(D, XY), wz[2 * k + h].reshape(D, Z)], axis=1
            )
            u = jnp.dot(gp[0], w, preferred_element_type=F32)
            uu = u * u
            t = jnp.tanh((GELU_C * u) * (1.0 + GELU_A * uu))
            cdf = 0.5 * (1.0 + t)
            slope = cdf + (0.5 * GELU_C) * u * (1.0 - t * t) * (1.0 + (3.0 * GELU_A) * uu)

            @pl.when(k < 3)
            def _():
                at = jnp.minimum(k, 2)
                gd[at, :, cols] = slope
                ub[at, :, cols] = u.astype(BF16)
                before = xs[2 * k + h].reshape(ROWS, HALF)
                after = (before.astype(F32) + u * cdf).astype(BF16)
                xs[2 * at + 2 + h] = after.reshape(4, 64, HALF)

            @pl.when(k == 3)
            def _():
                pre = (gr[:, cols].astype(F32) * slope).astype(BF16)
                gp[1, :, cols] = pre
                term = lane_sums(pre.astype(F32) * u)
                ms[...] = jnp.where(h == 0, term, ms[...] + term)

    own = unit(0)
    stage_p1(wz, own, UNITS)
    stage_p1(wa, own, own)
    raw_step(1)
    stage_p2(wz, own, UNITS)
    stage_p2(wa, own, own)
    raw_step(2)
    stage_q1(wz, own, UNITS)
    stage_q1(wa, own, own)
    for copy in in_x:
        copy.wait()
    for m in range(2):
        for q in range(2):
            rows = pl.ds(128 * m + 64 * q, 64)
            live = lax.broadcasted_iota(jnp.int32, (64, D), 0) < lens[m, q]
            gr[rows, :] = jnp.where(live, gr[rows, :].astype(F32), 0.0).astype(BF16)
    near = unit(1)
    stage_p1(wa, near, near)
    raw_step(3)
    stage_q2(wz, own, UNITS)
    stage_p2(wa, near, near)
    stage_q2(wa, own, own)
    stage_f(wz, own, UNITS)
    for i in range(2):
        up(1, i).start()
        down(1, i).start()
    raw_step(4)
    third = unit(2)
    stage_p1(wa, third, third)

    @pl.loop(1, UNITS + 3)
    def _(i):
        def when_unit(ahead, stage):
            @pl.when((i + ahead >= 0) & (i + ahead < UNITS))
            def _():
                u = unit(i + ahead)
                stage(wa, u, u)

        when_unit(0, stage_q1)
        pl.when(i == 2)(lambda: raw_landed(4))
        when_unit(2, stage_p1)
        when_unit(1, stage_p2)
        k = -1
        for section in range(4):
            for number in range(4):
                k = jnp.where((s == section) & (i == READY[section][number]), number, k)
        pl.when(k >= 0)(lambda: forward(jnp.maximum(k, 0)))
        when_unit(0, stage_q2)
        when_unit(-1, stage_f)
        pl.when(i == 1)(lambda: relay(1, 0))
        pl.when(i == 2)(lambda: relay(1, 1))
        pl.when(i == 3)(lambda: relay(2, 0))
        pl.when(i == 4)(lambda: relay(2, 1))

        @pl.when(i == 5)
        def _():
            relay(3, 0)
            relay(3, 1)

        pl.when(i == 6)(relay_end)

    @pl.loop(0, 3 - s)
    def _(step):
        k = 3 - step
        now = lax.rem(step + 1, 2)
        inv = iv[k][:, :1]
        factor = inv * inv * (jnp.sum(ms[...], axis=-1, keepdims=True) * (1.0 / D))
        sums = None
        for j in range(2):
            tile = jnp.concatenate(
                [
                    w[2 * k + h, j].reshape(HALF, width)
                    for h in range(2)
                    for w, width in ((wa, XY), (wz, Z))
                ],
                axis=1,
            )
            g = lax.dot_general(
                gp[now], tile, (((1,), (1,)), ((), ())), preferred_element_type=F32
            )
            cols = pl.ds(j * HALF, HALF)
            xf = xs[2 * k + j].reshape(ROWS, HALF).astype(F32)
            grad = (gr[:, cols].astype(F32) + inv * g - xf * factor).astype(BF16)
            gr[:, cols] = grad
            pre = (grad.astype(F32) * gd[k - 1, :, cols]).astype(BF16)
            gp[1 - now, :, cols] = pre
            term = lane_sums(pre.astype(F32) * ub[k - 1, :, cols].astype(F32))
            sums = term if sums is None else sums + term
        ms[...] = sums

    last_gp = lax.rem(s, 2)
    gw[c] = gp[last_gp, :, mine]
    give_g = remote(gp.at[last_gp, :, other], gw.at[c], nsend.at[1], nrecv.at[1], sib)
    give_g.start()

    remote(nw.at[1 - c], nw.at[1 - c], nsend.at[0], nrecv.at[0], sib).wait_recv()
    remote(gw.at[1 - c], gw.at[1 - c], nsend.at[1], nrecv.at[1], sib).wait_recv()

    def weight_term(v):
        @pl.loop(0, 4)
        def _(j):
            cols = pl.ds(pl.multiple_of(v * HALF + j * 256, 256), 256)
            total = None
            for half in range(2):
                part = lax.dot_general(
                    nw[half, :, cols], gw[half], (((0,), (0,)), ((), ())),
                    preferred_element_type=F32,
                )
                total = part if total is None else total + part
            xs[4 * v + j] = total.astype(BF16).reshape(4, 64, HALF)

    def grow(cc, v, i, first=0, count=4):
        if cc == 0:
            return xs.at[4 * v + i, pl.ds(first, count)]
        return xs.at[pl.ds(4 * v + first, count), i]

    def gchip(cc, v, i, part=None):
        at = (4 * v + y, i) if cc == 0 else (4 * v + i, x)
        return xs.at[at] if part is None else xs.at[at + (part,)]

    def r1_copies(cc, v):
        far = y2 if cc == 0 else x2
        to_plus, to_minus = (dyp, dym) if cc == 0 else (dxp, dxm)
        return (
            remote(grow(cc, v, far, 0, 2), r1.at[v, 0], gsend.at[0], r1r.at[v, 0], to_plus),
            remote(grow(cc, v, far, 2, 2), r1.at[v, 1], gsend.at[0], r1r.at[v, 1], to_minus),
        )

    def r2_copies(cc, v):
        plus, minus = (yp, ym) if cc == 0 else (xp, xm)
        to_plus, to_minus = (dyp, dym) if cc == 0 else (dxp, dxm)
        return (
            remote(grow(cc, v, plus), r2.at[v, 0], gsend.at[1], r2r.at[v], to_plus),
            remote(grow(cc, v, minus), r2.at[v, 1], gsend.at[1], r2r.at[v], to_minus),
        )

    def t1_copies(cc, v):
        far = x2 if cc == 0 else y2
        to_plus, to_minus = (dxp, dxm) if cc == 0 else (dyp, dym)
        return (
            remote(gchip(cc, v, far, TOP), t1.at[v, 0], gsend.at[2], t1r.at[v, 0], to_plus),
            remote(gchip(cc, v, far, BOTTOM), t1.at[v, 1], gsend.at[2], t1r.at[v, 1], to_minus),
        )

    def t2_copies(cc, v):
        plus, minus = (xp, xm) if cc == 0 else (yp, ym)
        to_plus, to_minus = (dxp, dxm) if cc == 0 else (dyp, dym)
        return (
            remote(gchip(cc, v, plus), t2.at[v, 0], gsend.at[3], t2r.at[v], to_plus),
            remote(gchip(cc, v, minus), t2.at[v, 1], gsend.at[3], t2r.at[v], to_minus),
        )

    def add_into(ref, *others):
        total = ref[...].astype(F32)
        for more in others:
            total = total + more[...].astype(F32)
        ref[...] = total.astype(BF16)

    def rs_a(v):
        def body(cc):
            for copy in r1_copies(cc, v):
                copy.start()

        by_core(body)

    def rs_b(v):
        def body(cc):
            plus, minus = (yp, ym) if cc == 0 else (xp, xm)
            arrive, leave = r1_copies(cc, v), r2_copies(cc, v)
            arrive[0].wait_recv()
            add_into(grow(cc, v, plus, 0, 2), r1.at[v, 0])
            leave[0].start()
            arrive[1].wait_recv()
            add_into(grow(cc, v, minus, 2, 2), r1.at[v, 1])
            leave[1].start()

        by_core(body)

    def rs_c(v):
        def body(cc):
            leave = t1_copies(cc, v)
            remote(r2.at[v], r2.at[v], gsend.at[1], r2r.at[v], sib).wait_recv()

            def add(i):
                add_into(gchip(cc, v, i), r2.at[v, 0, i], r2.at[v, 1, i])

            me, plus, minus, far = (x, xp, xm, x2) if cc == 0 else (y, yp, ym, y2)
            add(far)
            for copy in leave:
                copy.start()
            for i in (plus, minus, me):
                add(i)

        by_core(body)

    def rs_d(v):
        def body(cc):
            plus, minus = (xp, xm) if cc == 0 else (yp, ym)
            arrive, leave = t1_copies(cc, v), t2_copies(cc, v)
            arrive[0].wait_recv()
            add_into(gchip(cc, v, plus, TOP), t1.at[v, 0])
            leave[0].start()
            arrive[1].wait_recv()
            add_into(gchip(cc, v, minus, BOTTOM), t1.at[v, 1])
            leave[1].start()

        by_core(body)

    def rs_e(v):
        remote(t2.at[v], t2.at[v], gsend.at[3], t2r.at[v], sib).wait_recv()
        return (
            xs[4 * v + y, x].astype(F32) + t2[v, 0].astype(F32) + t2[v, 1].astype(F32)
        )

    v0, v1 = 1 - zl, zl
    weight_term(v0)
    rs_a(v0)
    weight_term(v1)
    rs_a(v1)

    def sent(block, sem):
        remote(block, block, sem, sem, sib).wait_send()

    for copy in gives(1 - c, my_rows):
        copy.wait_send()
    for way in range(2):
        sent(wa.at[pl.ds(0, 7), 0, 0, 0, TOP], rsend.at[way])
    sent(wa.at[0, :, pl.ds(0, 3)], psend.at[0])
    sent(wz.at[0, 0, 0, pl.ds(0, 3)], psend.at[1])
    sent(wa.at[pl.ds(0, 3)], qsend.at[0])
    sent(wz.at[0, 0, pl.ds(0, 3)], qsend.at[1])
    sent(wa.at[pl.ds(0, 4)], dsend.at[0])
    sent(wz.at[0, 0], dsend.at[1])
    sent(wz.at[pl.ds(0, 7), 0, pl.ds(0, 2)], usend)
    sent(wz.at[pl.ds(0, 7), 0, pl.ds(0, 2)], lsend)
    sent(wz.at[pl.ds(0, 7), :, pl.ds(0, 2)], esend)

    rs_b(v0)
    rs_b(v1)
    rs_c(v0)
    rs_c(v1)
    rs_d(v0)
    rs_d(v1)
    xs[4 * v0 + y, x] = rs_e(v0).astype(BF16)
    def cross(core):
        rows = pl.ds(pl.multiple_of(core * 32, 32), 32)
        dest = device(x, y, 2 * s + 1 - zl, core)
        return remote(xs.at[4 * v0 + y, x, rows], z1.at[c], zsend, zrecv, dest)

    cross(0).start()
    cross(1).start()
    sf[...] = rs_e(v1)
    last = remote(sf.at[sib_rows], o1, osend, orecv, sib)
    last.start()
    remote(z1, z1, zsend, zrecv, sib).wait_recv()
    out_ref[:, mine] = sf[my_rows, :] + z1[c].astype(F32)
    last.wait_recv()
    out_ref[:, other] = o1[...] + z1[1 - c].astype(F32)

    last.wait_send()
    sent(z1, zsend)
    give_g.wait_send()
    normed_copy().wait_send()
    sent(r1, gsend.at[0])
    sent(r2, gsend.at[1])
    sent(t1, gsend.at[2])
    sent(t2, gsend.at[3])


def local(inputs, weights, cotangents, lengths):
    rows = inputs.shape[0] * inputs.shape[1]
    dma = pltpu.SemaphoreType.DMA
    vmem = pl.BlockSpec(memory_space=pltpu.VMEM)
    out = pl.pallas_call(
        kernel,
        out_shape=jax.ShapeDtypeStruct((32, D), F32),
        in_specs=[
            pl.BlockSpec(memory_space=pl.ANY),
            vmem,
            pl.BlockSpec(memory_space=pl.ANY),
            pl.BlockSpec(memory_space=pl.ANY),
        ],
        out_specs=vmem,
        scratch_shapes=[
            pltpu.VMEM((8, 2, 4, 4, 64, XY), BF16),
            pltpu.VMEM((8, 2, 4, 4, 64, Z), BF16),
            pltpu.VMEM((8, 4, 64, HALF), BF16),
            pltpu.VMEM((3, ROWS, D), F32),
            pltpu.VMEM((3, ROWS, D), BF16),
            pltpu.VMEM((4, ROWS, 128), F32),
            pltpu.VMEM((2, ROWS, D), BF16),
            pltpu.VMEM((2, ROWS, D), BF16),
            pltpu.VMEM((2, ROWS, HALF), BF16),
            pltpu.VMEM((ROWS, D), BF16),
            pltpu.VMEM((ROWS, 128), F32),
            pltpu.VMEM((2, 2, 2, 64, HALF), BF16),
            pltpu.VMEM((2, 2, 4, 64, HALF), BF16),
            pltpu.VMEM((2, 2, 32, HALF), BF16),
            pltpu.VMEM((2, 2, 64, HALF), BF16),
            pltpu.VMEM((2, 32, HALF), BF16),
            pltpu.VMEM((64, HALF), F32),
            pltpu.VMEM((32, HALF), F32),
            pltpu.SMEM((2, 2), jnp.int32),
            dma((6,)),
            dma((2,)),
            dma((2,)),
            dma((2,)),
            dma((2, 4)),
            dma,
            dma((4, 2)),
            dma,
            dma((4, 2)),
            dma,
            dma((7,)),
            dma((2,)),
            dma((9, 3)),
            dma((2,)),
            dma((9, 4)),
            dma((2,)),
            dma((9,)),
            dma((2,)),
            dma((2,)),
            dma((4,)),
            dma((2, 2)),
            dma((2,)),
            dma((2, 2)),
            dma((2,)),
            dma,
            dma,
            dma,
            dma,
        ],
        compiler_params=pltpu.CompilerParams(
            collective_id=0, has_side_effects=True, vmem_limit_bytes=63 * 2**20
        ),
        cost_estimate=pl.CostEstimate(
            flops=9 * 2 * ROWS * D * D, bytes_accessed=36 * 2**20, transcendentals=4 * ROWS * D
        ),
    )(inputs.reshape(4, rows // 4, D), weights[0], cotangents.reshape(rows, D), lengths)
    return out[None]


def solution(mesh):
    in_specs = (
        P(None, "fsdp", None),
        P("section", "fsdp", None),
        P(None, "fsdp", None),
        P(None, "fsdp"),
    )
    out_specs = P("section", "fsdp", None)
    return jax.shard_map(local, mesh=mesh, in_specs=in_specs, out_specs=out_specs, check_vma=False)
```

```python
import functools

import jax
import jax.numpy as jnp
from jax import lax
from jax.experimental import pallas as pl
from jax.experimental.pallas import tpu as pltpu
from jax.sharding import PartitionSpec as P

MESH = pl.DeviceIdType.MESH
F32 = jnp.float32
BF16 = jnp.bfloat16
EPS = 1e-06
GELU_C = 0.7978845608028654
GELU_A = 0.044715

D = 2048
ROWS = 256
HALF = 1024
QUART = 512
CS = (pl.ds(0, QUART), pl.ds(QUART, QUART))
XY = 768
Z = HALF - XY
UNITS = 8
READY = ((3, 6, 7, 9), (6, 7, 8, 9), (7, 8, 9, 10), (6, 7, 9, 10))
FIRST, SECOND = pl.ds(0, 2), pl.ds(2, 2)
TOP, BOTTOM = pl.ds(0, 32), pl.ds(32, 32)


def position():
    s, f = lax.axis_index("section"), lax.axis_index("fsdp")
    c = lax.rem(f, 2)
    x = lax.rem(f // 2, 4)
    y = lax.rem(f // 8, 4)
    zl = f // 32
    return s, zl, x, y, c


def device(x, y, z, c):
    return (z // 2, lax.rem(z, 2) * 32 + y * 8 + x * 2 + c)


def remote(src, dst, send, recv, dev):
    return pltpu.make_async_remote_copy(
        src_ref=src, dst_ref=dst, send_sem=send, recv_sem=recv, device_id=dev, device_id_type=MESH
    )


def kernel(
    x_ref, w_ref, cot_ref, len_ref, out_ref,
    wa, wz, xs, gd, ub, iv, gp, nw, gw, gr, ms, r1, r2, t1, t2, u2, z1, o1,
    lens, loc, xsend, xrecv, rsend, rrecv, usend, urecv, lsend, lrecv, esend, erecv,
    psend, precv, qsend, qrecv, dsend, drecv,
    nsend, nrecv, gsend, r1r, r2r, t1r, t2r, u2r, zsend, zrecv, osend, orecv,
):
    s, zl, x, y, c = position()
    z = 2 * s + zl
    sib = device(x, y, z, 1 - c)
    xp, xm = lax.rem(x + 1, 4), lax.rem(x + 3, 4)
    yp, ym = lax.rem(y + 1, 4), lax.rem(y + 3, 4)
    x2, y2 = lax.rem(x + 2, 4), lax.rem(y + 2, 4)
    dxp, dxm = device(xp, y, z, c), device(xm, y, z, c)
    dyp, dym = device(x, yp, z, c), device(x, ym, z, c)

    barrier = pltpu.get_barrier_semaphore()
    above, below = device(x, y, lax.rem(z + 1, 8), c), device(x, y, lax.rem(z + 7, 8), c)
    pair_other = device(x, y, 2 * s + 1 - zl, 1 - c)
    def crossed(plus):
        return device(
            jnp.where(c == 0, x, xp if plus else xm), jnp.where(c == 0, yp if plus else ym, y), z, 1 - c
        )

    cross_plus, cross_minus = crossed(True), crossed(False)
    for partner in (dxp, dxm, dyp, dym, above, below, sib, pair_other, cross_plus, cross_minus):
        pl.semaphore_signal(barrier, inc=1, device_id=partner, device_id_type=MESH)

    def part(core, first, width):
        return pl.ds(pl.multiple_of(core * HALF + first, 256), width)

    in_x = [
        pltpu.make_async_copy(x_ref.at[:, :, h * HALF : (h + 1) * HALF], xs.at[h], loc.at[3 * h])
        for h in range(2)
    ]
    in_x.append(pltpu.make_async_copy(cot_ref, gr, loc.at[4]))
    in_x.append(pltpu.make_async_copy(len_ref, lens, loc.at[5]))
    for copy in in_x:
        copy.start()
    mine = pl.ds(pl.multiple_of(c * HALF, HALF), HALF)
    other = pl.ds(pl.multiple_of((1 - c) * HALF, HALF), HALF)
    my_rows = pl.ds(pl.multiple_of(c * 32, 32), 32)
    sib_rows = pl.ds(pl.multiple_of((1 - c) * 32, 32), 32)
    in_w = [
        pltpu.make_async_copy(src, dst, loc.at[1 + i])
        for i, (src, dst) in enumerate(
            (
                (w_ref.at[:, part(c, 0, XY)], wa.at[2 * s + c, zl, y, x, my_rows]),
                (w_ref.at[:, part(c, XY, Z)], wz.at[2 * s + c, zl, y, x, my_rows]),
            )
        )
    ]
    for copy in in_w:
        copy.start()
    pl.semaphore_wait(barrier, 10)

    def gives(core, rows):
        kh = 2 * s + core
        return (
            remote(
                w_ref.at[:, part(core, XY, Z)], wz.at[kh, zl, y, x, rows],
                xsend.at[0], xrecv.at[0], sib,
            ),
            remote(
                w_ref.at[:, part(core, 0, XY)], wa.at[kh, zl, y, x, rows],
                xsend.at[1], xrecv.at[1], sib,
            ),
        )

    for copy in gives(1 - c, my_rows):
        copy.start()
    for copy in in_w:
        copy.wait()
    for copy in gives(c, sib_rows):
        copy.wait_recv()

    def raw_block(d, half=None):
        v = lax.rem(z + 8 + d, 8)
        at = (2 * (v // 2) + c, lax.rem(v, 2), y, x)
        return wa.at[at] if half is None else wa.at[at + (half,)]

    def raw_up(r, half=None):
        block = raw_block(1 - r, half)
        return remote(block, block, rsend.at[0], rrecv.at[0, r - 1], above)

    def raw_down(r, half=None):
        block = raw_block(r - 1, half)
        return remote(block, block, rsend.at[1], rrecv.at[1, r - 1], below)

    def raw_landed(r):
        ups, downs = raw_block(-r, TOP if r == 4 else None), raw_block(r, BOTTOM if r == 4 else None)
        remote(ups, ups, rsend.at[0], rrecv.at[0, r - 1], above).wait_recv()
        remote(downs, downs, rsend.at[1], rrecv.at[1, r - 1], below).wait_recv()

    def raw_step(r):
        if r > 1:
            raw_landed(r - 1)
        raw_up(r, TOP if r == 4 else None).start()
        raw_down(r, BOTTOM if r == 4 else None).start()

    def row(w, cc, kh, uz, i, part=None):
        if cc == 0:
            return w.at[kh, uz, i] if part is None else w.at[kh, uz, i, part]
        return w.at[kh, uz, :, i] if part is None else w.at[kh, uz, part, i]

    def chip(w, cc, kh, uz, i, part=None):
        at = (kh, uz, y, i) if cc == 0 else (kh, uz, i, x)
        return w.at[at] if part is None else w.at[at + (part,)]

    def p_copies(w, cc, u, b):
        fam = 0 if w is wa else 1
        kh, uz = 2 * (u // 2) + cc, lax.rem(u, 2)
        me, plus, minus = (x, xp, xm) if cc == 0 else (y, yp, ym)
        to_plus, to_minus = (dxp, dxm) if cc == 0 else (dyp, dym)
        own = chip(w, cc, kh, uz, me)
        from_minus, from_plus = chip(w, cc, kh, uz, minus, TOP), chip(w, cc, kh, uz, plus, BOTTOM)
        return (
            remote(own, own, psend.at[fam], precv.at[b, 0], to_plus),
            remote(own, own, psend.at[fam], precv.at[b, 1], to_minus),
            remote(from_minus, from_minus, psend.at[fam], precv.at[b, 2], to_plus),
            remote(from_plus, from_plus, psend.at[fam], precv.at[b, 2], to_minus),
        )

    def p_landed(w, cc, u, b, i):
        kh, uz = 2 * (u // 2) + cc, lax.rem(u, 2)
        plus, minus, far = (xp, xm, x2) if cc == 0 else (yp, ym, y2)
        land = (
            chip(w, cc, kh, uz, minus),
            chip(w, cc, kh, uz, plus),
            chip(w, cc, kh, uz, far),
        )[i]
        remote(land, land, psend.at[0], precv.at[b, i], sib).wait_recv()

    def q_copies(w, cc, u, b):
        fam = 0 if w is wa else 1
        kh, uz = 2 * (u // 2) + cc, lax.rem(u, 2)
        me, plus, minus = (y, yp, ym) if cc == 0 else (x, xp, xm)
        to_plus, to_minus = (dyp, dym) if cc == 0 else (dxp, dxm)
        first, second = row(w, cc, kh, uz, me, FIRST), row(w, cc, kh, uz, me, SECOND)
        from_minus, from_plus = row(w, cc, kh, uz, minus, FIRST), row(w, cc, kh, uz, plus, SECOND)
        return (
            remote(first, first, qsend.at[fam], qrecv.at[b, 0], to_plus),
            remote(second, second, qsend.at[fam], qrecv.at[b, 1], to_minus),
            remote(second, second, qsend.at[fam], qrecv.at[b, 2], to_plus),
            remote(first, first, qsend.at[fam], qrecv.at[b, 2], to_minus),
            remote(from_minus, from_minus, qsend.at[fam], qrecv.at[b, 3], to_plus),
            remote(from_plus, from_plus, qsend.at[fam], qrecv.at[b, 3], to_minus),
        )

    def q_landed(w, cc, u, b, i):
        kh, uz = 2 * (u // 2) + cc, lax.rem(u, 2)
        plus, minus, far = (yp, ym, y2) if cc == 0 else (xp, xm, x2)
        land = (
            row(w, cc, kh, uz, minus, FIRST),
            row(w, cc, kh, uz, plus, SECOND),
            row(w, cc, kh, uz, far),
            row(w, cc, kh, uz, far),
        )[i]
        remote(land, land, qsend.at[0], qrecv.at[b, i], sib).wait_recv()

    def d_copy(w, cc, u, b, i):
        kh, uz = 2 * (u // 2) + cc, lax.rem(u, 2)
        at = ((y, ym, yp, y2) if cc == 0 else (x, xm, xp, x2))[i]
        block = row(w, cc, kh, uz, at)
        return remote(block, block, dsend.at[0 if w is wa else 1], drecv.at[b], sib)

    def by_core(body):
        for cc in (0, 1):
            pl.when(c == cc)(functools.partial(body, cc))

    def unit(t):
        rest = t - 2
        near = jnp.where(rest < 2, rest + 2, jnp.where(rest < 4, rest - 2, rest + 2))
        rest = jnp.where(s == 2, near, jnp.where(rest < 2 * s, rest, rest + 2))
        return jnp.where(t == 0, z, jnp.where(t == 1, 2 * s + 1 - zl, rest))

    def stage_p1(w, u, b):
        def body(cc):
            copies = p_copies(w, cc, u, b)
            copies[0].start()
            copies[1].start()

        by_core(body)

    def stage_p2(w, u, b):
        def body(cc):
            copies = p_copies(w, cc, u, b)
            p_landed(w, cc, u, b, 0)
            copies[2].start()
            p_landed(w, cc, u, b, 1)
            copies[3].start()

        by_core(body)

    def stage_q1(w, u, b):
        def body(cc):
            copies = q_copies(w, cc, u, b)
            p_landed(w, cc, u, b, 2)
            for copy in copies[:4]:
                copy.start()
            d_copy(w, cc, u, b, 0).start()

        by_core(body)

    def stage_q2(w, u, b):
        def body(cc):
            copies = q_copies(w, cc, u, b)
            q_landed(w, cc, u, b, 0)
            copies[4].start()
            q_landed(w, cc, u, b, 1)
            copies[5].start()

        by_core(body)

    def stage_f(w, u, b):
        def body(cc):
            q_landed(w, cc, u, b, 2)
            d_copy(w, cc, u, b, 1).start()
            d_copy(w, cc, u, b, 2).start()
            q_landed(w, cc, u, b, 3)
            d_copy(w, cc, u, b, 3).start()

        by_core(body)

    PARTS = (pl.ds(0, 2), pl.ds(2, 2))
    def plane(d, part, core=None):
        v = lax.rem(z + 8 + d, 8)
        core = c if core is None else core
        return wz.at[2 * (v // 2) + core, lax.rem(v, 2), PARTS[part]]

    def up(r, part):
        block = plane(1 - r, part)
        return remote(block, block, usend, urecv.at[r - 1, part], above)

    def down(r, part):
        block = plane(r - 1, part)
        return remote(block, block, lsend, lrecv.at[r - 1, part], below)

    def up_landed(r, part):
        block = plane(-r, part)
        remote(block, block, usend, urecv.at[r - 1, part], above).wait_recv()

    def down_landed(r, part):
        block = plane(r, part)
        remote(block, block, lsend, lrecv.at[r - 1, part], below).wait_recv()

    def e_copy(slot, part):
        d = (-1, -2, -3, 1, 2, 3, 4)[slot]
        block = plane(d, part)
        return remote(block, block, esend, erecv.at[slot], sib)

    def relay(r, part):
        up_landed(r, part)
        if r < 3 or part == 0:
            up(r + 1, part).start()
        down_landed(r, part)
        if r < 3 or part == 1:
            down(r + 1, part).start()
        e_copy(r - 1, part).start()
        e_copy(r + 2, part).start()

    def relay_end():
        up_landed(4, 0)
        e_copy(6, 0).start()
        down_landed(4, 1)
        e_copy(6, 1).start()

    def normed_copy():
        return remote(nw.at[c], nw.at[c], nsend.at[0], nrecv.at[0], sib)

    def section_rows(k, i):
        at = pl.ds(pl.multiple_of(lax.rem(i, 2) * 32, 32), 32)
        halves = [xs[2 * k + h, i // 2, at, :].astype(F32) for h in range(2)]
        return jnp.concatenate(halves, axis=1)

    def lane_sums(v):
        total = v[:, :128]
        for i in range(1, HALF // 128):
            total = total + v[:, i * 128 : (i + 1) * 128]
        return total

    def forward(k):
        @pl.loop(0, 2)
        def _(uz):
            u = 2 * k + uz

            block = wa.at[2 * k + 1 - c, uz]
            remote(block, block, dsend.at[0], drecv.at[u], sib).wait_recv()
            z_block = wz.at[2 * k + 1 - c, uz]

            @pl.when(u == z)
            def _():
                remote(z_block, z_block, dsend.at[1], drecv.at[UNITS], sib).wait_recv()

            @pl.when(u != z)
            def _():
                d = lax.rem(u - z + 8, 8)
                slot = jnp.where(d < 4, 2 + d, jnp.where(d == 4, 6, 7 - d))
                remote(z_block, z_block, esend, erecv.at[slot], sib).wait_recv()

        @pl.loop(0, ROWS // 32)
        def _(i):
            rows = pl.ds(pl.multiple_of(i * 32, 32), 32)
            xf = section_rows(k, i)
            inv = lax.rsqrt(jnp.mean(xf * xf, axis=-1, keepdims=True) + EPS)
            iv[k, rows, :] = jnp.broadcast_to(inv, (32, 128))
            gp[0, rows, :] = (xf * inv).astype(BF16)

        @pl.when(k == s)
        def _():
            nw[c] = gp[0]
            normed_copy().start()

        @pl.loop(0, 2)
        def _(h):
            cols = part(h, 0, HALF)
            w = jnp.concatenate(
                [wa[2 * k + h].reshape(D, XY), wz[2 * k + h].reshape(D, Z)], axis=1
            )
            u = jnp.dot(gp[0], w, preferred_element_type=F32)
            uu = u * u
            t = jnp.tanh((GELU_C * u) * (1.0 + GELU_A * uu))
            cdf = 0.5 * (1.0 + t)
            slope = cdf + (0.5 * GELU_C) * u * (1.0 - t * t) * (1.0 + (3.0 * GELU_A) * uu)

            @pl.when(k < 3)
            def _():
                at = jnp.minimum(k, 2)
                gd[at, :, cols] = slope
                ub[at, :, cols] = u.astype(BF16)
                before = xs[2 * k + h].reshape(ROWS, HALF)
                after = (before.astype(F32) + u * cdf).astype(BF16)
                xs[2 * at + 2 + h] = after.reshape(4, 64, HALF)

            @pl.when(k == 3)
            def _():
                pre = (gr[:, cols].astype(F32) * slope).astype(BF16)
                gp[1, :, cols] = pre
                term = lane_sums(pre.astype(F32) * u)
                ms[...] = jnp.where(h == 0, term, ms[...] + term)

    own = unit(0)
    stage_p1(wz, own, UNITS)
    stage_p1(wa, own, own)
    raw_step(1)
    stage_p2(wz, own, UNITS)
    stage_p2(wa, own, own)
    raw_step(2)
    stage_q1(wz, own, UNITS)
    stage_q1(wa, own, own)
    for copy in in_x:
        copy.wait()
    for m in range(2):
        for q in range(2):
            rows = pl.ds(128 * m + 64 * q, 64)
            live = lax.broadcasted_iota(jnp.int32, (64, D), 0) < lens[m, q]
            gr[rows, :] = jnp.where(live, gr[rows, :].astype(F32), 0.0).astype(BF16)
    near = unit(1)
    stage_p1(wa, near, near)
    raw_step(3)
    stage_q2(wz, own, UNITS)
    stage_p2(wa, near, near)
    stage_q2(wa, own, own)
    stage_f(wz, own, UNITS)
    for i in range(2):
        up(1, i).start()
        down(1, i).start()
    raw_step(4)
    third = unit(2)
    stage_p1(wa, third, third)

    @pl.loop(1, UNITS + 3)
    def _(i):
        def when_unit(ahead, stage):
            @pl.when((i + ahead >= 0) & (i + ahead < UNITS))
            def _():
                u = unit(i + ahead)
                stage(wa, u, u)

        when_unit(0, stage_q1)
        pl.when(i == 2)(lambda: raw_landed(4))
        when_unit(2, stage_p1)
        when_unit(1, stage_p2)
        k = -1
        for section in range(4):
            for number in range(4):
                k = jnp.where((s == section) & (i == READY[section][number]), number, k)
        pl.when(k >= 0)(lambda: forward(jnp.maximum(k, 0)))
        when_unit(0, stage_q2)
        when_unit(-1, stage_f)
        pl.when(i == 1)(lambda: relay(1, 0))
        pl.when(i == 2)(lambda: relay(1, 1))
        pl.when(i == 3)(lambda: relay(2, 0))
        pl.when(i == 4)(lambda: relay(2, 1))

        @pl.when(i == 5)
        def _():
            relay(3, 0)
            relay(3, 1)

        pl.when(i == 6)(relay_end)

    @pl.loop(0, 3 - s)
    def _(step):
        k = 3 - step
        now = lax.rem(step + 1, 2)
        inv = iv[k][:, :1]
        factor = inv * inv * (jnp.sum(ms[...], axis=-1, keepdims=True) * (1.0 / D))
        sums = None
        for j in range(2):
            tile = jnp.concatenate(
                [
                    w[2 * k + h, j].reshape(HALF, width)
                    for h in range(2)
                    for w, width in ((wa, XY), (wz, Z))
                ],
                axis=1,
            )
            g = lax.dot_general(
                gp[now], tile, (((1,), (1,)), ((), ())), preferred_element_type=F32
            )
            cols = pl.ds(j * HALF, HALF)
            xf = xs[2 * k + j].reshape(ROWS, HALF).astype(F32)
            grad = (gr[:, cols].astype(F32) + inv * g - xf * factor).astype(BF16)
            gr[:, cols] = grad
            pre = (grad.astype(F32) * gd[k - 1, :, cols]).astype(BF16)
            gp[1 - now, :, cols] = pre
            term = lane_sums(pre.astype(F32) * ub[k - 1, :, cols].astype(F32))
            sums = term if sums is None else sums + term
        ms[...] = sums

    last_gp = lax.rem(s, 2)
    def column_part(core, hc):
        return part(core, hc * QUART, QUART)

    def give_g(hc):
        return remote(
            gp.at[last_gp, :, column_part(1 - c, hc)], gw.at[c, :, CS[hc]],
            nsend.at[1 + hc], nrecv.at[1 + hc], sib,
        )

    for hc in range(2):
        give_g(hc).start()
    for hc in range(2):
        gw[c, :, CS[hc]] = gp[last_gp, :, column_part(c, hc)]
    remote(nw.at[1 - c], nw.at[1 - c], nsend.at[0], nrecv.at[0], sib).wait_recv()

    v0, v1 = 1 - zl, zl
    v_of = (v0, v0, v1, v1)

    def weight_term(q):
        v, cs = v_of[q], CS[q % 2]

        @pl.loop(0, 2)
        def _(j):
            rows = pl.ds(pl.multiple_of(v * HALF + j * 512, 512), 512)
            left = nw[:, :, rows].reshape(2 * ROWS, 512)
            right = gw[:, :, cs].reshape(2 * ROWS, QUART)
            total = lax.dot_general(
                left, right, (((0,), (0,)), ((), ())), preferred_element_type=F32
            )
            xs[pl.ds(4 * v + 2 * j, 2), :, :, cs] = total.astype(BF16).reshape(2, 4, 64, QUART)

    def grow(cc, q, i, first=0, count=4):
        v, cs = v_of[q], CS[q % 2]
        if cc == 0:
            return xs.at[4 * v + i, pl.ds(first, count), :, cs]
        return xs.at[pl.ds(4 * v + first, count), i, :, cs]

    def gchip(cc, q, i, rows=None):
        v, cs = v_of[q], CS[q % 2]
        rows = pl.ds(0, 64) if rows is None else rows
        return xs.at[4 * v + y, i, rows, cs] if cc == 0 else xs.at[4 * v + i, x, rows, cs]

    def q_axis(cc):
        return (y, yp, ym, y2, dyp, dym) if cc == 0 else (x, xp, xm, x2, dxp, dxm)

    def p_axis(cc):
        return (x, xp, xm, x2, dxp, dxm) if cc == 0 else (y, yp, ym, y2, dyp, dym)

    def r1_copies(cc, q):
        _, _, _, far, to_plus, to_minus = q_axis(cc)
        return (
            remote(grow(cc, q, far, 0, 2), r1.at[q, 0], gsend.at[0], r1r.at[q, 0], to_plus),
            remote(grow(cc, q, far, 2, 2), r1.at[q, 1], gsend.at[0], r1r.at[q, 1], to_minus),
        )

    def r2_copies(cc, q):
        _, plus, minus, _, to_plus, to_minus = q_axis(cc)
        return (
            remote(grow(cc, q, plus), r2.at[q, 0], gsend.at[1], r2r.at[q], to_plus),
            remote(grow(cc, q, minus), r2.at[q, 1], gsend.at[1], r2r.at[q], to_minus),
        )

    def t1_copies(cc, q):
        _, _, _, far, to_plus, to_minus = p_axis(cc)
        return (
            remote(gchip(cc, q, far, TOP), t1.at[q, 0], gsend.at[2], t1r.at[q, 0], to_plus),
            remote(gchip(cc, q, far, BOTTOM), t1.at[q, 1], gsend.at[2], t1r.at[q, 1], to_minus),
        )

    def t2_copies(cc, q, way):
        _, plus, minus, _, to_plus, to_minus = p_axis(cc)
        block, dest = ((plus, to_plus), (minus, to_minus))[way]
        if q < 2:
            return [
                remote(gchip(cc, q, block), t2.at[q, way], gsend.at[3], t2r.at[q], dest)
            ]
        at = (block, y) if cc == 0 else (x, block)
        return [
            remote(
                gchip(cc, q, block, (TOP, BOTTOM)[core]), u2.at[q - 2, cc, way],
                gsend.at[4], u2r.at[q - 2], device(*at, z, core),
            )
            for core in range(2)
        ]

    def add_into(ref, *others):
        total = ref[...].astype(F32)
        for more in others:
            total = total + more[...].astype(F32)
        ref[...] = total.astype(BF16)

    def rs_a(q):
        def body(cc):
            for copy in r1_copies(cc, q):
                copy.start()

        by_core(body)

    def rs_b(q):
        def body(cc):
            _, plus, minus, _, _, _ = q_axis(cc)
            arrive, leave = r1_copies(cc, q), r2_copies(cc, q)
            arrive[0].wait_recv()
            add_into(grow(cc, q, plus, 0, 2), r1.at[q, 0])
            leave[0].start()
            arrive[1].wait_recv()
            add_into(grow(cc, q, minus, 2, 2), r1.at[q, 1])
            leave[1].start()

        by_core(body)

    def own_part(q):
        block = xs.at[4 * v_of[q] + y, x, sib_rows, CS[q % 2]]
        return remote(block, o1.at[q - 2], osend, orecv.at[q - 2], sib)

    def rs_c(q):
        def body(cc):
            me, plus, minus, far, _, _ = p_axis(cc)
            remote(r2.at[q], r2.at[q], gsend.at[1], r2r.at[q], sib).wait_recv()

            def add(i):
                add_into(gchip(cc, q, i), r2.at[q, 0, i], r2.at[q, 1, i])

            add(far)
            for copy in t1_copies(cc, q):
                copy.start()
            add(plus)
            add(minus)
            add(me)
            if q >= 2:
                own_part(q).start()

        by_core(body)

    def rs_d(q):
        def body(cc):
            _, plus, minus, _, _, _ = p_axis(cc)
            arrive = t1_copies(cc, q)
            arrive[0].wait_recv()
            add_into(gchip(cc, q, plus, TOP), t1.at[q, 0])
            for copy in t2_copies(cc, q, 0):
                copy.start()
            arrive[1].wait_recv()
            add_into(gchip(cc, q, minus, BOTTOM), t1.at[q, 1])
            for copy in t2_copies(cc, q, 1):
                copy.start()

        by_core(body)

    def cross(q, core):
        rows = (TOP, BOTTOM)[core]
        block = xs.at[4 * v0 + y, x, rows, CS[q]]
        dest = device(x, y, 2 * s + 1 - zl, core)
        return remote(block, z1.at[c, :, CS[q]], zsend, zrecv, dest)

    def rs_e(q):
        remote(t2.at[q], t2.at[q], gsend.at[3], t2r.at[q], sib).wait_recv()
        add_into(xs.at[4 * v0 + y, x, :, CS[q]], t2.at[q, 0], t2.at[q, 1])
        cross(q, 0).start()
        cross(q, 1).start()

    def finish(q):
        hc = q - 2
        remote(o1.at[hc], o1.at[hc], osend, orecv.at[hc], sib).wait_recv()
        remote(u2.at[hc], u2.at[hc], gsend.at[4], u2r.at[hc], sib).wait_recv()
        for core, own_ in ((c, xs[4 * v1 + y, x, my_rows, CS[hc]]), (1 - c, o1[hc])):
            total = own_.astype(F32) + z1[core, :, CS[hc]].astype(F32)
            for way in range(2):
                total = total + u2[hc, core, way].astype(F32)
            out_ref[:, column_part(core, hc)] = total

    for q in range(4):
        if q < 2:
            got = gw.at[1 - c, :, CS[q]]
            remote(got, got, nsend.at[1 + q], nrecv.at[1 + q], sib).wait_recv()
        weight_term(q)
        rs_a(q)

    def sent(block, sem):
        remote(block, block, sem, sem, sib).wait_send()

    for copy in gives(1 - c, my_rows):
        copy.wait_send()
    for way in range(2):
        sent(wa.at[pl.ds(0, 7), 0, 0, 0, TOP], rsend.at[way])
    sent(wa.at[0, :, pl.ds(0, 3)], psend.at[0])
    sent(wz.at[0, 0, 0, pl.ds(0, 3)], psend.at[1])
    sent(wa.at[pl.ds(0, 3)], qsend.at[0])
    sent(wz.at[0, 0, pl.ds(0, 3)], qsend.at[1])
    sent(wa.at[pl.ds(0, 4)], dsend.at[0])
    sent(wz.at[0, 0], dsend.at[1])
    sent(wz.at[pl.ds(0, 7), 0, pl.ds(0, 2)], usend)
    sent(wz.at[pl.ds(0, 7), 0, pl.ds(0, 2)], lsend)
    sent(wz.at[pl.ds(0, 7), :, pl.ds(0, 2)], esend)

    for q in range(4):
        rs_b(q)
    rs_c(0)
    rs_c(1)
    rs_d(0)
    rs_c(2)
    rs_d(1)
    rs_e(0)
    rs_c(3)
    rs_d(2)
    rs_e(1)
    rs_d(3)
    remote(z1, z1, zsend, zrecv, sib).wait_recv()
    finish(2)
    finish(3)

    sent(o1, osend)
    sent(z1, zsend)
    give_g(0).wait_send()
    give_g(1).wait_send()
    normed_copy().wait_send()
    sent(r1, gsend.at[0])
    sent(r2, gsend.at[1])
    sent(t1, gsend.at[2])
    sent(t2, gsend.at[3])
    sent(u2, gsend.at[4])


def local(inputs, weights, cotangents, lengths):
    rows = inputs.shape[0] * inputs.shape[1]
    dma = pltpu.SemaphoreType.DMA
    vmem = pl.BlockSpec(memory_space=pltpu.VMEM)
    out = pl.pallas_call(
        kernel,
        out_shape=jax.ShapeDtypeStruct((32, D), F32),
        in_specs=[
            pl.BlockSpec(memory_space=pl.ANY),
            vmem,
            pl.BlockSpec(memory_space=pl.ANY),
            pl.BlockSpec(memory_space=pl.ANY),
        ],
        out_specs=vmem,
        scratch_shapes=[
            pltpu.VMEM((8, 2, 4, 4, 64, XY), BF16),
            pltpu.VMEM((8, 2, 4, 4, 64, Z), BF16),
            pltpu.VMEM((8, 4, 64, HALF), BF16),
            pltpu.VMEM((3, ROWS, D), F32),
            pltpu.VMEM((3, ROWS, D), BF16),
            pltpu.VMEM((4, ROWS, 128), F32),
            pltpu.VMEM((2, ROWS, D), BF16),
            pltpu.VMEM((2, ROWS, D), BF16),
            pltpu.VMEM((2, ROWS, HALF), BF16),
            pltpu.VMEM((ROWS, D), BF16),
            pltpu.VMEM((ROWS, 128), F32),
            pltpu.VMEM((4, 2, 2, 64, QUART), BF16),
            pltpu.VMEM((4, 2, 4, 64, QUART), BF16),
            pltpu.VMEM((4, 2, 32, QUART), BF16),
            pltpu.VMEM((2, 2, 64, QUART), BF16),
            pltpu.VMEM((2, 2, 2, 32, QUART), BF16),
            pltpu.VMEM((2, 32, HALF), BF16),
            pltpu.VMEM((2, 32, QUART), BF16),
            pltpu.SMEM((2, 2), jnp.int32),
            dma((6,)),
            dma((2,)),
            dma((2,)),
            dma((2,)),
            dma((2, 4)),
            dma,
            dma((4, 2)),
            dma,
            dma((4, 2)),
            dma,
            dma((7,)),
            dma((2,)),
            dma((9, 3)),
            dma((2,)),
            dma((9, 4)),
            dma((2,)),
            dma((9,)),
            dma((3,)),
            dma((3,)),
            dma((5,)),
            dma((4, 2)),
            dma((4,)),
            dma((4, 2)),
            dma((2,)),
            dma((2,)),
            dma,
            dma,
            dma,
            dma((2,)),
        ],
        compiler_params=pltpu.CompilerParams(
            collective_id=0, has_side_effects=True, vmem_limit_bytes=63 * 2**20
        ),
        cost_estimate=pl.CostEstimate(
            flops=9 * 2 * ROWS * D * D, bytes_accessed=36 * 2**20, transcendentals=4 * ROWS * D
        ),
    )(inputs.reshape(4, rows // 4, D), weights[0], cotangents.reshape(rows, D), lengths)
    return out[None]


def solution(mesh):
    in_specs = (
        P(None, "fsdp", None),
        P("section", "fsdp", None),
        P(None, "fsdp", None),
        P(None, "fsdp"),
    )
    out_specs = P("section", "fsdp", None)
    return jax.shard_map(local, mesh=mesh, in_specs=in_specs, out_specs=out_specs, check_vma=False)
```

```python
import functools

import jax
import jax.numpy as jnp
from jax import lax
from jax.experimental import pallas as pl
from jax.experimental.pallas import tpu as pltpu
from jax.sharding import PartitionSpec as P

MESH = pl.DeviceIdType.MESH
F32 = jnp.float32
BF16 = jnp.bfloat16
EPS = 1e-06
GELU_C = 0.7978845608028654
GELU_A = 0.044715

D = 2048
ROWS = 256
HALF = 1024
QUART = 512
CS = (pl.ds(0, QUART), pl.ds(QUART, QUART))
XY = 768
Z = HALF - XY
UNITS = 8
READY = ((4, 6, 8), (6, 7, 8), (8, 9), (6, 8))
FIRST, SECOND = pl.ds(0, 2), pl.ds(2, 2)
TOP, BOTTOM = pl.ds(0, 32), pl.ds(32, 32)


def position():
    s, f = lax.axis_index("section"), lax.axis_index("fsdp")
    c = lax.rem(f, 2)
    x = lax.rem(f // 2, 4)
    y = lax.rem(f // 8, 4)
    zl = f // 32
    return s, zl, x, y, c


def device(x, y, z, c):
    return (z // 2, lax.rem(z, 2) * 32 + y * 8 + x * 2 + c)


def remote(src, dst, send, recv, dev):
    return pltpu.make_async_remote_copy(
        src_ref=src, dst_ref=dst, send_sem=send, recv_sem=recv, device_id=dev, device_id_type=MESH
    )


def kernel(
    x_ref, w_ref, cot_ref, len_ref, out_ref,
    wa, wz, xs, gd, ub, iv, gp, nw, gw, gr, ms, r1, r2, t1, t2, u2, z1, o1,
    lens, loc, xsend, xrecv, rsend, rrecv, usend, urecv, lsend, lrecv, esend, erecv,
    psend, precv, qsend, qrecv, dsend, drecv,
    nsend, nrecv, gsend, r1r, r2r, t1r, t2r, u2r, zsend, zrecv, osend, orecv,
):
    s, zl, x, y, c = position()
    z = 2 * s + zl
    sib = device(x, y, z, 1 - c)
    xp, xm = lax.rem(x + 1, 4), lax.rem(x + 3, 4)
    yp, ym = lax.rem(y + 1, 4), lax.rem(y + 3, 4)
    x2, y2 = lax.rem(x + 2, 4), lax.rem(y + 2, 4)
    dxp, dxm = device(xp, y, z, c), device(xm, y, z, c)
    dyp, dym = device(x, yp, z, c), device(x, ym, z, c)

    barrier = pltpu.get_barrier_semaphore()
    above, below = device(x, y, lax.rem(z + 1, 8), c), device(x, y, lax.rem(z + 7, 8), c)
    pair_other = device(x, y, 2 * s + 1 - zl, 1 - c)
    def crossed(plus):
        return device(
            jnp.where(c == 0, x, xp if plus else xm), jnp.where(c == 0, yp if plus else ym, y), z, 1 - c
        )

    cross_plus, cross_minus = crossed(True), crossed(False)
    for partner in (dxp, dxm, dyp, dym, above, below, sib, pair_other, cross_plus, cross_minus):
        pl.semaphore_signal(barrier, inc=1, device_id=partner, device_id_type=MESH)

    def part(core, first, width):
        return pl.ds(pl.multiple_of(core * HALF + first, 256), width)

    in_x = [
        pltpu.make_async_copy(x_ref.at[:, :, h * HALF : (h + 1) * HALF], xs.at[h], loc.at[3 * h])
        for h in range(2)
    ]
    in_x.append(pltpu.make_async_copy(cot_ref, gr, loc.at[4]))
    in_x.append(pltpu.make_async_copy(len_ref, lens, loc.at[5]))
    for copy in in_x:
        copy.start()
    mine = pl.ds(pl.multiple_of(c * HALF, HALF), HALF)
    other = pl.ds(pl.multiple_of((1 - c) * HALF, HALF), HALF)
    my_rows = pl.ds(pl.multiple_of(c * 32, 32), 32)
    sib_rows = pl.ds(pl.multiple_of((1 - c) * 32, 32), 32)
    in_w = [
        pltpu.make_async_copy(src, dst, loc.at[1 + i])
        for i, (src, dst) in enumerate(
            (
                (w_ref.at[:, part(c, 0, XY)], wa.at[2 * s + c, zl, y, x, my_rows]),
                (w_ref.at[:, part(c, XY, Z)], wz.at[2 * s + c, zl, y, x, my_rows]),
            )
        )
    ]
    for copy in in_w:
        copy.start()
    pl.semaphore_wait(barrier, 10)

    def gives(core, rows):
        kh = 2 * s + core
        return (
            remote(
                w_ref.at[:, part(core, XY, Z)], wz.at[kh, zl, y, x, rows],
                xsend.at[0], xrecv.at[0], sib,
            ),
            remote(
                w_ref.at[:, part(core, 0, XY)], wa.at[kh, zl, y, x, rows],
                xsend.at[1], xrecv.at[1], sib,
            ),
        )

    for copy in gives(1 - c, my_rows):
        copy.start()
    for copy in in_w:
        copy.wait()
    for copy in gives(c, sib_rows):
        copy.wait_recv()

    def raw_block(d, half=None):
        v = lax.rem(z + 8 + d, 8)
        at = (2 * (v // 2) + c, lax.rem(v, 2), y, x)
        return wa.at[at] if half is None else wa.at[at + (half,)]

    def raw_up(r, half=None):
        block = raw_block(1 - r, half)
        return remote(block, block, rsend.at[0], rrecv.at[0, r - 1], above)

    def raw_down(r, half=None):
        block = raw_block(r - 1, half)
        return remote(block, block, rsend.at[1], rrecv.at[1, r - 1], below)

    def raw_landed(r):
        ups, downs = raw_block(-r, TOP if r == 4 else None), raw_block(r, BOTTOM if r == 4 else None)
        remote(ups, ups, rsend.at[0], rrecv.at[0, r - 1], above).wait_recv()
        remote(downs, downs, rsend.at[1], rrecv.at[1, r - 1], below).wait_recv()

    def raw_step(r):
        if r > 1:
            raw_landed(r - 1)
        raw_up(r, TOP if r == 4 else None).start()
        raw_down(r, BOTTOM if r == 4 else None).start()

    def row(w, cc, kh, uz, i, part=None):
        if cc == 0:
            return w.at[kh, uz, i] if part is None else w.at[kh, uz, i, part]
        return w.at[kh, uz, :, i] if part is None else w.at[kh, uz, part, i]

    def chip(w, cc, kh, uz, i, part=None):
        at = (kh, uz, y, i) if cc == 0 else (kh, uz, i, x)
        return w.at[at] if part is None else w.at[at + (part,)]

    def p_copies(w, cc, u, b):
        fam = 0 if w is wa else 1
        kh, uz = 2 * (u // 2) + cc, lax.rem(u, 2)
        me, plus, minus = (x, xp, xm) if cc == 0 else (y, yp, ym)
        to_plus, to_minus = (dxp, dxm) if cc == 0 else (dyp, dym)
        own = chip(w, cc, kh, uz, me)
        from_minus, from_plus = chip(w, cc, kh, uz, minus, TOP), chip(w, cc, kh, uz, plus, BOTTOM)
        return (
            remote(own, own, psend.at[fam], precv.at[b, 0], to_plus),
            remote(own, own, psend.at[fam], precv.at[b, 1], to_minus),
            remote(from_minus, from_minus, psend.at[fam], precv.at[b, 2], to_plus),
            remote(from_plus, from_plus, psend.at[fam], precv.at[b, 2], to_minus),
        )

    def p_landed(w, cc, u, b, i):
        kh, uz = 2 * (u // 2) + cc, lax.rem(u, 2)
        plus, minus, far = (xp, xm, x2) if cc == 0 else (yp, ym, y2)
        land = (
            chip(w, cc, kh, uz, minus),
            chip(w, cc, kh, uz, plus),
            chip(w, cc, kh, uz, far),
        )[i]
        remote(land, land, psend.at[0], precv.at[b, i], sib).wait_recv()

    def q_copies(w, cc, u, b):
        fam = 0 if w is wa else 1
        kh, uz = 2 * (u // 2) + cc, lax.rem(u, 2)
        me, plus, minus = (y, yp, ym) if cc == 0 else (x, xp, xm)
        to_plus, to_minus = (dyp, dym) if cc == 0 else (dxp, dxm)
        first, second = row(w, cc, kh, uz, me, FIRST), row(w, cc, kh, uz, me, SECOND)
        from_minus, from_plus = row(w, cc, kh, uz, minus, FIRST), row(w, cc, kh, uz, plus, SECOND)
        return (
            remote(first, first, qsend.at[fam], qrecv.at[b, 0], to_plus),
            remote(second, second, qsend.at[fam], qrecv.at[b, 1], to_minus),
            remote(second, second, qsend.at[fam], qrecv.at[b, 2], to_plus),
            remote(first, first, qsend.at[fam], qrecv.at[b, 2], to_minus),
            remote(from_minus, from_minus, qsend.at[fam], qrecv.at[b, 3], to_plus),
            remote(from_plus, from_plus, qsend.at[fam], qrecv.at[b, 3], to_minus),
        )

    def q_landed(w, cc, u, b, i):
        kh, uz = 2 * (u // 2) + cc, lax.rem(u, 2)
        plus, minus, far = (yp, ym, y2) if cc == 0 else (xp, xm, x2)
        land = (
            row(w, cc, kh, uz, minus, FIRST),
            row(w, cc, kh, uz, plus, SECOND),
            row(w, cc, kh, uz, far),
            row(w, cc, kh, uz, far),
        )[i]
        remote(land, land, qsend.at[0], qrecv.at[b, i], sib).wait_recv()

    def d_copy(w, cc, u, b, i):
        kh, uz = 2 * (u // 2) + cc, lax.rem(u, 2)
        at = ((y, ym, yp, y2) if cc == 0 else (x, xm, xp, x2))[i]
        block = row(w, cc, kh, uz, at)
        return remote(block, block, dsend.at[0 if w is wa else 1], drecv.at[b], sib)

    def by_core(body):
        for cc in (0, 1):
            pl.when(c == cc)(functools.partial(body, cc))

    def unit(t):
        rest = t - 2
        near = jnp.where(rest < 2, rest + 2, jnp.where(rest < 4, rest - 2, rest + 2))
        rest = jnp.where(s == 2, near, jnp.where(rest < 2 * s, rest, rest + 2))
        return jnp.where(t == 0, z, jnp.where(t == 1, 2 * s + 1 - zl, rest))

    def stage_p1(w, u, b):
        def body(cc):
            copies = p_copies(w, cc, u, b)
            copies[0].start()
            copies[1].start()

        by_core(body)

    def stage_p2(w, u, b):
        def body(cc):
            copies = p_copies(w, cc, u, b)
            p_landed(w, cc, u, b, 0)
            copies[2].start()
            p_landed(w, cc, u, b, 1)
            copies[3].start()

        by_core(body)

    def stage_q1(w, u, b):
        def body(cc):
            copies = q_copies(w, cc, u, b)
            p_landed(w, cc, u, b, 2)
            for copy in copies[:4]:
                copy.start()
            d_copy(w, cc, u, b, 0).start()

        by_core(body)

    def stage_q2(w, u, b):
        def body(cc):
            copies = q_copies(w, cc, u, b)
            q_landed(w, cc, u, b, 0)
            copies[4].start()
            q_landed(w, cc, u, b, 1)
            copies[5].start()

        by_core(body)

    def stage_f(w, u, b):
        def body(cc):
            q_landed(w, cc, u, b, 2)
            d_copy(w, cc, u, b, 1).start()
            d_copy(w, cc, u, b, 2).start()
            q_landed(w, cc, u, b, 3)
            d_copy(w, cc, u, b, 3).start()

        by_core(body)

    PARTS = (pl.ds(0, 2), pl.ds(2, 2))
    def plane(d, part, core=None):
        v = lax.rem(z + 8 + d, 8)
        core = c if core is None else core
        return wz.at[2 * (v // 2) + core, lax.rem(v, 2), PARTS[part]]

    def up(r, part):
        block = plane(1 - r, part)
        return remote(block, block, usend, urecv.at[r - 1, part], above)

    def down(r, part):
        block = plane(r - 1, part)
        return remote(block, block, lsend, lrecv.at[r - 1, part], below)

    def up_landed(r, part):
        block = plane(-r, part)
        remote(block, block, usend, urecv.at[r - 1, part], above).wait_recv()

    def down_landed(r, part):
        block = plane(r, part)
        remote(block, block, lsend, lrecv.at[r - 1, part], below).wait_recv()

    def e_copy(slot, part):
        d = (-1, -2, -3, 1, 2, 3, 4)[slot]
        block = plane(d, part)
        return remote(block, block, esend, erecv.at[slot], sib)

    def relay(r, part):
        up_landed(r, part)
        if r < 3 or part == 0:
            up(r + 1, part).start()
        down_landed(r, part)
        if r < 3 or part == 1:
            down(r + 1, part).start()
        e_copy(r - 1, part).start()
        e_copy(r + 2, part).start()

    def relay_end():
        up_landed(4, 0)
        e_copy(6, 0).start()
        down_landed(4, 1)
        e_copy(6, 1).start()

    def normed_copy():
        return remote(nw.at[c], nw.at[c], nsend.at[0], nrecv.at[0], sib)

    def section_rows(k, i):
        at = pl.ds(pl.multiple_of(lax.rem(i, 2) * 32, 32), 32)
        halves = [xs[2 * k + h, i // 2, at, :].astype(F32) for h in range(2)]
        return jnp.concatenate(halves, axis=1)

    def lane_sums(v):
        total = v[:, :128]
        for i in range(1, HALF // 128):
            total = total + v[:, i * 128 : (i + 1) * 128]
        return total

    def forward(k):
        @pl.loop(0, 2)
        def _(uz):
            u = 2 * k + uz

            block = wa.at[2 * k + 1 - c, uz]
            remote(block, block, dsend.at[0], drecv.at[u], sib).wait_recv()
            z_block = wz.at[2 * k + 1 - c, uz]

            @pl.when(u == z)
            def _():
                remote(z_block, z_block, dsend.at[1], drecv.at[UNITS], sib).wait_recv()

            @pl.when(u != z)
            def _():
                d = lax.rem(u - z + 8, 8)
                slot = jnp.where(d < 4, 2 + d, jnp.where(d == 4, 6, 7 - d))
                remote(z_block, z_block, esend, erecv.at[slot], sib).wait_recv()

        @pl.loop(0, ROWS // 32)
        def _(i):
            rows = pl.ds(pl.multiple_of(i * 32, 32), 32)
            xf = section_rows(k, i)
            inv = lax.rsqrt(jnp.mean(xf * xf, axis=-1, keepdims=True) + EPS)
            iv[k, rows, :] = jnp.broadcast_to(inv, (32, 128))
            gp[0, rows, :] = (xf * inv).astype(BF16)

        @pl.when(k == s)
        def _():
            nw[c] = gp[0]
            normed_copy().start()

        @pl.loop(0, 2)
        def _(h):
            cols = part(h, 0, HALF)
            w = jnp.concatenate(
                [wa[2 * k + h].reshape(D, XY), wz[2 * k + h].reshape(D, Z)], axis=1
            )
            u = jnp.dot(gp[0], w, preferred_element_type=F32)
            uu = u * u
            t = jnp.tanh((GELU_C * u) * (1.0 + GELU_A * uu))
            cdf = 0.5 * (1.0 + t)
            slope = cdf + (0.5 * GELU_C) * u * (1.0 - t * t) * (1.0 + (3.0 * GELU_A) * uu)

            @pl.when(k < 3)
            def _():
                at = jnp.minimum(k, 2)
                gd[at, :, cols] = slope
                ub[at, :, cols] = u.astype(BF16)
                before = xs[2 * k + h].reshape(ROWS, HALF)
                after = (before.astype(F32) + u * cdf).astype(BF16)
                xs[2 * at + 2 + h] = after.reshape(4, 64, HALF)

            @pl.when(k == 3)
            def _():
                pre = (gr[:, cols].astype(F32) * slope).astype(BF16)
                gp[1, :, cols] = pre
                term = lane_sums(pre.astype(F32) * u)
                ms[...] = jnp.where(h == 0, term, ms[...] + term)

    own = unit(0)
    stage_p1(wz, own, UNITS)
    stage_p1(wa, own, own)
    raw_step(1)
    stage_p2(wz, own, UNITS)
    stage_p2(wa, own, own)
    raw_step(2)
    stage_q1(wz, own, UNITS)
    stage_q1(wa, own, own)
    for copy in in_x:
        copy.wait()
    for m in range(2):
        for q in range(2):
            rows = pl.ds(128 * m + 64 * q, 64)
            live = lax.broadcasted_iota(jnp.int32, (64, D), 0) < lens[m, q]
            gr[rows, :] = jnp.where(live, gr[rows, :].astype(F32), 0.0).astype(BF16)
    near = unit(1)
    stage_p1(wa, near, near)
    raw_step(3)
    stage_q2(wz, own, UNITS)
    stage_p2(wa, near, near)
    stage_f(wz, own, UNITS)
    for i in range(2):
        up(1, i).start()
        down(1, i).start()
    raw_step(4)
    third = unit(2)
    stage_p1(wa, third, third)

    @pl.loop(1, UNITS + 2)
    def _(i):
        def when_unit(ahead, stage):
            @pl.when((i + ahead >= 0) & (i + ahead < UNITS))
            def _():
                u = unit(i + ahead)
                stage(wa, u, u)

        when_unit(0, stage_q1)
        pl.when(i == 2)(lambda: raw_landed(4))
        when_unit(2, stage_p1)
        when_unit(1, stage_p2)
        when_unit(-1, stage_q2)
        k = -1
        for section in range(4):
            for number, step in enumerate(READY[section]):
                k = jnp.where((s == section) & (i == step), number, k)
        pl.when(k >= 0)(lambda: forward(jnp.maximum(k, 0)))
        when_unit(-2, stage_f)
        pl.when(i == 2)(lambda: relay(1, 0))

        @pl.when(i == 3)
        def _():
            relay(1, 1)
            relay(2, 0)

        @pl.when(i == 4)
        def _():
            relay(2, 1)
            relay(3, 0)

        pl.when(i == 5)(lambda: relay(3, 1))
        pl.when(i == 6)(relay_end)

    done = jnp.int32(len(READY[0]))
    for section in range(1, 4):
        done = jnp.where(s == section, len(READY[section]), done)
    pl.loop(done, 4)(forward)

    @pl.loop(0, 3 - s)
    def _(step):
        k = 3 - step
        now = lax.rem(step + 1, 2)
        inv = iv[k][:, :1]
        factor = inv * inv * (jnp.sum(ms[...], axis=-1, keepdims=True) * (1.0 / D))
        sums = None
        for j in range(2):
            tile = jnp.concatenate(
                [
                    w[2 * k + h, j].reshape(HALF, width)
                    for h in range(2)
                    for w, width in ((wa, XY), (wz, Z))
                ],
                axis=1,
            )
            g = lax.dot_general(
                gp[now], tile, (((1,), (1,)), ((), ())), preferred_element_type=F32
            )
            cols = pl.ds(j * HALF, HALF)
            xf = xs[2 * k + j].reshape(ROWS, HALF).astype(F32)
            grad = (gr[:, cols].astype(F32) + inv * g - xf * factor).astype(BF16)
            gr[:, cols] = grad
            pre = (grad.astype(F32) * gd[k - 1, :, cols]).astype(BF16)
            gp[1 - now, :, cols] = pre
            term = lane_sums(pre.astype(F32) * ub[k - 1, :, cols].astype(F32))
            sums = term if sums is None else sums + term
        ms[...] = sums

    last_gp = lax.rem(s, 2)
    def column_part(core, hc):
        return part(core, hc * QUART, QUART)

    def give_g(hc):
        return remote(
            gp.at[last_gp, :, column_part(1 - c, hc)], gw.at[c, :, CS[hc]],
            nsend.at[1 + hc], nrecv.at[1 + hc], sib,
        )

    for hc in range(2):
        give_g(hc).start()
    for hc in range(2):
        gw[c, :, CS[hc]] = gp[last_gp, :, column_part(c, hc)]
    remote(nw.at[1 - c], nw.at[1 - c], nsend.at[0], nrecv.at[0], sib).wait_recv()

    v0, v1 = 1 - zl, zl
    v_of = (v0, v0, v1, v1)

    def weight_term(q):
        v, cs = v_of[q], CS[q % 2]

        @pl.loop(0, 2)
        def _(j):
            rows = pl.ds(pl.multiple_of(v * HALF + j * 512, 512), 512)
            left = nw[:, :, rows].reshape(2 * ROWS, 512)
            right = gw[:, :, cs].reshape(2 * ROWS, QUART)
            total = lax.dot_general(
                left, right, (((0,), (0,)), ((), ())), preferred_element_type=F32
            )
            xs[pl.ds(4 * v + 2 * j, 2), :, :, cs] = total.astype(BF16).reshape(2, 4, 64, QUART)

    def grow(cc, q, i, first=0, count=4):
        v, cs = v_of[q], CS[q % 2]
        if cc == 0:
            return xs.at[4 * v + i, pl.ds(first, count), :, cs]
        return xs.at[pl.ds(4 * v + first, count), i, :, cs]

    def gchip(cc, q, i, rows=None):
        v, cs = v_of[q], CS[q % 2]
        rows = pl.ds(0, 64) if rows is None else rows
        return xs.at[4 * v + y, i, rows, cs] if cc == 0 else xs.at[4 * v + i, x, rows, cs]

    def q_axis(cc):
        return (y, yp, ym, y2, dyp, dym) if cc == 0 else (x, xp, xm, x2, dxp, dxm)

    def p_axis(cc):
        return (x, xp, xm, x2, dxp, dxm) if cc == 0 else (y, yp, ym, y2, dyp, dym)

    def r1_copies(cc, q):
        _, _, _, far, to_plus, to_minus = q_axis(cc)
        return (
            remote(grow(cc, q, far, 0, 2), r1.at[q, 0], gsend.at[0], r1r.at[q, 0], to_plus),
            remote(grow(cc, q, far, 2, 2), r1.at[q, 1], gsend.at[0], r1r.at[q, 1], to_minus),
        )

    def r2_copies(cc, q):
        _, plus, minus, _, to_plus, to_minus = q_axis(cc)
        return (
            remote(grow(cc, q, plus), r2.at[q, 0], gsend.at[1], r2r.at[q], to_plus),
            remote(grow(cc, q, minus), r2.at[q, 1], gsend.at[1], r2r.at[q], to_minus),
        )

    def t1_copies(cc, q):
        _, _, _, far, to_plus, to_minus = p_axis(cc)
        return (
            remote(gchip(cc, q, far, TOP), t1.at[q, 0], gsend.at[2], t1r.at[q, 0], to_plus),
            remote(gchip(cc, q, far, BOTTOM), t1.at[q, 1], gsend.at[2], t1r.at[q, 1], to_minus),
        )

    def t2_copies(cc, q, way):
        _, plus, minus, _, to_plus, to_minus = p_axis(cc)
        block, dest = ((plus, to_plus), (minus, to_minus))[way]
        if q < 2:
            return [
                remote(gchip(cc, q, block), t2.at[q, way], gsend.at[3], t2r.at[q], dest)
            ]
        at = (block, y) if cc == 0 else (x, block)
        return [
            remote(
                gchip(cc, q, block, (TOP, BOTTOM)[core]), u2.at[q - 2, cc, way],
                gsend.at[4], u2r.at[q - 2], device(*at, z, core),
            )
            for core in range(2)
        ]

    def add_into(ref, *others):
        total = ref[...].astype(F32)
        for more in others:
            total = total + more[...].astype(F32)
        ref[...] = total.astype(BF16)

    def rs_a(q):
        def body(cc):
            for copy in r1_copies(cc, q):
                copy.start()

        by_core(body)

    def rs_b(q):
        def body(cc):
            _, plus, minus, _, _, _ = q_axis(cc)
            arrive, leave = r1_copies(cc, q), r2_copies(cc, q)
            arrive[0].wait_recv()
            add_into(grow(cc, q, plus, 0, 2), r1.at[q, 0])
            leave[0].start()
            arrive[1].wait_recv()
            add_into(grow(cc, q, minus, 2, 2), r1.at[q, 1])
            leave[1].start()

        by_core(body)

    def own_part(q):
        block = xs.at[4 * v_of[q] + y, x, sib_rows, CS[q % 2]]
        return remote(block, o1.at[q - 2], osend, orecv.at[q - 2], sib)

    def rs_c(q):
        def body(cc):
            me, plus, minus, far, _, _ = p_axis(cc)
            remote(r2.at[q], r2.at[q], gsend.at[1], r2r.at[q], sib).wait_recv()

            def add(i):
                add_into(gchip(cc, q, i), r2.at[q, 0, i], r2.at[q, 1, i])

            add(far)
            for copy in t1_copies(cc, q):
                copy.start()
            add(plus)
            add(minus)
            add(me)
            if q >= 2:
                own_part(q).start()

        by_core(body)

    def rs_d(q):
        def body(cc):
            _, plus, minus, _, _, _ = p_axis(cc)
            arrive = t1_copies(cc, q)
            arrive[0].wait_recv()
            add_into(gchip(cc, q, plus, TOP), t1.at[q, 0])
            for copy in t2_copies(cc, q, 0):
                copy.start()
            arrive[1].wait_recv()
            add_into(gchip(cc, q, minus, BOTTOM), t1.at[q, 1])
            for copy in t2_copies(cc, q, 1):
                copy.start()

        by_core(body)

    def cross(q, core):
        rows = (TOP, BOTTOM)[core]
        block = xs.at[4 * v0 + y, x, rows, CS[q]]
        dest = device(x, y, 2 * s + 1 - zl, core)
        return remote(block, z1.at[c, :, CS[q]], zsend, zrecv, dest)

    def rs_e(q):
        remote(t2.at[q], t2.at[q], gsend.at[3], t2r.at[q], sib).wait_recv()
        add_into(xs.at[4 * v0 + y, x, :, CS[q]], t2.at[q, 0], t2.at[q, 1])
        cross(q, 0).start()
        cross(q, 1).start()

    def finish(q):
        hc = q - 2
        remote(o1.at[hc], o1.at[hc], osend, orecv.at[hc], sib).wait_recv()
        remote(u2.at[hc], u2.at[hc], gsend.at[4], u2r.at[hc], sib).wait_recv()
        for core, own_ in ((c, xs[4 * v1 + y, x, my_rows, CS[hc]]), (1 - c, o1[hc])):
            total = own_.astype(F32) + z1[core, :, CS[hc]].astype(F32)
            for way in range(2):
                total = total + u2[hc, core, way].astype(F32)
            out_ref[:, column_part(core, hc)] = total

    for q in range(4):
        if q < 2:
            got = gw.at[1 - c, :, CS[q]]
            remote(got, got, nsend.at[1 + q], nrecv.at[1 + q], sib).wait_recv()
        weight_term(q)
        rs_a(q)

    def sent(block, sem):
        remote(block, block, sem, sem, sib).wait_send()

    for copy in gives(1 - c, my_rows):
        copy.wait_send()
    for way in range(2):
        sent(wa.at[pl.ds(0, 7), 0, 0, 0, TOP], rsend.at[way])
    sent(wa.at[0, :, pl.ds(0, 3)], psend.at[0])
    sent(wz.at[0, 0, 0, pl.ds(0, 3)], psend.at[1])
    sent(wa.at[pl.ds(0, 3)], qsend.at[0])
    sent(wz.at[0, 0, pl.ds(0, 3)], qsend.at[1])
    sent(wa.at[pl.ds(0, 4)], dsend.at[0])
    sent(wz.at[0, 0], dsend.at[1])
    sent(wz.at[pl.ds(0, 7), 0, pl.ds(0, 2)], usend)
    sent(wz.at[pl.ds(0, 7), 0, pl.ds(0, 2)], lsend)
    sent(wz.at[pl.ds(0, 7), :, pl.ds(0, 2)], esend)

    for q in range(4):
        rs_b(q)
    rs_c(0)
    rs_c(1)
    rs_d(0)
    rs_c(2)
    rs_d(1)
    rs_e(0)
    rs_c(3)
    rs_d(2)
    rs_e(1)
    rs_d(3)
    remote(z1, z1, zsend, zrecv, sib).wait_recv()
    finish(2)
    finish(3)

    sent(o1, osend)
    sent(z1, zsend)
    give_g(0).wait_send()
    give_g(1).wait_send()
    normed_copy().wait_send()
    sent(r1, gsend.at[0])
    sent(r2, gsend.at[1])
    sent(t1, gsend.at[2])
    sent(t2, gsend.at[3])
    sent(u2, gsend.at[4])


def local(inputs, weights, cotangents, lengths):
    rows = inputs.shape[0] * inputs.shape[1]
    dma = pltpu.SemaphoreType.DMA
    vmem = pl.BlockSpec(memory_space=pltpu.VMEM)
    out = pl.pallas_call(
        kernel,
        out_shape=jax.ShapeDtypeStruct((32, D), F32),
        in_specs=[
            pl.BlockSpec(memory_space=pl.ANY),
            vmem,
            pl.BlockSpec(memory_space=pl.ANY),
            pl.BlockSpec(memory_space=pl.ANY),
        ],
        out_specs=vmem,
        scratch_shapes=[
            pltpu.VMEM((8, 2, 4, 4, 64, XY), BF16),
            pltpu.VMEM((8, 2, 4, 4, 64, Z), BF16),
            pltpu.VMEM((8, 4, 64, HALF), BF16),
            pltpu.VMEM((3, ROWS, D), F32),
            pltpu.VMEM((3, ROWS, D), BF16),
            pltpu.VMEM((4, ROWS, 128), F32),
            pltpu.VMEM((2, ROWS, D), BF16),
            pltpu.VMEM((2, ROWS, D), BF16),
            pltpu.VMEM((2, ROWS, HALF), BF16),
            pltpu.VMEM((ROWS, D), BF16),
            pltpu.VMEM((ROWS, 128), F32),
            pltpu.VMEM((4, 2, 2, 64, QUART), BF16),
            pltpu.VMEM((4, 2, 4, 64, QUART), BF16),
            pltpu.VMEM((4, 2, 32, QUART), BF16),
            pltpu.VMEM((2, 2, 64, QUART), BF16),
            pltpu.VMEM((2, 2, 2, 32, QUART), BF16),
            pltpu.VMEM((2, 32, HALF), BF16),
            pltpu.VMEM((2, 32, QUART), BF16),
            pltpu.SMEM((2, 2), jnp.int32),
            dma((6,)),
            dma((2,)),
            dma((2,)),
            dma((2,)),
            dma((2, 4)),
            dma,
            dma((4, 2)),
            dma,
            dma((4, 2)),
            dma,
            dma((7,)),
            dma((2,)),
            dma((9, 3)),
            dma((2,)),
            dma((9, 4)),
            dma((2,)),
            dma((9,)),
            dma((3,)),
            dma((3,)),
            dma((5,)),
            dma((4, 2)),
            dma((4,)),
            dma((4, 2)),
            dma((2,)),
            dma((2,)),
            dma,
            dma,
            dma,
            dma((2,)),
        ],
        compiler_params=pltpu.CompilerParams(
            collective_id=0, has_side_effects=True, vmem_limit_bytes=63 * 2**20
        ),
        cost_estimate=pl.CostEstimate(
            flops=9 * 2 * ROWS * D * D, bytes_accessed=36 * 2**20, transcendentals=4 * ROWS * D
        ),
    )(inputs.reshape(4, rows // 4, D), weights[0], cotangents.reshape(rows, D), lengths)
    return out[None]


def solution(mesh):
    in_specs = (
        P(None, "fsdp", None),
        P("section", "fsdp", None),
        P(None, "fsdp", None),
        P(None, "fsdp"),
    )
    out_specs = P("section", "fsdp", None)
    return jax.shard_map(local, mesh=mesh, in_specs=in_specs, out_specs=out_specs, check_vma=False)
```

```python
import functools

import jax
import jax.numpy as jnp
from jax import lax
from jax.experimental import pallas as pl
from jax.experimental.pallas import tpu as pltpu
from jax.sharding import PartitionSpec as P

MESH = pl.DeviceIdType.MESH
F32 = jnp.float32
BF16 = jnp.bfloat16
EPS = 1e-06
GELU_C = 0.7978845608028654
GELU_A = 0.044715

D = 2048
ROWS = 256
HALF = 1024
QUART = 512
CS = (pl.ds(0, QUART), pl.ds(QUART, QUART))
XY = 768
Z = HALF - XY
UNITS = 8
READY = ((4, 6, 8), (6, 7, 8), (8, 9), (6, 8))
FIRST, SECOND = pl.ds(0, 2), pl.ds(2, 2)
TOP, BOTTOM = pl.ds(0, 32), pl.ds(32, 32)


def position():
    s, f = lax.axis_index("section"), lax.axis_index("fsdp")
    c = lax.rem(f, 2)
    x = lax.rem(f // 2, 4)
    y = lax.rem(f // 8, 4)
    zl = f // 32
    return s, zl, x, y, c


def device(x, y, z, c):
    return (z // 2, lax.rem(z, 2) * 32 + y * 8 + x * 2 + c)


def remote(src, dst, send, recv, dev):
    return pltpu.make_async_remote_copy(
        src_ref=src, dst_ref=dst, send_sem=send, recv_sem=recv, device_id=dev, device_id_type=MESH
    )


def kernel(
    x_ref, w_ref, cot_ref, len_ref, out_ref,
    wa, wz, xs, gd, ub, iv, gp, nw, gw, gr, ms, r1, r2, t1, t2, u2, z1, o1,
    lens, loc, xsend, xrecv, rsend, rrecv, usend, urecv, lsend, lrecv, esend, erecv,
    psend, precv, qsend, qrecv, dsend, drecv,
    nsend, nrecv, gsend, r1r, r2r, t1r, t2r, u2r, zsend, zrecv, osend, orecv,
):
    s, zl, x, y, c = position()
    z = 2 * s + zl
    sib = device(x, y, z, 1 - c)
    xp, xm = lax.rem(x + 1, 4), lax.rem(x + 3, 4)
    yp, ym = lax.rem(y + 1, 4), lax.rem(y + 3, 4)
    x2, y2 = lax.rem(x + 2, 4), lax.rem(y + 2, 4)
    dxp, dxm = device(xp, y, z, c), device(xm, y, z, c)
    dyp, dym = device(x, yp, z, c), device(x, ym, z, c)

    barrier = pltpu.get_barrier_semaphore()
    above, below = device(x, y, lax.rem(z + 1, 8), c), device(x, y, lax.rem(z + 7, 8), c)
    pair_other = device(x, y, 2 * s + 1 - zl, 1 - c)
    def crossed(plus):
        return device(
            jnp.where(c == 0, x, xp if plus else xm), jnp.where(c == 0, yp if plus else ym, y), z, 1 - c
        )

    cross_plus, cross_minus = crossed(True), crossed(False)
    for partner in (dxp, dxm, dyp, dym, above, below, sib, pair_other, cross_plus, cross_minus):
        pl.semaphore_signal(barrier, inc=1, device_id=partner, device_id_type=MESH)

    def part(core, first, width):
        return pl.ds(pl.multiple_of(core * HALF + first, 256), width)

    in_x = [
        pltpu.make_async_copy(x_ref.at[:, :, h * HALF : (h + 1) * HALF], xs.at[h], loc.at[3 * h])
        for h in range(2)
    ]
    in_x.append(pltpu.make_async_copy(cot_ref, gr, loc.at[4]))
    in_x.append(pltpu.make_async_copy(len_ref, lens, loc.at[5]))
    for copy in in_x:
        copy.start()
    mine = pl.ds(pl.multiple_of(c * HALF, HALF), HALF)
    other = pl.ds(pl.multiple_of((1 - c) * HALF, HALF), HALF)
    my_rows = pl.ds(pl.multiple_of(c * 32, 32), 32)
    sib_rows = pl.ds(pl.multiple_of((1 - c) * 32, 32), 32)
    in_w = [
        pltpu.make_async_copy(src, dst, loc.at[1 + i])
        for i, (src, dst) in enumerate(
            (
                (w_ref.at[:, part(c, 0, XY)], wa.at[2 * s + c, zl, y, x, my_rows]),
                (w_ref.at[:, part(c, XY, Z)], wz.at[2 * s + c, zl, y, x, my_rows]),
            )
        )
    ]
    for copy in in_w:
        copy.start()
    pl.semaphore_wait(barrier, 10)

    def gives(core, rows):
        kh = 2 * s + core
        return (
            remote(
                w_ref.at[:, part(core, XY, Z)], wz.at[kh, zl, y, x, rows],
                xsend.at[0], xrecv.at[0], sib,
            ),
            remote(
                w_ref.at[:, part(core, 0, XY)], wa.at[kh, zl, y, x, rows],
                xsend.at[1], xrecv.at[1], sib,
            ),
        )

    for copy in gives(1 - c, my_rows):
        copy.start()
    for copy in in_w:
        copy.wait()
    for copy in gives(c, sib_rows):
        copy.wait_recv()

    def raw_block(d, half=None):
        v = lax.rem(z + 8 + d, 8)
        at = (2 * (v // 2) + c, lax.rem(v, 2), y, x)
        return wa.at[at] if half is None else wa.at[at + (half,)]

    def raw_up(r, half=None):
        block = raw_block(1 - r, half)
        return remote(block, block, rsend.at[0], rrecv.at[0, r - 1], above)

    def raw_down(r, half=None):
        block = raw_block(r - 1, half)
        return remote(block, block, rsend.at[1], rrecv.at[1, r - 1], below)

    def raw_landed(r):
        ups, downs = raw_block(-r, TOP if r == 4 else None), raw_block(r, BOTTOM if r == 4 else None)
        remote(ups, ups, rsend.at[0], rrecv.at[0, r - 1], above).wait_recv()
        remote(downs, downs, rsend.at[1], rrecv.at[1, r - 1], below).wait_recv()

    def raw_step(r):
        if r > 1:
            raw_landed(r - 1)
        raw_up(r, TOP if r == 4 else None).start()
        raw_down(r, BOTTOM if r == 4 else None).start()

    def row(w, cc, kh, uz, i, part=None):
        if cc == 0:
            return w.at[kh, uz, i] if part is None else w.at[kh, uz, i, part]
        return w.at[kh, uz, :, i] if part is None else w.at[kh, uz, part, i]

    def chip(w, cc, kh, uz, i, part=None):
        at = (kh, uz, y, i) if cc == 0 else (kh, uz, i, x)
        return w.at[at] if part is None else w.at[at + (part,)]

    def p_copies(w, cc, u, b):
        fam = 0 if w is wa else 1
        kh, uz = 2 * (u // 2) + cc, lax.rem(u, 2)
        me, plus, minus = (x, xp, xm) if cc == 0 else (y, yp, ym)
        to_plus, to_minus = (dxp, dxm) if cc == 0 else (dyp, dym)
        own = chip(w, cc, kh, uz, me)
        from_minus, from_plus = chip(w, cc, kh, uz, minus, TOP), chip(w, cc, kh, uz, plus, BOTTOM)
        return (
            remote(own, own, psend.at[fam], precv.at[b, 0], to_plus),
            remote(own, own, psend.at[fam], precv.at[b, 1], to_minus),
            remote(from_minus, from_minus, psend.at[fam], precv.at[b, 2], to_plus),
            remote(from_plus, from_plus, psend.at[fam], precv.at[b, 2], to_minus),
        )

    def p_landed(w, cc, u, b, i):
        kh, uz = 2 * (u // 2) + cc, lax.rem(u, 2)
        plus, minus, far = (xp, xm, x2) if cc == 0 else (yp, ym, y2)
        land = (
            chip(w, cc, kh, uz, minus),
            chip(w, cc, kh, uz, plus),
            chip(w, cc, kh, uz, far),
        )[i]
        remote(land, land, psend.at[0], precv.at[b, i], sib).wait_recv()

    def q_copies(w, cc, u, b):
        fam = 0 if w is wa else 1
        kh, uz = 2 * (u // 2) + cc, lax.rem(u, 2)
        me, plus, minus = (y, yp, ym) if cc == 0 else (x, xp, xm)
        to_plus, to_minus = (dyp, dym) if cc == 0 else (dxp, dxm)
        first, second = row(w, cc, kh, uz, me, FIRST), row(w, cc, kh, uz, me, SECOND)
        from_minus, from_plus = row(w, cc, kh, uz, minus, FIRST), row(w, cc, kh, uz, plus, SECOND)
        return (
            remote(first, first, qsend.at[fam], qrecv.at[b, 0], to_plus),
            remote(second, second, qsend.at[fam], qrecv.at[b, 1], to_minus),
            remote(second, second, qsend.at[fam], qrecv.at[b, 2], to_plus),
            remote(first, first, qsend.at[fam], qrecv.at[b, 2], to_minus),
            remote(from_minus, from_minus, qsend.at[fam], qrecv.at[b, 3], to_plus),
            remote(from_plus, from_plus, qsend.at[fam], qrecv.at[b, 3], to_minus),
        )

    def q_landed(w, cc, u, b, i):
        kh, uz = 2 * (u // 2) + cc, lax.rem(u, 2)
        plus, minus, far = (yp, ym, y2) if cc == 0 else (xp, xm, x2)
        land = (
            row(w, cc, kh, uz, minus, FIRST),
            row(w, cc, kh, uz, plus, SECOND),
            row(w, cc, kh, uz, far),
            row(w, cc, kh, uz, far),
        )[i]
        remote(land, land, qsend.at[0], qrecv.at[b, i], sib).wait_recv()

    def d_copy(w, cc, u, b, i):
        kh, uz = 2 * (u // 2) + cc, lax.rem(u, 2)
        at = ((y, ym, yp, y2) if cc == 0 else (x, xm, xp, x2))[i]
        block = row(w, cc, kh, uz, at)
        return remote(block, block, dsend.at[0 if w is wa else 1], drecv.at[b], sib)

    def by_core(body):
        for cc in (0, 1):
            pl.when(c == cc)(functools.partial(body, cc))

    def unit(t):
        rest = t - 2
        near = jnp.where(rest < 2, rest + 2, jnp.where(rest < 4, rest - 2, rest + 2))
        rest = jnp.where(s == 2, near, jnp.where(rest < 2 * s, rest, rest + 2))
        return jnp.where(t == 0, z, jnp.where(t == 1, 2 * s + 1 - zl, rest))

    def stage_p1(w, u, b):
        def body(cc):
            copies = p_copies(w, cc, u, b)
            copies[0].start()
            copies[1].start()

        by_core(body)

    def stage_p2(w, u, b):
        def body(cc):
            copies = p_copies(w, cc, u, b)
            p_landed(w, cc, u, b, 0)
            copies[2].start()
            p_landed(w, cc, u, b, 1)
            copies[3].start()

        by_core(body)

    def stage_q1(w, u, b):
        def body(cc):
            copies = q_copies(w, cc, u, b)
            p_landed(w, cc, u, b, 2)
            for copy in copies[:4]:
                copy.start()
            d_copy(w, cc, u, b, 0).start()

        by_core(body)

    def stage_q2(w, u, b):
        def body(cc):
            copies = q_copies(w, cc, u, b)
            q_landed(w, cc, u, b, 0)
            copies[4].start()
            q_landed(w, cc, u, b, 1)
            copies[5].start()

        by_core(body)

    def stage_f(w, u, b):
        def body(cc):
            q_landed(w, cc, u, b, 2)
            d_copy(w, cc, u, b, 1).start()
            d_copy(w, cc, u, b, 2).start()
            q_landed(w, cc, u, b, 3)
            d_copy(w, cc, u, b, 3).start()

        by_core(body)

    PARTS = (pl.ds(0, 2), pl.ds(2, 2))
    def plane(d, part, core=None):
        v = lax.rem(z + 8 + d, 8)
        core = c if core is None else core
        return wz.at[2 * (v // 2) + core, lax.rem(v, 2), PARTS[part]]

    def up(r, part):
        block = plane(1 - r, part)
        return remote(block, block, usend, urecv.at[r - 1, part], above)

    def down(r, part):
        block = plane(r - 1, part)
        return remote(block, block, lsend, lrecv.at[r - 1, part], below)

    def up_landed(r, part):
        block = plane(-r, part)
        remote(block, block, usend, urecv.at[r - 1, part], above).wait_recv()

    def down_landed(r, part):
        block = plane(r, part)
        remote(block, block, lsend, lrecv.at[r - 1, part], below).wait_recv()

    def e_copy(slot, part):
        d = (-1, -2, -3, 1, 2, 3, 4)[slot]
        block = plane(d, part)
        return remote(block, block, esend, erecv.at[slot], sib)

    def relay(r, part):
        up_landed(r, part)
        if r < 3 or part == 0:
            up(r + 1, part).start()
        down_landed(r, part)
        if r < 3 or part == 1:
            down(r + 1, part).start()
        e_copy(r - 1, part).start()
        e_copy(r + 2, part).start()

    def relay_end():
        up_landed(4, 0)
        e_copy(6, 0).start()
        down_landed(4, 1)
        e_copy(6, 1).start()

    def normed_copy():
        return remote(nw.at[c], nw.at[c], nsend.at[0], nrecv.at[0], sib)

    def section_rows(k, i):
        at = pl.ds(pl.multiple_of(lax.rem(i, 2) * 32, 32), 32)
        halves = [xs[2 * k + h, i // 2, at, :].astype(F32) for h in range(2)]
        return jnp.concatenate(halves, axis=1)

    def lane_sums(v):
        total = v[:, :128]
        for i in range(1, HALF // 128):
            total = total + v[:, i * 128 : (i + 1) * 128]
        return total

    def norm(k):
        @pl.loop(0, ROWS // 32)
        def _(i):
            rows = pl.ds(pl.multiple_of(i * 32, 32), 32)
            xf = section_rows(k, i)
            inv = lax.rsqrt(jnp.mean(xf * xf, axis=-1, keepdims=True) + EPS)
            iv[k, rows, :] = jnp.broadcast_to(inv, (32, 128))
            gp[0, rows, :] = (xf * inv).astype(BF16)

        @pl.when(k == s)
        def _():
            nw[c] = gp[0]
            normed_copy().start()

    def arrived(k):
        @pl.loop(0, 2)
        def _(uz):
            u = 2 * k + uz

            block = wa.at[2 * k + 1 - c, uz]
            remote(block, block, dsend.at[0], drecv.at[u], sib).wait_recv()
            z_block = wz.at[2 * k + 1 - c, uz]

            @pl.when(u == z)
            def _():
                remote(z_block, z_block, dsend.at[1], drecv.at[UNITS], sib).wait_recv()

            @pl.when(u != z)
            def _():
                d = lax.rem(u - z + 8, 8)
                slot = jnp.where(d < 4, 2 + d, jnp.where(d == 4, 6, 7 - d))
                remote(z_block, z_block, esend, erecv.at[slot], sib).wait_recv()

    def preact(k, h):
        w = jnp.concatenate([wa[2 * k + h].reshape(D, XY), wz[2 * k + h].reshape(D, Z)], axis=1)
        u = jnp.dot(gp[0], w, preferred_element_type=F32)
        uu = u * u
        t = jnp.tanh((GELU_C * u) * (1.0 + GELU_A * uu))
        cdf = 0.5 * (1.0 + t)
        slope = cdf + (0.5 * GELU_C) * u * (1.0 - t * t) * (1.0 + (3.0 * GELU_A) * uu)
        return u, cdf, slope

    def forward(k):
        arrived(k)

        @pl.loop(0, 2)
        def _(h):
            cols = part(h, 0, HALF)
            u, cdf, slope = preact(k, h)
            gd[k, :, cols] = slope
            ub[k, :, cols] = u.astype(BF16)
            before = xs[2 * k + h].reshape(ROWS, HALF)
            after = (before.astype(F32) + u * cdf).astype(BF16)
            xs[2 * k + 2 + h] = after.reshape(4, 64, HALF)

        pl.when(k < 2)(lambda: norm(jnp.minimum(k + 1, 2)))

    def forward_last():
        norm(3)
        arrived(3)
        sums = None
        for h in range(2):
            cols = pl.ds(h * HALF, HALF)
            u, _, slope = preact(3, h)
            pre = (gr[:, cols].astype(F32) * slope).astype(BF16)
            gp[1, :, cols] = pre
            term = lane_sums(pre.astype(F32) * u)
            sums = term if sums is None else sums + term
        ms[...] = sums

    own = unit(0)
    stage_p1(wz, own, UNITS)
    stage_p1(wa, own, own)
    raw_step(1)
    stage_p2(wz, own, UNITS)
    stage_p2(wa, own, own)
    raw_step(2)
    stage_q1(wz, own, UNITS)
    stage_q1(wa, own, own)
    for copy in in_x:
        copy.wait()
    for m in range(2):
        for q in range(2):
            rows = pl.ds(128 * m + 64 * q, 64)
            live = lax.broadcasted_iota(jnp.int32, (64, D), 0) < lens[m, q]
            gr[rows, :] = jnp.where(live, gr[rows, :].astype(F32), 0.0).astype(BF16)
    near = unit(1)
    stage_p1(wa, near, near)
    raw_step(3)
    stage_q2(wz, own, UNITS)
    stage_p2(wa, near, near)
    stage_f(wz, own, UNITS)
    for i in range(2):
        up(1, i).start()
        down(1, i).start()
    raw_step(4)
    third = unit(2)
    stage_p1(wa, third, third)
    norm(0)

    @pl.loop(1, UNITS + 2)
    def _(i):
        def when_unit(ahead, stage):
            @pl.when((i + ahead >= 0) & (i + ahead < UNITS))
            def _():
                u = unit(i + ahead)
                stage(wa, u, u)

        when_unit(0, stage_q1)
        when_unit(1, stage_p2)
        when_unit(-1, stage_q2)
        pl.when(i == 2)(lambda: raw_landed(4))
        when_unit(2, stage_p1)
        k = -1
        for section in range(4):
            for number, step in enumerate(READY[section]):
                k = jnp.where((s == section) & (i == step), number, k)
        pl.when(k >= 0)(lambda: forward(jnp.maximum(k, 0)))
        when_unit(-2, stage_f)
        pl.when(i == 2)(lambda: relay(1, 0))

        @pl.when(i == 3)
        def _():
            relay(1, 1)
            relay(2, 0)

        @pl.when(i == 4)
        def _():
            relay(2, 1)
            relay(3, 0)

        pl.when(i == 5)(lambda: relay(3, 1))
        pl.when(i == 6)(relay_end)

    done = jnp.int32(len(READY[0]))
    for section in range(1, 4):
        done = jnp.where(s == section, len(READY[section]), done)
    pl.loop(done, 3)(forward)
    forward_last()

    @pl.loop(0, 3 - s)
    def _(step):
        k = 3 - step
        now = lax.rem(step + 1, 2)
        inv = iv[k][:, :1]
        factor = inv * inv * (jnp.sum(ms[...], axis=-1, keepdims=True) * (1.0 / D))
        sums = None
        for j in range(2):
            tile = jnp.concatenate(
                [
                    w[2 * k + h, j].reshape(HALF, width)
                    for h in range(2)
                    for w, width in ((wa, XY), (wz, Z))
                ],
                axis=1,
            )
            g = lax.dot_general(
                gp[now], tile, (((1,), (1,)), ((), ())), preferred_element_type=F32
            )
            cols = pl.ds(j * HALF, HALF)
            xf = xs[2 * k + j].reshape(ROWS, HALF).astype(F32)
            grad = (gr[:, cols].astype(F32) + inv * g - xf * factor).astype(BF16)
            gr[:, cols] = grad
            pre = (grad.astype(F32) * gd[k - 1, :, cols]).astype(BF16)
            gp[1 - now, :, cols] = pre
            term = lane_sums(pre.astype(F32) * ub[k - 1, :, cols].astype(F32))
            sums = term if sums is None else sums + term
        ms[...] = sums

    last_gp = lax.rem(s, 2)
    def column_part(core, hc):
        return part(core, hc * QUART, QUART)

    def give_g(hc):
        return remote(
            gp.at[last_gp, :, column_part(1 - c, hc)], gw.at[c, :, CS[hc]],
            nsend.at[1 + hc], nrecv.at[1 + hc], sib,
        )

    for hc in range(2):
        give_g(hc).start()
    for hc in range(2):
        gw[c, :, CS[hc]] = gp[last_gp, :, column_part(c, hc)]
    remote(nw.at[1 - c], nw.at[1 - c], nsend.at[0], nrecv.at[0], sib).wait_recv()

    v0, v1 = 1 - zl, zl
    v_of = (v0, v0, v1, v1)

    def weight_term(q):
        v, cs = v_of[q], CS[q % 2]

        @pl.loop(0, 2)
        def _(j):
            rows = pl.ds(pl.multiple_of(v * HALF + j * 512, 512), 512)
            left = nw[:, :, rows].reshape(2 * ROWS, 512)
            right = gw[:, :, cs].reshape(2 * ROWS, QUART)
            total = lax.dot_general(
                left, right, (((0,), (0,)), ((), ())), preferred_element_type=F32
            )
            xs[pl.ds(4 * v + 2 * j, 2), :, :, cs] = total.astype(BF16).reshape(2, 4, 64, QUART)

    def grow(cc, q, i, first=0, count=4):
        v, cs = v_of[q], CS[q % 2]
        if cc == 0:
            return xs.at[4 * v + i, pl.ds(first, count), :, cs]
        return xs.at[pl.ds(4 * v + first, count), i, :, cs]

    def gchip(cc, q, i, rows=None):
        v, cs = v_of[q], CS[q % 2]
        rows = pl.ds(0, 64) if rows is None else rows
        return xs.at[4 * v + y, i, rows, cs] if cc == 0 else xs.at[4 * v + i, x, rows, cs]

    def q_axis(cc):
        return (y, yp, ym, y2, dyp, dym) if cc == 0 else (x, xp, xm, x2, dxp, dxm)

    def p_axis(cc):
        return (x, xp, xm, x2, dxp, dxm) if cc == 0 else (y, yp, ym, y2, dyp, dym)

    def r1_copies(cc, q):
        _, _, _, far, to_plus, to_minus = q_axis(cc)
        return (
            remote(grow(cc, q, far, 0, 2), r1.at[q, 0], gsend.at[0], r1r.at[q, 0], to_plus),
            remote(grow(cc, q, far, 2, 2), r1.at[q, 1], gsend.at[0], r1r.at[q, 1], to_minus),
        )

    def r2_copies(cc, q):
        _, plus, minus, _, to_plus, to_minus = q_axis(cc)
        return (
            remote(grow(cc, q, plus), r2.at[q, 0], gsend.at[1], r2r.at[q], to_plus),
            remote(grow(cc, q, minus), r2.at[q, 1], gsend.at[1], r2r.at[q], to_minus),
        )

    def t1_copies(cc, q):
        _, _, _, far, to_plus, to_minus = p_axis(cc)
        return (
            remote(gchip(cc, q, far, TOP), t1.at[q, 0], gsend.at[2], t1r.at[q, 0], to_plus),
            remote(gchip(cc, q, far, BOTTOM), t1.at[q, 1], gsend.at[2], t1r.at[q, 1], to_minus),
        )

    def t2_copies(cc, q, way):
        _, plus, minus, _, to_plus, to_minus = p_axis(cc)
        block, dest = ((plus, to_plus), (minus, to_minus))[way]
        if q < 2:
            return [
                remote(gchip(cc, q, block), t2.at[q, way], gsend.at[3], t2r.at[q], dest)
            ]
        at = (block, y) if cc == 0 else (x, block)
        return [
            remote(
                gchip(cc, q, block, (TOP, BOTTOM)[core]), u2.at[q - 2, cc, way],
                gsend.at[4], u2r.at[q - 2], device(*at, z, core),
            )
            for core in range(2)
        ]

    def add_into(ref, *others):
        total = ref[...].astype(F32)
        for more in others:
            total = total + more[...].astype(F32)
        ref[...] = total.astype(BF16)

    def rs_a(q):
        def body(cc):
            for copy in r1_copies(cc, q):
                copy.start()

        by_core(body)

    def rs_b(q):
        def body(cc):
            _, plus, minus, _, _, _ = q_axis(cc)
            arrive, leave = r1_copies(cc, q), r2_copies(cc, q)
            arrive[0].wait_recv()
            add_into(grow(cc, q, plus, 0, 2), r1.at[q, 0])
            leave[0].start()
            arrive[1].wait_recv()
            add_into(grow(cc, q, minus, 2, 2), r1.at[q, 1])
            leave[1].start()

        by_core(body)

    def own_part(q):
        block = xs.at[4 * v_of[q] + y, x, sib_rows, CS[q % 2]]
        return remote(block, o1.at[q - 2], osend, orecv.at[q - 2], sib)

    def rs_c(q):
        def body(cc):
            me, plus, minus, far, _, _ = p_axis(cc)
            remote(r2.at[q], r2.at[q], gsend.at[1], r2r.at[q], sib).wait_recv()

            def add(i):
                add_into(gchip(cc, q, i), r2.at[q, 0, i], r2.at[q, 1, i])

            add(far)
            for copy in t1_copies(cc, q):
                copy.start()
            add(plus)
            add(minus)
            add(me)
            if q >= 2:
                own_part(q).start()

        by_core(body)

    def rs_d(q):
        def body(cc):
            _, plus, minus, _, _, _ = p_axis(cc)
            arrive = t1_copies(cc, q)
            arrive[0].wait_recv()
            add_into(gchip(cc, q, plus, TOP), t1.at[q, 0])
            for copy in t2_copies(cc, q, 0):
                copy.start()
            arrive[1].wait_recv()
            add_into(gchip(cc, q, minus, BOTTOM), t1.at[q, 1])
            for copy in t2_copies(cc, q, 1):
                copy.start()

        by_core(body)

    def cross(q, core):
        rows = (TOP, BOTTOM)[core]
        block = xs.at[4 * v0 + y, x, rows, CS[q]]
        dest = device(x, y, 2 * s + 1 - zl, core)
        return remote(block, z1.at[c, :, CS[q]], zsend, zrecv, dest)

    def rs_e(q):
        remote(t2.at[q], t2.at[q], gsend.at[3], t2r.at[q], sib).wait_recv()
        add_into(xs.at[4 * v0 + y, x, :, CS[q]], t2.at[q, 0], t2.at[q, 1])
        cross(q, 0).start()
        cross(q, 1).start()

    def finish(q):
        hc = q - 2
        remote(o1.at[hc], o1.at[hc], osend, orecv.at[hc], sib).wait_recv()
        remote(u2.at[hc], u2.at[hc], gsend.at[4], u2r.at[hc], sib).wait_recv()
        for core, own_ in ((c, xs[4 * v1 + y, x, my_rows, CS[hc]]), (1 - c, o1[hc])):
            total = own_.astype(F32) + z1[core, :, CS[hc]].astype(F32)
            for way in range(2):
                total = total + u2[hc, core, way].astype(F32)
            out_ref[:, column_part(core, hc)] = total

    for q in range(4):
        if q < 2:
            got = gw.at[1 - c, :, CS[q]]
            remote(got, got, nsend.at[1 + q], nrecv.at[1 + q], sib).wait_recv()
        weight_term(q)
        rs_a(q)

    def sent(block, sem):
        remote(block, block, sem, sem, sib).wait_send()

    for copy in gives(1 - c, my_rows):
        copy.wait_send()
    for way in range(2):
        sent(wa.at[pl.ds(0, 7), 0, 0, 0, TOP], rsend.at[way])
    sent(wa.at[0, :, pl.ds(0, 3)], psend.at[0])
    sent(wz.at[0, 0, 0, pl.ds(0, 3)], psend.at[1])
    sent(wa.at[pl.ds(0, 3)], qsend.at[0])
    sent(wz.at[0, 0, pl.ds(0, 3)], qsend.at[1])
    sent(wa.at[pl.ds(0, 4)], dsend.at[0])
    sent(wz.at[0, 0], dsend.at[1])
    sent(wz.at[pl.ds(0, 7), 0, pl.ds(0, 2)], usend)
    sent(wz.at[pl.ds(0, 7), 0, pl.ds(0, 2)], lsend)
    sent(wz.at[pl.ds(0, 7), :, pl.ds(0, 2)], esend)

    for q in range(4):
        rs_b(q)
    rs_c(0)
    rs_c(1)
    rs_d(0)
    rs_c(2)
    rs_d(1)
    rs_e(0)
    rs_c(3)
    rs_d(2)
    rs_e(1)
    rs_d(3)
    remote(z1, z1, zsend, zrecv, sib).wait_recv()
    finish(2)
    finish(3)

    sent(o1, osend)
    sent(z1, zsend)
    give_g(0).wait_send()
    give_g(1).wait_send()
    normed_copy().wait_send()
    sent(r1, gsend.at[0])
    sent(r2, gsend.at[1])
    sent(t1, gsend.at[2])
    sent(t2, gsend.at[3])
    sent(u2, gsend.at[4])


def local(inputs, weights, cotangents, lengths):
    rows = inputs.shape[0] * inputs.shape[1]
    dma = pltpu.SemaphoreType.DMA
    vmem = pl.BlockSpec(memory_space=pltpu.VMEM)
    out = pl.pallas_call(
        kernel,
        out_shape=jax.ShapeDtypeStruct((32, D), F32),
        in_specs=[
            pl.BlockSpec(memory_space=pl.ANY),
            vmem,
            pl.BlockSpec(memory_space=pl.ANY),
            pl.BlockSpec(memory_space=pl.ANY),
        ],
        out_specs=vmem,
        scratch_shapes=[
            pltpu.VMEM((8, 2, 4, 4, 64, XY), BF16),
            pltpu.VMEM((8, 2, 4, 4, 64, Z), BF16),
            pltpu.VMEM((8, 4, 64, HALF), BF16),
            pltpu.VMEM((3, ROWS, D), F32),
            pltpu.VMEM((3, ROWS, D), BF16),
            pltpu.VMEM((4, ROWS, 128), F32),
            pltpu.VMEM((2, ROWS, D), BF16),
            pltpu.VMEM((2, ROWS, D), BF16),
            pltpu.VMEM((2, ROWS, HALF), BF16),
            pltpu.VMEM((ROWS, D), BF16),
            pltpu.VMEM((ROWS, 128), F32),
            pltpu.VMEM((4, 2, 2, 64, QUART), BF16),
            pltpu.VMEM((4, 2, 4, 64, QUART), BF16),
            pltpu.VMEM((4, 2, 32, QUART), BF16),
            pltpu.VMEM((2, 2, 64, QUART), BF16),
            pltpu.VMEM((2, 2, 2, 32, QUART), BF16),
            pltpu.VMEM((2, 32, HALF), BF16),
            pltpu.VMEM((2, 32, QUART), BF16),
            pltpu.SMEM((2, 2), jnp.int32),
            dma((6,)),
            dma((2,)),
            dma((2,)),
            dma((2,)),
            dma((2, 4)),
            dma,
            dma((4, 2)),
            dma,
            dma((4, 2)),
            dma,
            dma((7,)),
            dma((2,)),
            dma((9, 3)),
            dma((2,)),
            dma((9, 4)),
            dma((2,)),
            dma((9,)),
            dma((3,)),
            dma((3,)),
            dma((5,)),
            dma((4, 2)),
            dma((4,)),
            dma((4, 2)),
            dma((2,)),
            dma((2,)),
            dma,
            dma,
            dma,
            dma((2,)),
        ],
        compiler_params=pltpu.CompilerParams(
            collective_id=0, has_side_effects=True, vmem_limit_bytes=63 * 2**20
        ),
        cost_estimate=pl.CostEstimate(
            flops=9 * 2 * ROWS * D * D, bytes_accessed=36 * 2**20, transcendentals=4 * ROWS * D
        ),
    )(inputs.reshape(4, rows // 4, D), weights[0], cotangents.reshape(rows, D), lengths)
    return out[None]


def solution(mesh):
    in_specs = (
        P(None, "fsdp", None),
        P("section", "fsdp", None),
        P(None, "fsdp", None),
        P(None, "fsdp"),
    )
    out_specs = P("section", "fsdp", None)
    return jax.shard_map(local, mesh=mesh, in_specs=in_specs, out_specs=out_specs, check_vma=False)
```

```python
import functools

import jax
import jax.numpy as jnp
from jax import lax
from jax.experimental import pallas as pl
from jax.experimental.pallas import tpu as pltpu
from jax.sharding import PartitionSpec as P

MESH = pl.DeviceIdType.MESH
F32 = jnp.float32
BF16 = jnp.bfloat16
EPS = 1e-06
GELU_C = 0.7978845608028654
GELU_A = 0.044715

D = 2048
ROWS = 256
HALF = 1024
QUART = 512
CS = (pl.ds(0, QUART), pl.ds(QUART, QUART))
XY = 768
Z = HALF - XY
UNITS = 8
READY = ((4, 6, 8), (6, 7, 8), (8, 9), (6, 8))
FIRST, SECOND = pl.ds(0, 2), pl.ds(2, 2)
TOP, BOTTOM = pl.ds(0, 32), pl.ds(32, 32)


def position():
    s, f = lax.axis_index("section"), lax.axis_index("fsdp")
    c = lax.rem(f, 2)
    x = lax.rem(f // 2, 4)
    y = lax.rem(f // 8, 4)
    zl = f // 32
    return s, zl, x, y, c


def device(x, y, z, c):
    return (z // 2, lax.rem(z, 2) * 32 + y * 8 + x * 2 + c)


def remote(src, dst, send, recv, dev):
    return pltpu.make_async_remote_copy(
        src_ref=src, dst_ref=dst, send_sem=send, recv_sem=recv, device_id=dev, device_id_type=MESH
    )


def kernel(
    x_ref, w_ref, cot_ref, len_ref, out_ref,
    wa, wz, xs, gd, ub, iv, gp, nw, gw, gr, ms, r1, r2, t1, t2, u2, z1, o1,
    lens, loc, xsend, xrecv, rsend, rrecv, usend, urecv, lsend, lrecv, esend, erecv,
    psend, precv, qsend, qrecv, dsend, drecv,
    nsend, nrecv, gsend, r1r, r2r, t1r, t2r, u2r, zsend, zrecv, osend, orecv,
):
    s, zl, x, y, c = position()
    z = 2 * s + zl
    sib = device(x, y, z, 1 - c)
    xp, xm = lax.rem(x + 1, 4), lax.rem(x + 3, 4)
    yp, ym = lax.rem(y + 1, 4), lax.rem(y + 3, 4)
    x2, y2 = lax.rem(x + 2, 4), lax.rem(y + 2, 4)
    dxp, dxm = device(xp, y, z, c), device(xm, y, z, c)
    dyp, dym = device(x, yp, z, c), device(x, ym, z, c)

    barrier = pltpu.get_barrier_semaphore()
    above, below = device(x, y, lax.rem(z + 1, 8), c), device(x, y, lax.rem(z + 7, 8), c)
    pair_other = device(x, y, 2 * s + 1 - zl, 1 - c)
    def crossed(plus):
        return device(
            jnp.where(c == 0, x, xp if plus else xm), jnp.where(c == 0, yp if plus else ym, y), z, 1 - c
        )

    cross_plus, cross_minus = crossed(True), crossed(False)
    for partner in (dxp, dxm, dyp, dym, above, below, sib, pair_other, cross_plus, cross_minus):
        pl.semaphore_signal(barrier, inc=1, device_id=partner, device_id_type=MESH)

    def part(core, first, width):
        return pl.ds(pl.multiple_of(core * HALF + first, 256), width)

    in_x = [
        pltpu.make_async_copy(x_ref.at[:, :, h * HALF : (h + 1) * HALF], xs.at[h], loc.at[3 * h])
        for h in range(2)
    ]
    in_x.append(pltpu.make_async_copy(cot_ref, gr, loc.at[4]))
    in_x.append(pltpu.make_async_copy(len_ref, lens, loc.at[5]))
    for copy in in_x:
        copy.start()
    mine = pl.ds(pl.multiple_of(c * HALF, HALF), HALF)
    other = pl.ds(pl.multiple_of((1 - c) * HALF, HALF), HALF)
    my_rows = pl.ds(pl.multiple_of(c * 32, 32), 32)
    sib_rows = pl.ds(pl.multiple_of((1 - c) * 32, 32), 32)
    in_w = [
        pltpu.make_async_copy(src, dst, loc.at[1 + i])
        for i, (src, dst) in enumerate(
            (
                (w_ref.at[:, part(c, 0, XY)], wa.at[2 * s + c, zl, y, x, my_rows]),
                (w_ref.at[:, part(c, XY, Z)], wz.at[2 * s + c, zl, y, x, my_rows]),
            )
        )
    ]
    for copy in in_w:
        copy.start()
    pl.semaphore_wait(barrier, 10)

    def gives(core, rows):
        kh = 2 * s + core
        return (
            remote(
                w_ref.at[:, part(core, XY, Z)], wz.at[kh, zl, y, x, rows],
                xsend.at[0], xrecv.at[0], sib,
            ),
            remote(
                w_ref.at[:, part(core, 0, XY)], wa.at[kh, zl, y, x, rows],
                xsend.at[1], xrecv.at[1], sib,
            ),
        )

    for copy in gives(1 - c, my_rows):
        copy.start()
    for copy in in_w:
        copy.wait()
    for copy in gives(c, sib_rows):
        copy.wait_recv()

    def raw_block(d, half=None):
        v = lax.rem(z + 8 + d, 8)
        at = (2 * (v // 2) + c, lax.rem(v, 2), y, x)
        return wa.at[at] if half is None else wa.at[at + (half,)]

    def raw_up(r, half=None):
        block = raw_block(1 - r, half)
        return remote(block, block, rsend.at[0], rrecv.at[0, r - 1], above)

    def raw_down(r, half=None):
        block = raw_block(r - 1, half)
        return remote(block, block, rsend.at[1], rrecv.at[1, r - 1], below)

    def raw_landed(r):
        ups, downs = raw_block(-r, TOP if r == 4 else None), raw_block(r, BOTTOM if r == 4 else None)
        remote(ups, ups, rsend.at[0], rrecv.at[0, r - 1], above).wait_recv()
        remote(downs, downs, rsend.at[1], rrecv.at[1, r - 1], below).wait_recv()

    def raw_step(r):
        if r > 1:
            raw_landed(r - 1)
        raw_up(r, TOP if r == 4 else None).start()
        raw_down(r, BOTTOM if r == 4 else None).start()

    def row(w, cc, kh, uz, i, part=None):
        if cc == 0:
            return w.at[kh, uz, i] if part is None else w.at[kh, uz, i, part]
        return w.at[kh, uz, :, i] if part is None else w.at[kh, uz, part, i]

    def chip(w, cc, kh, uz, i, part=None):
        at = (kh, uz, y, i) if cc == 0 else (kh, uz, i, x)
        return w.at[at] if part is None else w.at[at + (part,)]

    def p_copies(w, cc, u, b):
        fam = 0 if w is wa else 1
        kh, uz = 2 * (u // 2) + cc, lax.rem(u, 2)
        me, plus, minus = (x, xp, xm) if cc == 0 else (y, yp, ym)
        to_plus, to_minus = (dxp, dxm) if cc == 0 else (dyp, dym)
        own = chip(w, cc, kh, uz, me)
        from_minus, from_plus = chip(w, cc, kh, uz, minus, TOP), chip(w, cc, kh, uz, plus, BOTTOM)
        return (
            remote(own, own, psend.at[fam], precv.at[b, 0], to_plus),
            remote(own, own, psend.at[fam], precv.at[b, 1], to_minus),
            remote(from_minus, from_minus, psend.at[fam], precv.at[b, 2], to_plus),
            remote(from_plus, from_plus, psend.at[fam], precv.at[b, 2], to_minus),
        )

    def p_landed(w, cc, u, b, i):
        kh, uz = 2 * (u // 2) + cc, lax.rem(u, 2)
        plus, minus, far = (xp, xm, x2) if cc == 0 else (yp, ym, y2)
        land = (
            chip(w, cc, kh, uz, minus),
            chip(w, cc, kh, uz, plus),
            chip(w, cc, kh, uz, far),
        )[i]
        remote(land, land, psend.at[0], precv.at[b, i], sib).wait_recv()

    def q_copies(w, cc, u, b):
        fam = 0 if w is wa else 1
        kh, uz = 2 * (u // 2) + cc, lax.rem(u, 2)
        me, plus, minus = (y, yp, ym) if cc == 0 else (x, xp, xm)
        to_plus, to_minus = (dyp, dym) if cc == 0 else (dxp, dxm)
        first, second = row(w, cc, kh, uz, me, FIRST), row(w, cc, kh, uz, me, SECOND)
        from_minus, from_plus = row(w, cc, kh, uz, minus, FIRST), row(w, cc, kh, uz, plus, SECOND)
        return (
            remote(first, first, qsend.at[fam], qrecv.at[b, 0], to_plus),
            remote(second, second, qsend.at[fam], qrecv.at[b, 1], to_minus),
            remote(second, second, qsend.at[fam], qrecv.at[b, 2], to_plus),
            remote(first, first, qsend.at[fam], qrecv.at[b, 2], to_minus),
            remote(from_minus, from_minus, qsend.at[fam], qrecv.at[b, 3], to_plus),
            remote(from_plus, from_plus, qsend.at[fam], qrecv.at[b, 3], to_minus),
        )

    def q_landed(w, cc, u, b, i):
        kh, uz = 2 * (u // 2) + cc, lax.rem(u, 2)
        plus, minus, far = (yp, ym, y2) if cc == 0 else (xp, xm, x2)
        land = (
            row(w, cc, kh, uz, minus, FIRST),
            row(w, cc, kh, uz, plus, SECOND),
            row(w, cc, kh, uz, far),
            row(w, cc, kh, uz, far),
        )[i]
        remote(land, land, qsend.at[0], qrecv.at[b, i], sib).wait_recv()

    def d_copy(w, cc, u, b, i):
        kh, uz = 2 * (u // 2) + cc, lax.rem(u, 2)
        at = ((y, ym, yp, y2) if cc == 0 else (x, xm, xp, x2))[i]
        block = row(w, cc, kh, uz, at)
        return remote(block, block, dsend.at[0 if w is wa else 1], drecv.at[b], sib)

    def by_core(body):
        for cc in (0, 1):
            pl.when(c == cc)(functools.partial(body, cc))

    def unit(t):
        rest = t - 2
        near = jnp.where(rest < 2, rest + 2, jnp.where(rest < 4, rest - 2, rest + 2))
        rest = jnp.where(s == 2, near, jnp.where(rest < 2 * s, rest, rest + 2))
        return jnp.where(t == 0, z, jnp.where(t == 1, 2 * s + 1 - zl, rest))

    def stage_p1(w, u, b):
        def body(cc):
            copies = p_copies(w, cc, u, b)
            copies[0].start()
            copies[1].start()

        by_core(body)

    def stage_p2(w, u, b):
        def body(cc):
            copies = p_copies(w, cc, u, b)
            p_landed(w, cc, u, b, 0)
            copies[2].start()
            p_landed(w, cc, u, b, 1)
            copies[3].start()

        by_core(body)

    def stage_q1(w, u, b):
        def body(cc):
            copies = q_copies(w, cc, u, b)
            p_landed(w, cc, u, b, 2)
            for copy in copies[:4]:
                copy.start()
            d_copy(w, cc, u, b, 0).start()

        by_core(body)

    def stage_q2(w, u, b):
        def body(cc):
            copies = q_copies(w, cc, u, b)
            q_landed(w, cc, u, b, 0)
            copies[4].start()
            q_landed(w, cc, u, b, 1)
            copies[5].start()

        by_core(body)

    def stage_f(w, u, b):
        def body(cc):
            q_landed(w, cc, u, b, 2)
            d_copy(w, cc, u, b, 1).start()
            d_copy(w, cc, u, b, 2).start()
            q_landed(w, cc, u, b, 3)
            d_copy(w, cc, u, b, 3).start()

        by_core(body)

    PARTS = (pl.ds(0, 2), pl.ds(2, 2))
    def plane(d, part, core=None):
        v = lax.rem(z + 8 + d, 8)
        core = c if core is None else core
        return wz.at[2 * (v // 2) + core, lax.rem(v, 2), PARTS[part]]

    def up(r, part):
        block = plane(1 - r, part)
        return remote(block, block, usend, urecv.at[r - 1, part], above)

    def down(r, part):
        block = plane(r - 1, part)
        return remote(block, block, lsend, lrecv.at[r - 1, part], below)

    def up_landed(r, part):
        block = plane(-r, part)
        remote(block, block, usend, urecv.at[r - 1, part], above).wait_recv()

    def down_landed(r, part):
        block = plane(r, part)
        remote(block, block, lsend, lrecv.at[r - 1, part], below).wait_recv()

    def e_copy(slot, part):
        d = (-1, -2, -3, 1, 2, 3, 4)[slot]
        block = plane(d, part)
        return remote(block, block, esend, erecv.at[slot], sib)

    def relay(r, part):
        up_landed(r, part)
        if r < 3 or part == 0:
            up(r + 1, part).start()
        down_landed(r, part)
        if r < 3 or part == 1:
            down(r + 1, part).start()
        e_copy(r - 1, part).start()
        e_copy(r + 2, part).start()

    def relay_end():
        up_landed(4, 0)
        e_copy(6, 0).start()
        down_landed(4, 1)
        e_copy(6, 1).start()

    def normed_copy():
        return remote(nw.at[c], nw.at[c], nsend.at[0], nrecv.at[0], sib)

    def section_rows(k, i):
        at = pl.ds(pl.multiple_of(lax.rem(i, 2) * 32, 32), 32)
        halves = [xs[2 * k + h, i // 2, at, :].astype(F32) for h in range(2)]
        return jnp.concatenate(halves, axis=1)

    def lane_sums(v):
        total = v[:, :128]
        for i in range(1, HALF // 128):
            total = total + v[:, i * 128 : (i + 1) * 128]
        return total

    def norm(k):
        @pl.loop(0, ROWS // 32)
        def _(i):
            rows = pl.ds(pl.multiple_of(i * 32, 32), 32)
            xf = section_rows(k, i)
            inv = lax.rsqrt(jnp.mean(xf * xf, axis=-1, keepdims=True) + EPS)
            iv[k, rows, :] = jnp.broadcast_to(inv, (32, 128))
            gp[0, rows, :] = (xf * inv).astype(BF16)

        @pl.when(k == s)
        def _():
            nw[c] = gp[0]
            normed_copy().start()

    def arrived(k):
        @pl.loop(0, 2)
        def _(uz):
            u = 2 * k + uz

            block = wa.at[2 * k + 1 - c, uz]
            remote(block, block, dsend.at[0], drecv.at[u], sib).wait_recv()
            z_block = wz.at[2 * k + 1 - c, uz]

            @pl.when(u == z)
            def _():
                remote(z_block, z_block, dsend.at[1], drecv.at[UNITS], sib).wait_recv()

            @pl.when(u != z)
            def _():
                d = lax.rem(u - z + 8, 8)
                slot = jnp.where(d < 4, 2 + d, jnp.where(d == 4, 6, 7 - d))
                remote(z_block, z_block, esend, erecv.at[slot], sib).wait_recv()

    def preact(k, h):
        w = jnp.concatenate([wa[2 * k + h].reshape(D, XY), wz[2 * k + h].reshape(D, Z)], axis=1)
        u = jnp.dot(gp[0], w, preferred_element_type=F32)
        uu = u * u
        t = jnp.tanh((GELU_C * u) * (1.0 + GELU_A * uu))
        cdf = 0.5 * (1.0 + t)
        slope = cdf + (0.5 * GELU_C) * u * (1.0 - t * t) * (1.0 + (3.0 * GELU_A) * uu)
        return u, cdf, slope

    def forward(k):
        arrived(k)

        @pl.loop(0, 2)
        def _(h):
            cols = part(h, 0, HALF)
            u, cdf, slope = preact(k, h)
            gd[k, :, cols] = slope
            ub[k, :, cols] = u.astype(BF16)
            before = xs[2 * k + h].reshape(ROWS, HALF)
            after = (before.astype(F32) + u * cdf).astype(BF16)
            xs[2 * k + 2 + h] = after.reshape(4, 64, HALF)

        pl.when(k < 2)(lambda: norm(jnp.minimum(k + 1, 2)))

    def forward_last():
        norm(3)
        arrived(3)
        sums = None
        for h in range(2):
            cols = pl.ds(h * HALF, HALF)
            u, _, slope = preact(3, h)
            pre = (gr[:, cols].astype(F32) * slope).astype(BF16)
            gp[1, :, cols] = pre
            term = lane_sums(pre.astype(F32) * u)
            sums = term if sums is None else sums + term
        ms[...] = sums

    own = unit(0)
    stage_p1(wz, own, UNITS)
    stage_p1(wa, own, own)
    raw_step(1)
    stage_p2(wz, own, UNITS)
    stage_p2(wa, own, own)
    raw_step(2)
    stage_q1(wz, own, UNITS)
    stage_q1(wa, own, own)
    for copy in in_x:
        copy.wait()
    for m in range(2):
        for q in range(2):
            rows = pl.ds(128 * m + 64 * q, 64)
            live = lax.broadcasted_iota(jnp.int32, (64, D), 0) < lens[m, q]
            gr[rows, :] = jnp.where(live, gr[rows, :].astype(F32), 0.0).astype(BF16)
    near = unit(1)
    stage_p1(wa, near, near)
    raw_step(3)
    stage_q2(wz, own, UNITS)
    stage_p2(wa, near, near)
    stage_f(wz, own, UNITS)
    for i in range(2):
        up(1, i).start()
        down(1, i).start()
    raw_step(4)
    third = unit(2)
    stage_p1(wa, third, third)
    norm(0)

    @pl.loop(1, UNITS + 2)
    def _(i):
        def when_unit(ahead, stage):
            @pl.when((i + ahead >= 0) & (i + ahead < UNITS))
            def _():
                u = unit(i + ahead)
                stage(wa, u, u)

        when_unit(0, stage_q1)
        when_unit(1, stage_p2)
        when_unit(-1, stage_q2)
        pl.when(i == 2)(lambda: raw_landed(4))
        when_unit(2, stage_p1)
        k = -1
        for section in range(4):
            for number, step in enumerate(READY[section]):
                k = jnp.where((s == section) & (i == step), number, k)
        pl.when(k >= 0)(lambda: forward(jnp.maximum(k, 0)))
        when_unit(-2, stage_f)
        pl.when(i == 2)(lambda: relay(1, 0))

        @pl.when(i == 3)
        def _():
            relay(1, 1)
            relay(2, 0)

        @pl.when(i == 4)
        def _():
            relay(2, 1)
            relay(3, 0)

        pl.when(i == 5)(lambda: relay(3, 1))
        pl.when(i == 6)(relay_end)

    done = jnp.int32(len(READY[0]))
    for section in range(1, 4):
        done = jnp.where(s == section, len(READY[section]), done)
    pl.loop(done, 3)(forward)
    forward_last()

    def backward_step(step, order, after_first):
        k = 3 - step
        now = lax.rem(step + 1, 2)
        inv = iv[k][:, :1]
        factor = inv * inv * (jnp.sum(ms[...], axis=-1, keepdims=True) * (1.0 / D))
        sums = None
        for j in order:
            tile = jnp.concatenate(
                [
                    w[2 * k + h, j].reshape(HALF, width)
                    for h in range(2)
                    for w, width in ((wa, XY), (wz, Z))
                ],
                axis=1,
            )
            g = lax.dot_general(
                gp[now], tile, (((1,), (1,)), ((), ())), preferred_element_type=F32
            )
            cols = part(j, 0, HALF)
            xf = xs[2 * k + j].reshape(ROWS, HALF).astype(F32)
            grad = (gr[:, cols].astype(F32) + inv * g - xf * factor).astype(BF16)
            gr[:, cols] = grad
            pre = (grad.astype(F32) * gd[k - 1, :, cols]).astype(BF16)
            gp[1 - now, :, cols] = pre
            if after_first is None:
                term = lane_sums(pre.astype(F32) * ub[k - 1, :, cols].astype(F32))
                sums = term if sums is None else sums + term
            elif j is order[0]:
                after_first()
        if sums is not None:
            ms[...] = sums

    last_gp = lax.rem(s, 2)

    def column_part(core, hc):
        return part(core, hc * QUART, QUART)

    def give_g(hc):
        return remote(
            gp.at[last_gp, :, column_part(1 - c, hc)], gw.at[c, :, CS[hc]],
            nsend.at[1 + hc], nrecv.at[1 + hc], sib,
        )

    def give():
        for hc in range(2):
            give_g(hc).start()

    pl.loop(0, 2 - jnp.minimum(s, 2))(lambda step: backward_step(step, (0, 1), None))
    pl.when(s < 3)(lambda: backward_step(2 - s, (1 - c, c), give))
    pl.when(s == 3)(give)
    for hc in range(2):
        gw[c, :, CS[hc]] = gp[last_gp, :, column_part(c, hc)]
    remote(nw.at[1 - c], nw.at[1 - c], nsend.at[0], nrecv.at[0], sib).wait_recv()

    v0, v1 = 1 - zl, zl
    v_of = (v0, v0, v1, v1)

    def weight_term(q):
        v, cs = v_of[q], CS[q % 2]

        @pl.loop(0, 2)
        def _(j):
            rows = pl.ds(pl.multiple_of(v * HALF + j * 512, 512), 512)
            left = nw[:, :, rows].reshape(2 * ROWS, 512)
            right = gw[:, :, cs].reshape(2 * ROWS, QUART)
            total = lax.dot_general(
                left, right, (((0,), (0,)), ((), ())), preferred_element_type=F32
            )
            xs[pl.ds(4 * v + 2 * j, 2), :, :, cs] = total.astype(BF16).reshape(2, 4, 64, QUART)

    def grow(cc, q, i, first=0, count=4):
        v, cs = v_of[q], CS[q % 2]
        if cc == 0:
            return xs.at[4 * v + i, pl.ds(first, count), :, cs]
        return xs.at[pl.ds(4 * v + first, count), i, :, cs]

    def gchip(cc, q, i, rows=None):
        v, cs = v_of[q], CS[q % 2]
        rows = pl.ds(0, 64) if rows is None else rows
        return xs.at[4 * v + y, i, rows, cs] if cc == 0 else xs.at[4 * v + i, x, rows, cs]

    def q_axis(cc):
        return (y, yp, ym, y2, dyp, dym) if cc == 0 else (x, xp, xm, x2, dxp, dxm)

    def p_axis(cc):
        return (x, xp, xm, x2, dxp, dxm) if cc == 0 else (y, yp, ym, y2, dyp, dym)

    def r1_copies(cc, q):
        _, _, _, far, to_plus, to_minus = q_axis(cc)
        return (
            remote(grow(cc, q, far, 0, 2), r1.at[q, 0], gsend.at[0], r1r.at[q, 0], to_plus),
            remote(grow(cc, q, far, 2, 2), r1.at[q, 1], gsend.at[0], r1r.at[q, 1], to_minus),
        )

    def r2_copies(cc, q):
        _, plus, minus, _, to_plus, to_minus = q_axis(cc)
        return (
            remote(grow(cc, q, plus), r2.at[q, 0], gsend.at[1], r2r.at[q], to_plus),
            remote(grow(cc, q, minus), r2.at[q, 1], gsend.at[1], r2r.at[q], to_minus),
        )

    def t1_copies(cc, q):
        _, _, _, far, to_plus, to_minus = p_axis(cc)
        return (
            remote(gchip(cc, q, far, TOP), t1.at[q, 0], gsend.at[2], t1r.at[q, 0], to_plus),
            remote(gchip(cc, q, far, BOTTOM), t1.at[q, 1], gsend.at[2], t1r.at[q, 1], to_minus),
        )

    def t2_copies(cc, q, way):
        _, plus, minus, _, to_plus, to_minus = p_axis(cc)
        block, dest = ((plus, to_plus), (minus, to_minus))[way]
        if q < 2:
            return [
                remote(gchip(cc, q, block), t2.at[q, way], gsend.at[3], t2r.at[q], dest)
            ]
        at = (block, y) if cc == 0 else (x, block)
        return [
            remote(
                gchip(cc, q, block, (TOP, BOTTOM)[core]), u2.at[q - 2, cc, way],
                gsend.at[4], u2r.at[q - 2], device(*at, z, core),
            )
            for core in range(2)
        ]

    def add_into(ref, *others):
        total = ref[...].astype(F32)
        for more in others:
            total = total + more[...].astype(F32)
        ref[...] = total.astype(BF16)

    def rs_a(q):
        def body(cc):
            for copy in r1_copies(cc, q):
                copy.start()

        by_core(body)

    def rs_b(q):
        def body(cc):
            _, plus, minus, _, _, _ = q_axis(cc)
            arrive, leave = r1_copies(cc, q), r2_copies(cc, q)
            arrive[0].wait_recv()
            add_into(grow(cc, q, plus, 0, 2), r1.at[q, 0])
            leave[0].start()
            arrive[1].wait_recv()
            add_into(grow(cc, q, minus, 2, 2), r1.at[q, 1])
            leave[1].start()

        by_core(body)

    def own_part(q):
        block = xs.at[4 * v_of[q] + y, x, sib_rows, CS[q % 2]]
        return remote(block, o1.at[q - 2], osend, orecv.at[q - 2], sib)

    def rs_c(q):
        def body(cc):
            me, plus, minus, far, _, _ = p_axis(cc)
            remote(r2.at[q], r2.at[q], gsend.at[1], r2r.at[q], sib).wait_recv()

            def add(i):
                add_into(gchip(cc, q, i), r2.at[q, 0, i], r2.at[q, 1, i])

            add(far)
            for copy in t1_copies(cc, q):
                copy.start()
            add(plus)
            add(minus)
            add(me)
            if q >= 2:
                own_part(q).start()

        by_core(body)

    def rs_d(q):
        def body(cc):
            _, plus, minus, _, _, _ = p_axis(cc)
            arrive = t1_copies(cc, q)
            arrive[0].wait_recv()
            add_into(gchip(cc, q, plus, TOP), t1.at[q, 0])
            for copy in t2_copies(cc, q, 0):
                copy.start()
            arrive[1].wait_recv()
            add_into(gchip(cc, q, minus, BOTTOM), t1.at[q, 1])
            for copy in t2_copies(cc, q, 1):
                copy.start()

        by_core(body)

    def cross(q, core):
        rows = (TOP, BOTTOM)[core]
        block = xs.at[4 * v0 + y, x, rows, CS[q]]
        dest = device(x, y, 2 * s + 1 - zl, core)
        return remote(block, z1.at[c, :, CS[q]], zsend, zrecv, dest)

    def rs_e(q):
        remote(t2.at[q], t2.at[q], gsend.at[3], t2r.at[q], sib).wait_recv()
        add_into(xs.at[4 * v0 + y, x, :, CS[q]], t2.at[q, 0], t2.at[q, 1])
        cross(q, 0).start()
        cross(q, 1).start()

    def finish(q):
        hc = q - 2
        remote(o1.at[hc], o1.at[hc], osend, orecv.at[hc], sib).wait_recv()
        remote(u2.at[hc], u2.at[hc], gsend.at[4], u2r.at[hc], sib).wait_recv()
        for core, own_ in ((c, xs[4 * v1 + y, x, my_rows, CS[hc]]), (1 - c, o1[hc])):
            total = own_.astype(F32) + z1[core, :, CS[hc]].astype(F32)
            for way in range(2):
                total = total + u2[hc, core, way].astype(F32)
            out_ref[:, column_part(core, hc)] = total

    for q in range(4):
        if q < 2:
            got = gw.at[1 - c, :, CS[q]]
            remote(got, got, nsend.at[1 + q], nrecv.at[1 + q], sib).wait_recv()
        weight_term(q)
        rs_a(q)

    def sent(block, sem):
        remote(block, block, sem, sem, sib).wait_send()

    for copy in gives(1 - c, my_rows):
        copy.wait_send()
    for way in range(2):
        sent(wa.at[pl.ds(0, 7), 0, 0, 0, TOP], rsend.at[way])
    sent(wa.at[0, :, pl.ds(0, 3)], psend.at[0])
    sent(wz.at[0, 0, 0, pl.ds(0, 3)], psend.at[1])
    sent(wa.at[pl.ds(0, 3)], qsend.at[0])
    sent(wz.at[0, 0, pl.ds(0, 3)], qsend.at[1])
    sent(wa.at[pl.ds(0, 4)], dsend.at[0])
    sent(wz.at[0, 0], dsend.at[1])
    sent(wz.at[pl.ds(0, 7), 0, pl.ds(0, 2)], usend)
    sent(wz.at[pl.ds(0, 7), 0, pl.ds(0, 2)], lsend)
    sent(wz.at[pl.ds(0, 7), :, pl.ds(0, 2)], esend)

    for q in range(4):
        rs_b(q)
    rs_c(0)
    rs_c(1)
    rs_d(0)
    rs_c(2)
    rs_d(1)
    rs_e(0)
    rs_c(3)
    rs_d(2)
    rs_e(1)
    rs_d(3)
    remote(z1, z1, zsend, zrecv, sib).wait_recv()
    finish(2)
    finish(3)

    sent(o1, osend)
    sent(z1, zsend)
    give_g(0).wait_send()
    give_g(1).wait_send()
    normed_copy().wait_send()
    sent(r1, gsend.at[0])
    sent(r2, gsend.at[1])
    sent(t1, gsend.at[2])
    sent(t2, gsend.at[3])
    sent(u2, gsend.at[4])


def local(inputs, weights, cotangents, lengths):
    rows = inputs.shape[0] * inputs.shape[1]
    dma = pltpu.SemaphoreType.DMA
    vmem = pl.BlockSpec(memory_space=pltpu.VMEM)
    out = pl.pallas_call(
        kernel,
        out_shape=jax.ShapeDtypeStruct((32, D), F32),
        in_specs=[
            pl.BlockSpec(memory_space=pl.ANY),
            vmem,
            pl.BlockSpec(memory_space=pl.ANY),
            pl.BlockSpec(memory_space=pl.ANY),
        ],
        out_specs=vmem,
        scratch_shapes=[
            pltpu.VMEM((8, 2, 4, 4, 64, XY), BF16),
            pltpu.VMEM((8, 2, 4, 4, 64, Z), BF16),
            pltpu.VMEM((8, 4, 64, HALF), BF16),
            pltpu.VMEM((3, ROWS, D), F32),
            pltpu.VMEM((3, ROWS, D), BF16),
            pltpu.VMEM((4, ROWS, 128), F32),
            pltpu.VMEM((2, ROWS, D), BF16),
            pltpu.VMEM((2, ROWS, D), BF16),
            pltpu.VMEM((2, ROWS, HALF), BF16),
            pltpu.VMEM((ROWS, D), BF16),
            pltpu.VMEM((ROWS, 128), F32),
            pltpu.VMEM((4, 2, 2, 64, QUART), BF16),
            pltpu.VMEM((4, 2, 4, 64, QUART), BF16),
            pltpu.VMEM((4, 2, 32, QUART), BF16),
            pltpu.VMEM((2, 2, 64, QUART), BF16),
            pltpu.VMEM((2, 2, 2, 32, QUART), BF16),
            pltpu.VMEM((2, 32, HALF), BF16),
            pltpu.VMEM((2, 32, QUART), BF16),
            pltpu.SMEM((2, 2), jnp.int32),
            dma((6,)),
            dma((2,)),
            dma((2,)),
            dma((2,)),
            dma((2, 4)),
            dma,
            dma((4, 2)),
            dma,
            dma((4, 2)),
            dma,
            dma((7,)),
            dma((2,)),
            dma((9, 3)),
            dma((2,)),
            dma((9, 4)),
            dma((2,)),
            dma((9,)),
            dma((3,)),
            dma((3,)),
            dma((5,)),
            dma((4, 2)),
            dma((4,)),
            dma((4, 2)),
            dma((2,)),
            dma((2,)),
            dma,
            dma,
            dma,
            dma((2,)),
        ],
        compiler_params=pltpu.CompilerParams(
            collective_id=0, has_side_effects=True, vmem_limit_bytes=63 * 2**20
        ),
        cost_estimate=pl.CostEstimate(
            flops=9 * 2 * ROWS * D * D, bytes_accessed=36 * 2**20, transcendentals=4 * ROWS * D
        ),
    )(inputs.reshape(4, rows // 4, D), weights[0], cotangents.reshape(rows, D), lengths)
    return out[None]


def solution(mesh):
    in_specs = (
        P(None, "fsdp", None),
        P("section", "fsdp", None),
        P(None, "fsdp", None),
        P(None, "fsdp"),
    )
    out_specs = P("section", "fsdp", None)
    return jax.shard_map(local, mesh=mesh, in_specs=in_specs, out_specs=out_specs, check_vma=False)
```

```python
import functools

import jax
import jax.numpy as jnp
from jax import lax
from jax.experimental import pallas as pl
from jax.experimental.pallas import tpu as pltpu
from jax.sharding import PartitionSpec as P

MESH = pl.DeviceIdType.MESH
F32 = jnp.float32
BF16 = jnp.bfloat16
EPS = 1e-06
GELU_C = 0.7978845608028654
GELU_A = 0.044715

D = 2048
ROWS = 256
HALF = 1024
QUART = 512
CS = (pl.ds(0, QUART), pl.ds(QUART, QUART))
XY = 768
Z = HALF - XY
UNITS = 8
READY = ((4, 6, 8), (6, 7, 8), (8, 9), (6, 8))
FIRST, SECOND = pl.ds(0, 2), pl.ds(2, 2)
TOP, BOTTOM = pl.ds(0, 32), pl.ds(32, 32)


def position():
    s, f = lax.axis_index("section"), lax.axis_index("fsdp")
    c = lax.rem(f, 2)
    x = lax.rem(f // 2, 4)
    y = lax.rem(f // 8, 4)
    zl = f // 32
    return s, zl, x, y, c


def device(x, y, z, c):
    return (z // 2, lax.rem(z, 2) * 32 + y * 8 + x * 2 + c)


def remote(src, dst, send, recv, dev):
    return pltpu.make_async_remote_copy(
        src_ref=src, dst_ref=dst, send_sem=send, recv_sem=recv, device_id=dev, device_id_type=MESH
    )


def kernel(
    x_ref, w_ref, cot_ref, len_ref, out_ref,
    wa, wz, xs, gd, ub, iv, gp, nw, gw, gr, ms, r1, r2, t1, t2, u2, z1, o1,
    lens, loc, xsend, xrecv, rsend, rrecv, usend, urecv, lsend, lrecv, esend, erecv,
    psend, precv, qsend, qrecv, dsend, drecv,
    nsend, nrecv, gsend, r1r, r2r, t1r, t2r, u2r, zsend, zrecv, osend, orecv,
):
    s, zl, x, y, c = position()
    z = 2 * s + zl
    sib = device(x, y, z, 1 - c)
    xp, xm = lax.rem(x + 1, 4), lax.rem(x + 3, 4)
    yp, ym = lax.rem(y + 1, 4), lax.rem(y + 3, 4)
    x2, y2 = lax.rem(x + 2, 4), lax.rem(y + 2, 4)
    dxp, dxm = device(xp, y, z, c), device(xm, y, z, c)
    dyp, dym = device(x, yp, z, c), device(x, ym, z, c)

    barrier = pltpu.get_barrier_semaphore()
    above, below = device(x, y, lax.rem(z + 1, 8), c), device(x, y, lax.rem(z + 7, 8), c)
    pair_other = device(x, y, 2 * s + 1 - zl, 1 - c)
    def crossed(plus):
        return device(
            jnp.where(c == 0, x, xp if plus else xm), jnp.where(c == 0, yp if plus else ym, y), z, 1 - c
        )

    cross_plus, cross_minus = crossed(True), crossed(False)
    for partner in (dxp, dxm, dyp, dym, above, below, sib, pair_other, cross_plus, cross_minus):
        pl.semaphore_signal(barrier, inc=1, device_id=partner, device_id_type=MESH)

    def part(core, first, width):
        return pl.ds(pl.multiple_of(core * HALF + first, 256), width)

    in_x = [
        pltpu.make_async_copy(x_ref.at[:, :, h * HALF : (h + 1) * HALF], xs.at[h], loc.at[3 * h])
        for h in range(2)
    ]
    in_x.append(pltpu.make_async_copy(cot_ref, gr, loc.at[4]))
    in_x.append(pltpu.make_async_copy(len_ref, lens, loc.at[5]))
    for copy in in_x:
        copy.start()
    mine = pl.ds(pl.multiple_of(c * HALF, HALF), HALF)
    other = pl.ds(pl.multiple_of((1 - c) * HALF, HALF), HALF)
    my_rows = pl.ds(pl.multiple_of(c * 32, 32), 32)
    sib_rows = pl.ds(pl.multiple_of((1 - c) * 32, 32), 32)
    in_w = [
        pltpu.make_async_copy(src, dst, loc.at[1 + i])
        for i, (src, dst) in enumerate(
            (
                (w_ref.at[:, part(c, 0, XY)], wa.at[2 * s + c, zl, y, x, my_rows]),
                (w_ref.at[:, part(c, XY, Z)], wz.at[2 * s + c, zl, y, x, my_rows]),
            )
        )
    ]
    for copy in in_w:
        copy.start()
    pl.semaphore_wait(barrier, 10)

    def gives(core, rows):
        kh = 2 * s + core
        return (
            remote(
                w_ref.at[:, part(core, XY, Z)], wz.at[kh, zl, y, x, rows],
                xsend.at[0], xrecv.at[0], sib,
            ),
            remote(
                w_ref.at[:, part(core, 0, XY)], wa.at[kh, zl, y, x, rows],
                xsend.at[1], xrecv.at[1], sib,
            ),
        )

    for copy in gives(1 - c, my_rows):
        copy.start()
    for copy in in_w:
        copy.wait()
    for copy in gives(c, sib_rows):
        copy.wait_recv()

    def raw_block(d, half=None):
        v = lax.rem(z + 8 + d, 8)
        at = (2 * (v // 2) + c, lax.rem(v, 2), y, x)
        return wa.at[at] if half is None else wa.at[at + (half,)]

    def raw_up(r, half=None):
        block = raw_block(1 - r, half)
        return remote(block, block, rsend.at[0], rrecv.at[0, r - 1], above)

    def raw_down(r, half=None):
        block = raw_block(r - 1, half)
        return remote(block, block, rsend.at[1], rrecv.at[1, r - 1], below)

    def raw_landed(r):
        ups, downs = raw_block(-r, TOP if r == 4 else None), raw_block(r, BOTTOM if r == 4 else None)
        remote(ups, ups, rsend.at[0], rrecv.at[0, r - 1], above).wait_recv()
        remote(downs, downs, rsend.at[1], rrecv.at[1, r - 1], below).wait_recv()

    def raw_step(r):
        if r > 1:
            raw_landed(r - 1)
        raw_up(r, TOP if r == 4 else None).start()
        raw_down(r, BOTTOM if r == 4 else None).start()

    def row(w, cc, kh, uz, i, part=None):
        if cc == 0:
            return w.at[kh, uz, i] if part is None else w.at[kh, uz, i, part]
        return w.at[kh, uz, :, i] if part is None else w.at[kh, uz, part, i]

    def chip(w, cc, kh, uz, i, part=None):
        at = (kh, uz, y, i) if cc == 0 else (kh, uz, i, x)
        return w.at[at] if part is None else w.at[at + (part,)]

    def p_copies(w, cc, u, b):
        fam = 0 if w is wa else 1
        kh, uz = 2 * (u // 2) + cc, lax.rem(u, 2)
        me, plus, minus = (x, xp, xm) if cc == 0 else (y, yp, ym)
        to_plus, to_minus = (dxp, dxm) if cc == 0 else (dyp, dym)
        own = chip(w, cc, kh, uz, me)
        from_minus, from_plus = chip(w, cc, kh, uz, minus, TOP), chip(w, cc, kh, uz, plus, BOTTOM)
        return (
            remote(own, own, psend.at[fam], precv.at[b, 0], to_plus),
            remote(own, own, psend.at[fam], precv.at[b, 1], to_minus),
            remote(from_minus, from_minus, psend.at[fam], precv.at[b, 2], to_plus),
            remote(from_plus, from_plus, psend.at[fam], precv.at[b, 2], to_minus),
        )

    def p_landed(w, cc, u, b, i):
        kh, uz = 2 * (u // 2) + cc, lax.rem(u, 2)
        plus, minus, far = (xp, xm, x2) if cc == 0 else (yp, ym, y2)
        land = (
            chip(w, cc, kh, uz, minus),
            chip(w, cc, kh, uz, plus),
            chip(w, cc, kh, uz, far),
        )[i]
        remote(land, land, psend.at[0], precv.at[b, i], sib).wait_recv()

    def q_copies(w, cc, u, b):
        fam = 0 if w is wa else 1
        kh, uz = 2 * (u // 2) + cc, lax.rem(u, 2)
        me, plus, minus = (y, yp, ym) if cc == 0 else (x, xp, xm)
        to_plus, to_minus = (dyp, dym) if cc == 0 else (dxp, dxm)
        first, second = row(w, cc, kh, uz, me, FIRST), row(w, cc, kh, uz, me, SECOND)
        from_minus, from_plus = row(w, cc, kh, uz, minus, FIRST), row(w, cc, kh, uz, plus, SECOND)
        return (
            remote(first, first, qsend.at[fam], qrecv.at[b, 0], to_plus),
            remote(second, second, qsend.at[fam], qrecv.at[b, 1], to_minus),
            remote(second, second, qsend.at[fam], qrecv.at[b, 2], to_plus),
            remote(first, first, qsend.at[fam], qrecv.at[b, 2], to_minus),
            remote(from_minus, from_minus, qsend.at[fam], qrecv.at[b, 3], to_plus),
            remote(from_plus, from_plus, qsend.at[fam], qrecv.at[b, 3], to_minus),
        )

    def q_landed(w, cc, u, b, i):
        kh, uz = 2 * (u // 2) + cc, lax.rem(u, 2)
        plus, minus, far = (yp, ym, y2) if cc == 0 else (xp, xm, x2)
        land = (
            row(w, cc, kh, uz, minus, FIRST),
            row(w, cc, kh, uz, plus, SECOND),
            row(w, cc, kh, uz, far),
            row(w, cc, kh, uz, far),
        )[i]
        remote(land, land, qsend.at[0], qrecv.at[b, i], sib).wait_recv()

    def d_copy(w, cc, u, b, i):
        kh, uz = 2 * (u // 2) + cc, lax.rem(u, 2)
        at = ((y, ym, yp, y2) if cc == 0 else (x, xm, xp, x2))[i]
        block = row(w, cc, kh, uz, at)
        return remote(block, block, dsend.at[0 if w is wa else 1], drecv.at[b], sib)

    def by_core(body):
        for cc in (0, 1):
            pl.when(c == cc)(functools.partial(body, cc))

    def unit(t):
        rest = t - 2
        near = jnp.where(rest < 2, rest + 2, jnp.where(rest < 4, rest - 2, rest + 2))
        rest = jnp.where(s == 2, near, jnp.where(rest < 2 * s, rest, rest + 2))
        return jnp.where(t == 0, z, jnp.where(t == 1, 2 * s + 1 - zl, rest))

    def stage_p1(w, u, b):
        def body(cc):
            copies = p_copies(w, cc, u, b)
            copies[0].start()
            copies[1].start()

        by_core(body)

    def stage_p2(w, u, b):
        def body(cc):
            copies = p_copies(w, cc, u, b)
            p_landed(w, cc, u, b, 0)
            copies[2].start()
            p_landed(w, cc, u, b, 1)
            copies[3].start()

        by_core(body)

    def stage_q1(w, u, b):
        def body(cc):
            copies = q_copies(w, cc, u, b)
            p_landed(w, cc, u, b, 2)
            for copy in copies[:4]:
                copy.start()
            d_copy(w, cc, u, b, 0).start()

        by_core(body)

    def stage_q2(w, u, b):
        def body(cc):
            copies = q_copies(w, cc, u, b)
            q_landed(w, cc, u, b, 0)
            copies[4].start()
            q_landed(w, cc, u, b, 1)
            copies[5].start()

        by_core(body)

    def stage_f(w, u, b):
        def body(cc):
            q_landed(w, cc, u, b, 2)
            d_copy(w, cc, u, b, 1).start()
            d_copy(w, cc, u, b, 2).start()
            q_landed(w, cc, u, b, 3)
            d_copy(w, cc, u, b, 3).start()

        by_core(body)

    PARTS = (pl.ds(0, 2), pl.ds(2, 2))
    def plane(d, part, core=None):
        v = lax.rem(z + 8 + d, 8)
        core = c if core is None else core
        return wz.at[2 * (v // 2) + core, lax.rem(v, 2), PARTS[part]]

    def up(r, part):
        block = plane(1 - r, part)
        return remote(block, block, usend, urecv.at[r - 1, part], above)

    def down(r, part):
        block = plane(r - 1, part)
        return remote(block, block, lsend, lrecv.at[r - 1, part], below)

    def up_landed(r, part):
        block = plane(-r, part)
        remote(block, block, usend, urecv.at[r - 1, part], above).wait_recv()

    def down_landed(r, part):
        block = plane(r, part)
        remote(block, block, lsend, lrecv.at[r - 1, part], below).wait_recv()

    def e_copy(slot, part):
        d = (-1, -2, -3, 1, 2, 3, 4)[slot]
        block = plane(d, part)
        return remote(block, block, esend, erecv.at[slot], sib)

    def relay(r, part):
        up_landed(r, part)
        if r < 3 or part == 0:
            up(r + 1, part).start()
        down_landed(r, part)
        if r < 3 or part == 1:
            down(r + 1, part).start()
        e_copy(r - 1, part).start()
        e_copy(r + 2, part).start()

    def relay_end():
        up_landed(4, 0)
        e_copy(6, 0).start()
        down_landed(4, 1)
        e_copy(6, 1).start()

    def normed_copy():
        return remote(nw.at[c], nw.at[c], nsend.at[0], nrecv.at[0], sib)

    def section_rows(k, i):
        at = pl.ds(pl.multiple_of(lax.rem(i, 2) * 32, 32), 32)
        halves = [xs[2 * k + h, i // 2, at, :].astype(F32) for h in range(2)]
        return jnp.concatenate(halves, axis=1)

    def lane_sums(v):
        total = v[:, :128]
        for i in range(1, HALF // 128):
            total = total + v[:, i * 128 : (i + 1) * 128]
        return total

    def norm(k):
        @pl.loop(0, ROWS // 32)
        def _(i):
            rows = pl.ds(pl.multiple_of(i * 32, 32), 32)
            xf = section_rows(k, i)
            inv = lax.rsqrt(jnp.mean(xf * xf, axis=-1, keepdims=True) + EPS)
            iv[k, rows, :] = jnp.broadcast_to(inv, (32, 128))
            gp[0, rows, :] = (xf * inv).astype(BF16)

        @pl.when(k == s)
        def _():
            nw[c] = gp[0]
            normed_copy().start()

    def arrived(k):
        @pl.loop(0, 2)
        def _(uz):
            u = 2 * k + uz

            block = wa.at[2 * k + 1 - c, uz]
            remote(block, block, dsend.at[0], drecv.at[u], sib).wait_recv()
            z_block = wz.at[2 * k + 1 - c, uz]

            @pl.when(u == z)
            def _():
                remote(z_block, z_block, dsend.at[1], drecv.at[UNITS], sib).wait_recv()

            @pl.when(u != z)
            def _():
                d = lax.rem(u - z + 8, 8)
                slot = jnp.where(d < 4, 2 + d, jnp.where(d == 4, 6, 7 - d))
                remote(z_block, z_block, esend, erecv.at[slot], sib).wait_recv()

    def preact(k, h):
        w = jnp.concatenate([wa[2 * k + h].reshape(D, XY), wz[2 * k + h].reshape(D, Z)], axis=1)
        u = jnp.dot(gp[0], w, preferred_element_type=F32)
        uu = u * u
        t = jnp.tanh((GELU_C * u) * (1.0 + GELU_A * uu))
        cdf = 0.5 * (1.0 + t)
        slope = cdf + (0.5 * GELU_C) * u * (1.0 - t * t) * (1.0 + (3.0 * GELU_A) * uu)
        return u, cdf, slope

    def forward(k):
        arrived(k)

        @pl.loop(0, 2)
        def _(h):
            cols = part(h, 0, HALF)
            u, cdf, slope = preact(k, h)
            gd[k, :, cols] = slope
            ub[k, :, cols] = u.astype(BF16)
            before = xs[2 * k + h].reshape(ROWS, HALF)
            after = (before.astype(F32) + u * cdf).astype(BF16)
            xs[2 * k + 2 + h] = after.reshape(4, 64, HALF)

        pl.when(k < 2)(lambda: norm(jnp.minimum(k + 1, 2)))

    def forward_last():
        norm(3)
        arrived(3)
        sums = None
        for h in range(2):
            cols = pl.ds(h * HALF, HALF)
            u, _, slope = preact(3, h)
            pre = (gr[:, cols].astype(F32) * slope).astype(BF16)
            gp[1, :, cols] = pre
            term = lane_sums(pre.astype(F32) * u)
            sums = term if sums is None else sums + term
        ms[...] = sums

    own = unit(0)
    stage_p1(wz, own, UNITS)
    stage_p1(wa, own, own)
    raw_step(1)
    stage_p2(wz, own, UNITS)
    stage_p2(wa, own, own)
    raw_step(2)
    stage_q1(wz, own, UNITS)
    stage_q1(wa, own, own)
    near = unit(1)
    stage_p1(wa, near, near)
    raw_step(3)
    stage_q2(wz, own, UNITS)
    stage_p2(wa, near, near)
    stage_f(wz, own, UNITS)
    for i in range(2):
        up(1, i).start()
        down(1, i).start()
    raw_step(4)
    third = unit(2)
    stage_p1(wa, third, third)

    @pl.loop(1, UNITS + 2)
    def _(i):
        def when_unit(ahead, stage):
            @pl.when((i + ahead >= 0) & (i + ahead < UNITS))
            def _():
                u = unit(i + ahead)
                stage(wa, u, u)

        when_unit(0, stage_q1)
        when_unit(1, stage_p2)
        when_unit(-1, stage_q2)
        pl.when(i == 2)(lambda: raw_landed(4))
        when_unit(2, stage_p1)
        k = -1
        for section in range(4):
            for number, step in enumerate(READY[section]):
                k = jnp.where((s == section) & (i == step), number, k)
        pl.when(k >= 0)(lambda: forward(jnp.maximum(k, 0)))
        when_unit(-2, stage_f)
        @pl.when(i == 1)
        def _():
            for copy in in_x:
                copy.wait()
            for m in range(2):
                for q in range(2):
                    rows = pl.ds(128 * m + 64 * q, 64)
                    live = lax.broadcasted_iota(jnp.int32, (64, D), 0) < lens[m, q]
                    gr[rows, :] = jnp.where(live, gr[rows, :].astype(F32), 0.0).astype(BF16)
            norm(0)

        pl.when(i == 2)(lambda: relay(1, 0))

        @pl.when(i == 3)
        def _():
            relay(1, 1)
            relay(2, 0)

        @pl.when(i == 4)
        def _():
            relay(2, 1)
            relay(3, 0)

        pl.when(i == 5)(lambda: relay(3, 1))
        pl.when(i == 6)(relay_end)

    done = jnp.int32(len(READY[0]))
    for section in range(1, 4):
        done = jnp.where(s == section, len(READY[section]), done)
    pl.loop(done, 3)(forward)
    forward_last()

    def backward_step(step, order, after_first):
        k = 3 - step
        now = lax.rem(step + 1, 2)
        inv = iv[k][:, :1]
        factor = inv * inv * (jnp.sum(ms[...], axis=-1, keepdims=True) * (1.0 / D))
        sums = None
        for j in order:
            tile = jnp.concatenate(
                [
                    w[2 * k + h, j].reshape(HALF, width)
                    for h in range(2)
                    for w, width in ((wa, XY), (wz, Z))
                ],
                axis=1,
            )
            g = lax.dot_general(
                gp[now], tile, (((1,), (1,)), ((), ())), preferred_element_type=F32
            )
            cols = part(j, 0, HALF)
            xf = xs[2 * k + j].reshape(ROWS, HALF).astype(F32)
            grad = (gr[:, cols].astype(F32) + inv * g - xf * factor).astype(BF16)
            gr[:, cols] = grad
            pre = (grad.astype(F32) * gd[k - 1, :, cols]).astype(BF16)
            gp[1 - now, :, cols] = pre
            if after_first is None:
                term = lane_sums(pre.astype(F32) * ub[k - 1, :, cols].astype(F32))
                sums = term if sums is None else sums + term
            elif j is order[0]:
                after_first()
        if sums is not None:
            ms[...] = sums

    last_gp = lax.rem(s, 2)

    def column_part(core, hc):
        return part(core, hc * QUART, QUART)

    def give_g(hc):
        return remote(
            gp.at[last_gp, :, column_part(1 - c, hc)], gw.at[c, :, CS[hc]],
            nsend.at[1 + hc], nrecv.at[1 + hc], sib,
        )

    def give():
        for hc in range(2):
            give_g(hc).start()

    pl.loop(0, 2 - jnp.minimum(s, 2))(lambda step: backward_step(step, (0, 1), None))
    pl.when(s < 3)(lambda: backward_step(2 - s, (1 - c, c), give))
    pl.when(s == 3)(give)
    for hc in range(2):
        gw[c, :, CS[hc]] = gp[last_gp, :, column_part(c, hc)]
    remote(nw.at[1 - c], nw.at[1 - c], nsend.at[0], nrecv.at[0], sib).wait_recv()

    v0, v1 = 1 - zl, zl
    v_of = (v0, v0, v1, v1)

    def weight_term(q):
        v, cs = v_of[q], CS[q % 2]

        @pl.loop(0, 2)
        def _(j):
            rows = pl.ds(pl.multiple_of(v * HALF + j * 512, 512), 512)
            left = nw[:, :, rows].reshape(2 * ROWS, 512)
            right = gw[:, :, cs].reshape(2 * ROWS, QUART)
            total = lax.dot_general(
                left, right, (((0,), (0,)), ((), ())), preferred_element_type=F32
            )
            xs[pl.ds(4 * v + 2 * j, 2), :, :, cs] = total.astype(BF16).reshape(2, 4, 64, QUART)

    def grow(cc, q, i, first=0, count=4):
        v, cs = v_of[q], CS[q % 2]
        if cc == 0:
            return xs.at[4 * v + i, pl.ds(first, count), :, cs]
        return xs.at[pl.ds(4 * v + first, count), i, :, cs]

    def gchip(cc, q, i, rows=None):
        v, cs = v_of[q], CS[q % 2]
        rows = pl.ds(0, 64) if rows is None else rows
        return xs.at[4 * v + y, i, rows, cs] if cc == 0 else xs.at[4 * v + i, x, rows, cs]

    def q_axis(cc):
        return (y, yp, ym, y2, dyp, dym) if cc == 0 else (x, xp, xm, x2, dxp, dxm)

    def p_axis(cc):
        return (x, xp, xm, x2, dxp, dxm) if cc == 0 else (y, yp, ym, y2, dyp, dym)

    def r1_copies(cc, q):
        _, _, _, far, to_plus, to_minus = q_axis(cc)
        return (
            remote(grow(cc, q, far, 0, 2), r1.at[q, 0], gsend.at[0], r1r.at[q, 0], to_plus),
            remote(grow(cc, q, far, 2, 2), r1.at[q, 1], gsend.at[0], r1r.at[q, 1], to_minus),
        )

    def r2_copies(cc, q):
        _, plus, minus, _, to_plus, to_minus = q_axis(cc)
        return (
            remote(grow(cc, q, plus), r2.at[q, 0], gsend.at[1], r2r.at[q], to_plus),
            remote(grow(cc, q, minus), r2.at[q, 1], gsend.at[1], r2r.at[q], to_minus),
        )

    def t1_copies(cc, q):
        _, _, _, far, to_plus, to_minus = p_axis(cc)
        return (
            remote(gchip(cc, q, far, TOP), t1.at[q, 0], gsend.at[2], t1r.at[q, 0], to_plus),
            remote(gchip(cc, q, far, BOTTOM), t1.at[q, 1], gsend.at[2], t1r.at[q, 1], to_minus),
        )

    def t2_copies(cc, q, way):
        _, plus, minus, _, to_plus, to_minus = p_axis(cc)
        block, dest = ((plus, to_plus), (minus, to_minus))[way]
        if q < 2:
            return [
                remote(gchip(cc, q, block), t2.at[q, way], gsend.at[3], t2r.at[q], dest)
            ]
        at = (block, y) if cc == 0 else (x, block)
        return [
            remote(
                gchip(cc, q, block, (TOP, BOTTOM)[core]), u2.at[q - 2, cc, way],
                gsend.at[4], u2r.at[q - 2], device(*at, z, core),
            )
            for core in range(2)
        ]

    def add_into(ref, *others):
        total = ref[...].astype(F32)
        for more in others:
            total = total + more[...].astype(F32)
        ref[...] = total.astype(BF16)

    def rs_a(q):
        def body(cc):
            for copy in r1_copies(cc, q):
                copy.start()

        by_core(body)

    def rs_b(q):
        def body(cc):
            _, plus, minus, _, _, _ = q_axis(cc)
            arrive, leave = r1_copies(cc, q), r2_copies(cc, q)
            arrive[0].wait_recv()
            add_into(grow(cc, q, plus, 0, 2), r1.at[q, 0])
            leave[0].start()
            arrive[1].wait_recv()
            add_into(grow(cc, q, minus, 2, 2), r1.at[q, 1])
            leave[1].start()

        by_core(body)

    def own_part(q):
        block = xs.at[4 * v_of[q] + y, x, sib_rows, CS[q % 2]]
        return remote(block, o1.at[q - 2], osend, orecv.at[q - 2], sib)

    def rs_c(q):
        def body(cc):
            me, plus, minus, far, _, _ = p_axis(cc)
            remote(r2.at[q], r2.at[q], gsend.at[1], r2r.at[q], sib).wait_recv()

            def add(i):
                add_into(gchip(cc, q, i), r2.at[q, 0, i], r2.at[q, 1, i])

            add(far)
            for copy in t1_copies(cc, q):
                copy.start()
            add(plus)
            add(minus)
            add(me)
            if q >= 2:
                own_part(q).start()

        by_core(body)

    def rs_d(q):
        def body(cc):
            _, plus, minus, _, _, _ = p_axis(cc)
            arrive = t1_copies(cc, q)
            arrive[0].wait_recv()
            add_into(gchip(cc, q, plus, TOP), t1.at[q, 0])
            for copy in t2_copies(cc, q, 0):
                copy.start()
            arrive[1].wait_recv()
            add_into(gchip(cc, q, minus, BOTTOM), t1.at[q, 1])
            for copy in t2_copies(cc, q, 1):
                copy.start()

        by_core(body)

    def cross(q, core):
        rows = (TOP, BOTTOM)[core]
        block = xs.at[4 * v0 + y, x, rows, CS[q]]
        dest = device(x, y, 2 * s + 1 - zl, core)
        return remote(block, z1.at[c, :, CS[q]], zsend, zrecv, dest)

    def rs_e(q):
        remote(t2.at[q], t2.at[q], gsend.at[3], t2r.at[q], sib).wait_recv()
        add_into(xs.at[4 * v0 + y, x, :, CS[q]], t2.at[q, 0], t2.at[q, 1])
        cross(q, 0).start()
        cross(q, 1).start()

    def finish(q):
        hc = q - 2
        remote(o1.at[hc], o1.at[hc], osend, orecv.at[hc], sib).wait_recv()
        remote(u2.at[hc], u2.at[hc], gsend.at[4], u2r.at[hc], sib).wait_recv()
        for core, own_ in ((c, xs[4 * v1 + y, x, my_rows, CS[hc]]), (1 - c, o1[hc])):
            total = own_.astype(F32) + z1[core, :, CS[hc]].astype(F32)
            for way in range(2):
                total = total + u2[hc, core, way].astype(F32)
            out_ref[:, column_part(core, hc)] = total

    for q in range(4):
        if q < 2:
            got = gw.at[1 - c, :, CS[q]]
            remote(got, got, nsend.at[1 + q], nrecv.at[1 + q], sib).wait_recv()
        weight_term(q)
        rs_a(q)

    def sent(block, sem):
        remote(block, block, sem, sem, sib).wait_send()

    for copy in gives(1 - c, my_rows):
        copy.wait_send()
    for way in range(2):
        sent(wa.at[pl.ds(0, 7), 0, 0, 0, TOP], rsend.at[way])
    sent(wa.at[0, :, pl.ds(0, 3)], psend.at[0])
    sent(wz.at[0, 0, 0, pl.ds(0, 3)], psend.at[1])
    sent(wa.at[pl.ds(0, 3)], qsend.at[0])
    sent(wz.at[0, 0, pl.ds(0, 3)], qsend.at[1])
    sent(wa.at[pl.ds(0, 4)], dsend.at[0])
    sent(wz.at[0, 0], dsend.at[1])
    sent(wz.at[pl.ds(0, 7), 0, pl.ds(0, 2)], usend)
    sent(wz.at[pl.ds(0, 7), 0, pl.ds(0, 2)], lsend)
    sent(wz.at[pl.ds(0, 7), :, pl.ds(0, 2)], esend)

    for q in range(4):
        rs_b(q)
    rs_c(0)
    rs_c(1)
    rs_d(0)
    rs_c(2)
    rs_d(1)
    rs_e(0)
    rs_c(3)
    rs_d(2)
    rs_e(1)
    rs_d(3)
    remote(z1, z1, zsend, zrecv, sib).wait_recv()
    finish(2)
    finish(3)

    sent(o1, osend)
    sent(z1, zsend)
    give_g(0).wait_send()
    give_g(1).wait_send()
    normed_copy().wait_send()
    sent(r1, gsend.at[0])
    sent(r2, gsend.at[1])
    sent(t1, gsend.at[2])
    sent(t2, gsend.at[3])
    sent(u2, gsend.at[4])


def local(inputs, weights, cotangents, lengths):
    rows = inputs.shape[0] * inputs.shape[1]
    dma = pltpu.SemaphoreType.DMA
    vmem = pl.BlockSpec(memory_space=pltpu.VMEM)
    out = pl.pallas_call(
        kernel,
        out_shape=jax.ShapeDtypeStruct((32, D), F32),
        in_specs=[
            pl.BlockSpec(memory_space=pl.ANY),
            vmem,
            pl.BlockSpec(memory_space=pl.ANY),
            pl.BlockSpec(memory_space=pl.ANY),
        ],
        out_specs=vmem,
        scratch_shapes=[
            pltpu.VMEM((8, 2, 4, 4, 64, XY), BF16),
            pltpu.VMEM((8, 2, 4, 4, 64, Z), BF16),
            pltpu.VMEM((8, 4, 64, HALF), BF16),
            pltpu.VMEM((3, ROWS, D), F32),
            pltpu.VMEM((3, ROWS, D), BF16),
            pltpu.VMEM((4, ROWS, 128), F32),
            pltpu.VMEM((2, ROWS, D), BF16),
            pltpu.VMEM((2, ROWS, D), BF16),
            pltpu.VMEM((2, ROWS, HALF), BF16),
            pltpu.VMEM((ROWS, D), BF16),
            pltpu.VMEM((ROWS, 128), F32),
            pltpu.VMEM((4, 2, 2, 64, QUART), BF16),
            pltpu.VMEM((4, 2, 4, 64, QUART), BF16),
            pltpu.VMEM((4, 2, 32, QUART), BF16),
            pltpu.VMEM((2, 2, 64, QUART), BF16),
            pltpu.VMEM((2, 2, 2, 32, QUART), BF16),
            pltpu.VMEM((2, 32, HALF), BF16),
            pltpu.VMEM((2, 32, QUART), BF16),
            pltpu.SMEM((2, 2), jnp.int32),
            dma((6,)),
            dma((2,)),
            dma((2,)),
            dma((2,)),
            dma((2, 4)),
            dma,
            dma((4, 2)),
            dma,
            dma((4, 2)),
            dma,
            dma((7,)),
            dma((2,)),
            dma((9, 3)),
            dma((2,)),
            dma((9, 4)),
            dma((2,)),
            dma((9,)),
            dma((3,)),
            dma((3,)),
            dma((5,)),
            dma((4, 2)),
            dma((4,)),
            dma((4, 2)),
            dma((2,)),
            dma((2,)),
            dma,
            dma,
            dma,
            dma((2,)),
        ],
        compiler_params=pltpu.CompilerParams(
            collective_id=0, has_side_effects=True, vmem_limit_bytes=63 * 2**20
        ),
        cost_estimate=pl.CostEstimate(
            flops=9 * 2 * ROWS * D * D, bytes_accessed=36 * 2**20, transcendentals=4 * ROWS * D
        ),
    )(inputs.reshape(4, rows // 4, D), weights[0], cotangents.reshape(rows, D), lengths)
    return out[None]


def solution(mesh):
    in_specs = (
        P(None, "fsdp", None),
        P("section", "fsdp", None),
        P(None, "fsdp", None),
        P(None, "fsdp"),
    )
    out_specs = P("section", "fsdp", None)
    return jax.shard_map(local, mesh=mesh, in_specs=in_specs, out_specs=out_specs, check_vma=False)
```
